32 devices in a mesh: azim: 4 (over x, core), sect: 8 (over z, y).
Axes of the slice: x: 2, y: 2, z: 4, core: 2. Of those that a mesh axis runs over, the one named last changes fastest.
Arguments:
- signals: bfloat16 [1024, 256], P(('azim', 'sect')), may hold values from -6 to 6
- observer_xyz: bfloat16 [1024, 3], P(('azim', 'sect'))
- panel_geometry: float32 [7, 32768], P(None, ('azim', 'sect'))
- delays: int32 [256, 1024], P(('azim', 'sect')), may hold values from 0 to 127
- counts: int32 [32], P(('azim', 'sect')), may hold values from 1 to 1024, as said below
- connectivity: int32 [4, 32768], P(None, ('azim', 'sect')), may hold values from 0 to 1160, as said below
- owners: int32 [32768], P(('azim', 'sect')), may hold values from 0 to 2047, as said below
Outputs:
- node_grad: float32 [33024, 128], P(('azim', 'sect'))
- cell_grad: float32 [8192, 128], P(('azim', 'sect'))
The draws below stay inside these ranges and needn't reach their ends.
Inputs may be any that keep to these rules, and one draw needn't show every extreme that they name: counts[d] panels of device d are live, the first ones of its 1024 slots; the others are padding. In every azim group the last section holds 1024. `connectivity`: A value k below 1032 is node k of the panel's own device; otherwise k - 1032 is below 129 and names that node of the next device along sect, the last section's next being the first. owners[p] // 256 is the section and owners[p] % 256 the cell within the panel's azim group. The four panels of each aligned group of four slots share one owner. At most 64 groups of one device have owners in one section, and every device reaches that number.
All inputs are finite; a program needn't handle non-finite values.
Results may differ from the reference program's by a relative error of at most 0.006.
Values may be sent and summed in bfloat16 or wider, within the bound.
No kernel may reach another device: no remote copies, remote signals or barrier semaphores. Data moves between devices by JAX's collectives and lax.ppermute only.
A program may use at most 64 MiB of HBM per device.

```python
import math
import jax
import jax.numpy as jnp
from jax import lax

NV = 8
NPU = 128
BLK = 128
OBS = 1024
TW = 128
DMAX = 127
TG = 256
P_DEV = 1024
PANELS = 32768
NBLK = 256
CELL_DEV = 256
CELLS = 8192
NODE_DEV = 1032
NODES = 33024
N_SECT = 8
DEVICES = 32


def draw_observer_xyz(key, part):
    key = jax.random.fold_in(key, 23)
    plane_key, height_key, side_key = jax.random.split(key, 3)
    plane = jax.random.uniform(plane_key, (OBS, 2), jnp.float32, -6.0, 6.0)
    height = jax.random.uniform(height_key, (OBS, 1), jnp.float32, 3.0, 6.0)
    side = (jax.random.randint(side_key, (OBS, 1), 0, 2) * 2 - 1).astype(jnp.float32)
    return jnp.concatenate([plane, height * side], 1).astype(jnp.bfloat16)


def draw_panel_geometry(key, part):
    key = jax.random.fold_in(key, 11)
    place_key, normal_key, area_key = jax.random.split(key, 3)
    position = jax.random.uniform(place_key, (3, PANELS), jnp.float32, -1.5, 1.5)
    normal = jax.random.uniform(normal_key, (3, PANELS), jnp.float32, -1.0, 1.0)
    area = jnp.exp(jax.random.uniform(area_key, (1, PANELS), jnp.float32, math.log(0.01), math.log(0.04)))
    return jnp.concatenate([position, normal * area, area], 0)


def draw_counts(key, part):
    key = jax.random.fold_in(key, 5)
    device = jnp.arange(DEVICES, dtype=jnp.int32)
    section = device % N_SECT
    base = P_DEV // 16 + 15 * P_DEV // 16 * section * section // ((N_SECT - 1) * (N_SECT - 1))
    jitter = jax.random.randint(key, (DEVICES,), 0, P_DEV // 16)
    return jnp.where(section == N_SECT - 1, P_DEV, base - jitter).astype(jnp.int32)


def draw_connectivity(key, part):
    key = jax.random.fold_in(key, 9)
    groups = P_DEV // 4
    half_row = NPU // 2

    def one_device(device_key):
        grid = jax.random.permutation(device_key, groups)
        inner = jnp.arange(4, dtype=jnp.int32)
        column = (2 * (grid % half_row))[:, None] + (inner % 2)[None, :]
        row_number = (2 * (grid // half_row))[:, None] + (inner // 2)[None, :]
        column = column.reshape(-1)
        row_number = row_number.reshape(-1)
        stacked = []
        for corner in range(4):
            corner_col = column + corner % 2
            corner_row = row_number + corner // 2
            stacked.append(jnp.where(corner_row < NV, corner_row * (NPU + 1) + corner_col, NODE_DEV + corner_col))
        return jnp.stack(stacked, 0)
    device_keys = jax.random.split(key, DEVICES)
    result = jax.vmap(one_device)(device_keys)
    return result.transpose(1, 0, 2).reshape(4, PANELS).astype(jnp.int32)


def draw_owners(key, part):
    key = jax.random.fold_in(key, 7)
    groups = P_DEV // 4
    home = 2 * groups // N_SECT

    def one_device(device_key, device):
        order_key, cell_key = jax.random.split(device_key)
        rank = jax.random.permutation(order_key, groups)
        section = device % N_SECT
        spread = (section + 1 + (rank - home) % (N_SECT - 1)) % N_SECT
        target = jnp.where(rank < home, section, spread)
        cell = jax.random.randint(cell_key, (groups,), 0, CELL_DEV)
        cell = jnp.where(rank == groups - 1, CELL_DEV - 1, cell)
        cell = jnp.where(rank == 0, 0, cell)
        return jnp.repeat(target * CELL_DEV + cell, 4)
    device_keys = jax.random.split(key, DEVICES)
    result = jax.vmap(one_device)(device_keys, jnp.arange(DEVICES, dtype=jnp.int32))
    return result.reshape(-1).astype(jnp.int32)


def set_ends(values, key, smallest, largest):
    index_at = [jax.random.randint(jax.random.fold_in(key, axis), (), 0, length) for axis, length in enumerate(values.shape)]
    widest = values.shape.index(max(values.shape))
    beside = index_at[:widest] + [(index_at[widest] + 1) % values.shape[widest]] + index_at[widest + 1:]
    return values.at[tuple(index_at)].set(smallest).at[tuple(beside)].set(largest)


def steps_of(stream_key, extent, cuts, smallest, high):
    def one(dim, shards_of):
        draws = jax.random.uniform(jax.random.fold_in(jax.random.fold_in(stream_key, 6), dim), (shards_of,), jnp.float32, smallest / len(cuts), high / len(cuts))
        return jnp.repeat(jnp.exp(draws), extent[dim] // shards_of).reshape((-1,) + (1,) * (len(extent) - dim - 1))

    gain = one(*cuts[0])
    for cut in cuts[1:]:
        gain = gain * one(*cut)
    return gain


def scatter_about(stream_key, dims, deviation, most, cuts=(), held_as=jnp.bfloat16):
    loudness = steps_of(stream_key, dims, cuts, -0.22, 0.18) if cuts else 1.0
    entries = jax.random.normal(stream_key, dims, jnp.float32) * deviation * loudness
    return jnp.minimum(jnp.maximum(entries, -most), most).astype(held_as)


def setup_inputs(seed: int = 0) -> dict:
    keys = jax.random.split(jax.random.key(seed), 8)
    return {
        "signals": scatter_about(keys[0], (OBS, TG), 1.0, 6.0, ((0, 32),)),
        "observer_xyz": draw_observer_xyz(jax.random.fold_in(keys[7], 71), 0),
        "panel_geometry": draw_panel_geometry(jax.random.fold_in(keys[7], 71), 0),
        "delays": set_ends(jax.random.randint(keys[3], (NBLK, OBS), 0, DMAX + 1), jax.random.fold_in(keys[3], 1), 0, DMAX).astype(jnp.int32),
        "counts": draw_counts(jax.random.fold_in(keys[7], 71), 0),
        "connectivity": draw_connectivity(jax.random.fold_in(keys[7], 71), 0),
        "owners": draw_owners(jax.random.fold_in(keys[7], 71), 0),
    }


RADIUS = 4.0

def block_sources(geometry, signal, observers, shift):
    points = observers.astype(jnp.float32)
    delta_x = points[:, 0][None, :] - geometry[0][:, None]
    delta_y = points[:, 1][None, :] - geometry[1][:, None]
    delta_z = points[:, 2][None, :] - geometry[2][:, None]
    distance = jnp.sqrt(delta_x * delta_x + delta_y * delta_y + delta_z * delta_z)
    inverse = RADIUS / distance
    facing = (geometry[3][:, None] * delta_x + geometry[4][:, None] * delta_y + geometry[5][:, None] * delta_z) / distance
    near_weight = (facing * inverse * inverse).astype(jnp.bfloat16)
    far_weight = (facing * inverse).astype(jnp.bfloat16)
    thick_weight = (geometry[6][:, None] * inverse).astype(jnp.bfloat16)
    sample_offsets = jnp.arange(TW + 1, dtype=jnp.int32)
    sample_index = shift.astype(jnp.int32)[:, None] + sample_offsets[None, :]
    window = jnp.take_along_axis(signal, sample_index, axis=1)
    current = window[:, :TW]
    change = (window[:, 1:].astype(jnp.float32) - current.astype(jnp.float32)).astype(jnp.bfloat16)
    loading = jnp.dot(near_weight, current, preferred_element_type=jnp.float32)
    loading = loading + jnp.dot(far_weight, change, preferred_element_type=jnp.float32)
    thickness = jnp.dot(thick_weight, change, preferred_element_type=jnp.float32)
    return (loading, thickness)

def reference(signals, observer_xyz, panel_geometry, delays, counts, connectivity, owners):
    panels = NPU * NV
    blocks = panels // BLK

    def device(carried, device_index):
        node_sums, cell_sums = carried
        geometry = lax.dynamic_slice_in_dim(panel_geometry, device_index * panels, panels, 1)
        shifts = lax.dynamic_slice_in_dim(delays, device_index * blocks, blocks, 0)
        pieces = geometry.reshape(7, blocks, BLK).transpose(1, 0, 2)

        def one_block(element):
            return block_sources(element[0], signals, observer_xyz, element[1])
        loading, thickness = lax.map(one_block, (pieces, shifts))
        keep_mask = (jnp.arange(panels, dtype=jnp.int32) < counts[device_index]).astype(jnp.float32)[:, None]
        loading = loading.reshape(panels, TW) * keep_mask
        thickness = thickness.reshape(panels, TW) * keep_mask
        corners = lax.dynamic_slice_in_dim(connectivity, device_index * panels, panels, 1)
        sect_index = device_index % N_SECT
        following = device_index - sect_index + (sect_index + 1) % N_SECT
        node_ids = jnp.where(corners < NODE_DEV, device_index * NODE_DEV + corners, following * NODE_DEV + corners - NODE_DEV).astype(jnp.int32)
        quarter = 0.25 * loading
        for corner in range(4):
            node_sums = node_sums.at[node_ids[corner]].add(quarter)
        target = lax.dynamic_slice_in_dim(owners, device_index * panels, panels, 0)
        cell_ids = ((device_index - sect_index) * CELL_DEV + target).astype(jnp.int32)
        cell_sums = cell_sums.at[cell_ids].add(thickness)
        return ((node_sums, cell_sums), None)
    start_nodes = jnp.zeros((NODES, TW), jnp.float32)
    start_cells = jnp.zeros((CELLS, TW), jnp.float32)
    finals, _ = lax.scan(device, (start_nodes, start_cells), jnp.arange(DEVICES, dtype=jnp.int32))
    return (finals[0], finals[1])
```

```python
import functools

import jax
import jax.numpy as jnp
from jax import lax
from jax.experimental import pallas as pl
from jax.experimental.pallas import tpu as pltpu
from jax.sharding import PartitionSpec as P

NPU = 128
BLK = 128
TW = 128
CELL_DEV = 256
NODE_DEV = 1032
RIM = NPU + 1
NODE_ROWS = 1168
EXTRA = 16
F32 = jnp.float32
BF16 = jnp.bfloat16
VMEM = pltpu.VMEM
SMEM = pltpu.SMEM


def params(mib=24):
    return pltpu.CompilerParams(vmem_limit_bytes=mib * 1024 * 1024)


def route_kernel(cap, place_ref, conn_ref, owner_ref, corner_ref, slot_ref, ids_ref):
    panels = conn_ref.shape[1]
    sections = ids_ref.shape[0] // EXTRA * EXTRA
    live = place_ref[1]

    def corner_rows(step, carried):
        row = pl.multiple_of(step * 16, 16)
        node = row + lax.broadcasted_iota(jnp.int32, (16, panels), 0)
        panel = lax.broadcasted_iota(jnp.int32, (16, panels), 1)
        node = jnp.where(panel < live, node, -1)
        total = jnp.zeros((16, panels), F32)
        for corner in range(4):
            total = total + jnp.where(conn_ref[corner : corner + 1, :] == node, 0.25, 0.0)
        corner_ref[pl.ds(row, 16), :] = total.astype(BF16)
        return carried

    lax.fori_loop(0, NODE_ROWS // 16, corner_rows, 0)

    owner = owner_ref[...]
    dest = owner // CELL_DEV
    lane = lax.broadcasted_iota(jnp.int32, (sections, panels), 1)
    mine = dest == lax.broadcasted_iota(jnp.int32, (sections, panels), 0)
    count = jnp.where(mine, 1, 0)
    span = 1
    while span < panels:
        count = count + jnp.where(lane >= span, pltpu.roll(count, span, 1), 0)
        span *= 2
    before = jnp.sum(jnp.where(mine, count - 1, 0), axis=0, keepdims=True)
    rank = before // 4
    slot = dest * cap + rank

    def slot_rows(step, carried):
        row = pl.multiple_of(step * 16, 16)
        number = row + lax.broadcasted_iota(jnp.int32, (16, panels), 0)
        panel = lax.broadcasted_iota(jnp.int32, (16, panels), 1)
        number = jnp.where(panel < live, number, -1)
        slot_ref[pl.ds(row, 16), :] = jnp.where(slot == number, 1.0, 0.0).astype(BF16)
        return carried

    lax.fori_loop(0, slot_ref.shape[0] // 16, slot_rows, 0)

    first = place_ref[0] * cap % 128
    at_lane = rank + first == lax.broadcasted_iota(jnp.int32, (128, panels), 0)
    at_lane = jnp.where(at_lane, 1.0, 0.0).astype(BF16)
    cell = jnp.where(mine & (lane % 4 == 0), owner % CELL_DEV, 0).astype(F32).astype(BF16)
    ids = lax.dot_general(cell, at_lane, (((1,), (1,)), ((), ())), preferred_element_type=F32)
    ids_ref[...] = ids.astype(BF16)


def route_matrices(sections, place, connectivity, owners):
    panels = connectivity.shape[1]
    cap = 2 * CELL_DEV // sections
    padded = -(-sections // EXTRA) * EXTRA
    return pl.pallas_call(
        functools.partial(route_kernel, cap),
        out_shape=(
            jax.ShapeDtypeStruct((NODE_ROWS, panels), BF16),
            jax.ShapeDtypeStruct((sections * cap, panels), BF16),
            jax.ShapeDtypeStruct((padded, 128), BF16),
        ),
        in_specs=[
            pl.BlockSpec(memory_space=SMEM),
            pl.BlockSpec(memory_space=VMEM),
            pl.BlockSpec(memory_space=VMEM),
        ],
        out_specs=[pl.BlockSpec(memory_space=VMEM)] * 3,
        compiler_params=params(),
        cost_estimate=pl.CostEstimate(flops=20_000_000, bytes_accessed=4_000_000, transcendentals=0),
        name="route",
    )(place, connectivity, owners.reshape(1, panels))


def sources_kernel(chunk_order, cap, place_ref, *refs):
    chunks = refs[: len(chunk_order)]
    (delay_ref, geometry_ref, corner_ref, slot_ref, ids_ref) = refs[len(chunk_order) : len(chunk_order) + 5]
    (node_ref, rim_ref, message_ref) = refs[len(chunk_order) + 5 : len(chunk_order) + 8]
    (low_ref, high_ref, shift_ref, panel_ref, weight_ref, window_ref, loading_ref, thick_ref) = refs[len(chunk_order) + 8 :]
    span = chunks[0].shape[0] - EXTRA
    observers = span * len(chunks)
    panels = geometry_ref.shape[1]
    live = place_ref[1]
    azim = place_ref[2]

    points = []
    for number, chunk in enumerate(chunks):
        rows = pl.ds(number * span, span)
        low_ref[rows, :] = chunk[:span, :128].astype(F32)
        high_ref[rows, :] = chunk[:span, 128:].astype(F32)
        points.append(chunk[span : span + EXTRA, :].astype(F32) * 0.25)
        begin = pl.multiple_of((azim ^ chunk_order[number]) * span, span)
        for row in range(delay_ref.shape[0]):
            shift_ref[row, :, rows] = delay_ref[row : row + 1, pl.ds(begin, span)]

    lanes = lax.broadcasted_iota(jnp.int32, (128, 128), 1)

    def column(row):
        return jnp.broadcast_to(row, (128, 128)).T

    def block(index, carried):
        start = pl.multiple_of(index * BLK, BLK)
        for part in range(7):
            scale = 0.25 if part < 3 else 1.0
            panel_ref[part] = column(geometry_ref[part : part + 1, pl.ds(start, BLK)] * scale)
        for number in range(len(chunk_order)):
            for piece in range(span // 128):
                here = number * span + piece * 128
                cols = pl.ds(here, 128)
                shift = column(shift_ref[index, :, cols])
                source = shift + lanes
                at = source & 127
                low = jnp.take_along_axis(low_ref[cols, :], at, axis=1, mode="promise_in_bounds")
                high = jnp.take_along_axis(high_ref[cols, :], at, axis=1, mode="promise_in_bounds")
                current = jnp.where(source < 128, low, high)
                following = pltpu.roll(jnp.where(lanes == 0, high, current), 127, 1)
                window_ref[cols, :128] = current.astype(BF16)
                window_ref[cols, 128:] = (following - current).astype(BF16)

                at_x, at_y, at_z = (points[number][i : i + 1, piece * 128 : piece * 128 + 128] for i in range(3))
                for strip in range(BLK // 32):
                    rows = pl.ds(strip * 32, 32)
                    delta_x = at_x - panel_ref[0, rows, :]
                    delta_y = at_y - panel_ref[1, rows, :]
                    delta_z = at_z - panel_ref[2, rows, :]
                    inverse = lax.rsqrt(delta_x * delta_x + delta_y * delta_y + delta_z * delta_z)
                    flux = (
                        panel_ref[3, rows, :] * delta_x
                        + panel_ref[4, rows, :] * delta_y
                        + panel_ref[5, rows, :] * delta_z
                    )
                    far = flux * inverse * inverse
                    weight_ref[pl.ds(strip * 32, 32), cols] = (far * inverse).astype(BF16)
                    weight_ref[pl.ds(BLK + strip * 32, 32), cols] = far.astype(BF16)
                    weight_ref[pl.ds(2 * BLK + strip * 32, 32), cols] = (panel_ref[6, rows, :] * inverse).astype(BF16)
        products = jnp.dot(weight_ref[...], window_ref[...], preferred_element_type=F32)
        alive = start + lax.broadcasted_iota(jnp.int32, (BLK, TW), 0) < live
        loading = products[:BLK, :TW] + products[BLK : 2 * BLK, TW:]
        loading_ref[pl.ds(start, BLK), :] = jnp.where(alive, loading, 0.0).astype(BF16)
        thick_ref[pl.ds(start, BLK), :] = jnp.where(alive, products[2 * BLK :, TW:], 0.0).astype(BF16)
        return carried

    lax.fori_loop(0, panels // BLK, block, 0)

    nodes = jnp.dot(corner_ref[...], loading_ref[...], preferred_element_type=F32)
    node_ref[...] = nodes[:NODE_DEV]
    rim_ref[...] = nodes[NODE_DEV : NODE_DEV + RIM]
    slots = jnp.dot(slot_ref[...], thick_ref[...], preferred_element_type=F32).astype(BF16)
    for section in range(message_ref.shape[0]):
        message_ref[section, :cap, :] = slots[section * cap : (section + 1) * cap]
        message_ref[section, cap:, :] = jnp.broadcast_to(
            ids_ref[section : section + 1, :].astype(F32), (EXTRA, 128)
        ).astype(BF16)


def sources(sections, chunk_order, place, chunks, delays, geometry, corners, slots, ids):
    panels = geometry.shape[1]
    observers = delays.shape[1]
    cap = 2 * CELL_DEV // sections
    return pl.pallas_call(
        functools.partial(sources_kernel, chunk_order, cap),
        out_shape=(
            jax.ShapeDtypeStruct((NODE_DEV, TW), F32),
            jax.ShapeDtypeStruct((RIM, TW), F32),
            jax.ShapeDtypeStruct((sections, cap + EXTRA, TW), BF16),
        ),
        in_specs=[pl.BlockSpec(memory_space=SMEM)] + [pl.BlockSpec(memory_space=VMEM)] * (len(chunks) + 5),
        out_specs=[pl.BlockSpec(memory_space=VMEM)] * 3,
        scratch_shapes=[
            VMEM((observers, 128), F32),
            VMEM((observers, 128), F32),
            VMEM((panels // BLK, 1, observers), jnp.int32),
            VMEM((7, BLK, 128), F32),
            VMEM((3 * BLK, observers), BF16),
            VMEM((observers, 2 * TW), BF16),
            VMEM((panels, TW), BF16),
            VMEM((panels, TW), BF16),
        ],
        compiler_params=params(),
        cost_estimate=pl.CostEstimate(flops=2_000_000_000, bytes_accessed=6_000_000, transcendentals=1_000_000),
        name="sources",
    )(place, *chunks, delays, geometry, corners, slots, ids)


def finish_kernel(cap, message_ref, rim_ref, node_in_ref, node_ref, cell_ref, rows_ref):
    sections = message_ref.shape[0]
    per = 128 // cap
    node_ref[...] = node_in_ref[...]
    node_ref[:RIM, :] = node_in_ref[:RIM, :] + rim_ref[...]
    total = jnp.zeros((CELL_DEV, TW), F32)
    for group in range(sections // per):
        ids = jnp.zeros((8, 128), F32)
        for inner in range(per):
            section = group * per + inner
            ids = ids + message_ref[section, cap : cap + EXTRA, :].astype(F32)[:8]
            rows_ref[group * 128 + inner * cap : group * 128 + (inner + 1) * cap, :] = message_ref[section, :cap, :]
        cell = lax.broadcasted_iota(jnp.int32, (CELL_DEV, 128), 0)
        match = jnp.where(ids[:1].astype(jnp.int32) == cell, 1.0, 0.0).astype(BF16)
        total = total + jnp.dot(match, rows_ref[group * 128 : (group + 1) * 128, :], preferred_element_type=F32)
    cell_ref[...] = total


def finish(sections, message, rim, nodes):
    cap = 2 * CELL_DEV // sections
    head = 136
    return pl.pallas_call(
        functools.partial(finish_kernel, cap),
        grid=(1,),
        out_shape=(
            jax.ShapeDtypeStruct((NODE_DEV, TW), F32),
            jax.ShapeDtypeStruct((CELL_DEV, TW), F32),
        ),
        in_specs=[
            pl.BlockSpec(message.shape, lambda i: (0, 0, 0)),
            pl.BlockSpec(rim.shape, lambda i: (0, 0)),
            pl.BlockSpec((head, TW), lambda i: (0, 0)),
        ],
        out_specs=[
            pl.BlockSpec((head, TW), lambda i: (0, 0)),
            pl.BlockSpec((CELL_DEV, TW), lambda i: (0, 0)),
        ],
        scratch_shapes=[VMEM((sections * cap, TW), BF16)],
        input_output_aliases={2: 0},
        compiler_params=params(),
        name="finish",
    )(message, rim, nodes)


def swapped(array, axis, bit):
    peers = lax.axis_size(axis)
    return lax.ppermute(array, axis, [(i, i ^ bit) for i in range(peers)])


def gathered(signals, xyz):
    count = signals.shape[0]
    sections = lax.axis_size("sect")
    section = lax.axis_index("sect")
    extra = jnp.zeros((EXTRA, signals.shape[1]), BF16)
    extra = lax.dynamic_update_slice(extra, xyz.T, (0, section * count))
    payload = jnp.concatenate([signals, extra], 0)
    everyone = jnp.broadcast_to(payload[None], (sections,) + payload.shape)
    received = lax.all_to_all(everyone, "sect", split_axis=0, concat_axis=0, tiled=True)
    span = sections * count
    chunk = jnp.concatenate(
        [received[:, :count].reshape(span, -1), received[:, count:].astype(F32).sum(0).astype(BF16)], 0
    )
    chunks = {0: chunk}
    bit = lax.axis_size("azim") // 2
    while bit:
        for offset in list(chunks):
            chunks[offset ^ bit] = swapped(chunks[offset], "azim", bit)
        bit //= 2
    return tuple(chunks), tuple(chunks.values())


def per_device(signals, observer_xyz, panel_geometry, delays, counts, connectivity, owners):
    sections = lax.axis_size("sect")
    section = lax.axis_index("sect")
    place = jnp.stack([section, counts[0], lax.axis_index("azim")]).astype(jnp.int32)
    chunk_order, chunks = gathered(signals, observer_xyz)
    corners, slots, ids = route_matrices(sections, place, connectivity, owners)
    nodes, rim, message = sources(
        sections, chunk_order, place, chunks, delays, panel_geometry, corners, slots, ids
    )
    rim = lax.ppermute(rim, "sect", [(i, (i + 1) % sections) for i in range(sections)])
    message = lax.all_to_all(message, "sect", split_axis=0, concat_axis=0, tiled=True)
    return finish(sections, message, rim, nodes)


def solution(mesh):
    in_specs = (
        P(("azim", "sect"), None),
        P(("azim", "sect"), None),
        P(None, ("azim", "sect")),
        P(("azim", "sect"), None),
        P(("azim", "sect")),
        P(None, ("azim", "sect")),
        P(("azim", "sect")),
    )
    out_specs = (P(("azim", "sect"), None), P(("azim", "sect"), None))
    return jax.shard_map(
        per_device, mesh=mesh, in_specs=in_specs, out_specs=out_specs, check_vma=False
    )
```

```python
import functools

import jax
import jax.numpy as jnp
from jax import lax
from jax.experimental import pallas as pl
from jax.experimental.pallas import tpu as pltpu
from jax.sharding import PartitionSpec as P

NPU = 128
BLK = 128
TW = 128
CELL_DEV = 256
NODE_DEV = 1032
RIM = NPU + 1
HEAD = 136
NODE_ROWS = 1168
EXTRA = 16
F32 = jnp.float32
BF16 = jnp.bfloat16
VMEM = pltpu.VMEM
SMEM = pl.BlockSpec(memory_space=pltpu.SMEM)
WHOLE = pl.BlockSpec(memory_space=pltpu.VMEM)
PLACE = pl.BlockSpec(memory_space=pl.ANY)
COPY = pltpu.SemaphoreType.DMA


def call(kernel, name, out_shape, in_specs, out_specs, scratch_shapes=(), aliases=None, work=1_000_000):
    return pl.pallas_call(
        kernel,
        out_shape=out_shape,
        in_specs=in_specs,
        out_specs=out_specs,
        scratch_shapes=list(scratch_shapes),
        input_output_aliases=aliases or {},
        compiler_params=pltpu.CompilerParams(vmem_limit_bytes=24 * 1024 * 1024),
        cost_estimate=pl.CostEstimate(flops=work, bytes_accessed=4_000_000, transcendentals=0),
        name=name,
    )


def route_kernel(
    sections, place_ref, conn_at, owner_at, delay_at, geometry_at,
    corner_ref, slot_ref, ids_ref, source_ref, panel_ref,
    conn_ref, owner_ref, delay_ref, geometry_ref, sems,
):
    copies = [
        pltpu.make_async_copy(source, target, sems.at[number])
        for number, (source, target) in enumerate(
            ((delay_at, delay_ref), (geometry_at, geometry_ref), (conn_at, conn_ref), (owner_at, owner_ref))
        )
    ]
    for copy in copies:
        copy.start()
    for copy in copies:
        copy.wait()
    panels = conn_ref.shape[1]
    cap = slot_ref.shape[0] // sections
    padded = ids_ref.shape[0]
    section = place_ref[0]
    live = place_ref[1]
    groups, blocks, span, _ = source_ref.shape

    lanes = lax.broadcasted_iota(jnp.int32, (128, 128), 1)
    for piece in range(groups * span // 128):
        columns = delay_ref[:, piece * 128 : (piece + 1) * 128].T
        begin = piece * 128 % span
        for block in range(blocks):
            source = jnp.broadcast_to(columns[:, block : block + 1], (128, 128)) + lanes
            source_ref[piece * 128 // span, block, begin : begin + 128, :] = source
    for block in range(blocks):
        values = geometry_ref[:, block * BLK : (block + 1) * BLK]
        columns = jnp.concatenate([values, values[:1]], 0).T
        for part in range(7):
            column = columns[:, part : part + 1] * (0.25 if part < 3 else 1.0)
            panel_ref[block, part] = jnp.broadcast_to(column, (BLK, 128))

    def corner_rows(step, carried):
        row = pl.multiple_of(step * 16, 16)
        node = row + lax.broadcasted_iota(jnp.int32, (16, panels), 0)
        panel = lax.broadcasted_iota(jnp.int32, (16, panels), 1)
        node = jnp.where(panel < live, node, -1)
        total = jnp.zeros((16, panels), F32)
        for corner in range(4):
            total = total + jnp.where(conn_ref[corner : corner + 1, :] == node, 0.25, 0.0)
        corner_ref[pl.ds(row, 16), :] = total.astype(BF16)
        return carried

    lax.fori_loop(0, NODE_ROWS // 16, corner_rows, 0)

    owner = owner_ref[...]
    away = owner // CELL_DEV - section
    away = jnp.where(away < 0, away + sections, away)
    lane = lax.broadcasted_iota(jnp.int32, (padded, panels), 1)
    mine = away == lax.broadcasted_iota(jnp.int32, (padded, panels), 0)
    count = jnp.where(mine, 1, 0)
    span = 1
    while span < panels:
        count = count + jnp.where(lane >= span, pltpu.roll(count, span, 1), 0)
        span *= 2
    before = jnp.sum(jnp.where(mine, count - 1, 0), axis=0, keepdims=True)
    slot = away * cap + before // 4

    def slot_rows(step, carried):
        row = pl.multiple_of(step * 16, 16)
        number = row + lax.broadcasted_iota(jnp.int32, (16, panels), 0)
        panel = lax.broadcasted_iota(jnp.int32, (16, panels), 1)
        number = jnp.where(panel < live, number, -1)
        slot_ref[pl.ds(row, 16), :] = jnp.where(slot == number, 1.0, 0.0).astype(BF16)
        return carried

    lax.fori_loop(0, slot_ref.shape[0] // 16, slot_rows, 0)

    at_lane = slot % 128 == lax.broadcasted_iota(jnp.int32, (128, panels), 0)
    at_lane = jnp.where(at_lane, 1.0, 0.0).astype(BF16)
    cell = jnp.where(mine & (lane % 4 == 0), owner % CELL_DEV, 0).astype(F32).astype(BF16)
    ids_ref[...] = lax.dot_general(cell, at_lane, (((1,), (1,)), ((), ())), preferred_element_type=F32)


def route(sections, groups, place, connectivity, owners, delays, geometry):
    panels = connectivity.shape[1]
    blocks, observers = delays.shape
    cap = 2 * CELL_DEV // sections
    padded = -(-sections // EXTRA) * EXTRA
    return call(
        functools.partial(route_kernel, sections),
        "route",
        (
            jax.ShapeDtypeStruct((NODE_ROWS, panels), BF16),
            jax.ShapeDtypeStruct((sections * cap, panels), BF16),
            jax.ShapeDtypeStruct((padded, 128), F32),
            jax.ShapeDtypeStruct((groups, blocks, observers // groups, 128), jnp.int32),
            jax.ShapeDtypeStruct((blocks, 7, BLK, 128), F32),
        ),
        [SMEM] + [PLACE] * 4,
        [WHOLE] * 5,
        [
            VMEM(connectivity.shape, jnp.int32),
            VMEM((1, panels), jnp.int32),
            VMEM(delays.shape, jnp.int32),
            VMEM(geometry.shape, F32),
            COPY((4,)),
        ],
        work=4_000_000_000,
    )(place, connectivity, owners.reshape(1, panels), delays, geometry)


def join_kernel(sections, place_ref, *refs):
    signals = refs[:sections]
    points = refs[sections : 2 * sections]
    chunk_ref, wide_ref = refs[2 * sections :]
    count = signals[0].shape[0]
    span = sections * count
    wide_ref[...] = jnp.zeros_like(wide_ref)
    total = jnp.zeros(wide_ref.shape, F32)
    for number in range(sections):
        origin = place_ref[0] - number
        origin = jnp.where(origin < 0, origin + sections, origin)
        chunk_ref[pl.ds(pl.multiple_of(origin * count, count), count), :] = signals[number][...]
        wide_ref[:3, :count] = points[number][...].astype(F32)
        total = total + pltpu.roll(wide_ref[...], origin * count, 1)
    chunk_ref[span : span + EXTRA, :] = total.astype(BF16)


def join(sections, place, signals, points):
    count, width = signals[0].shape
    return call(
        functools.partial(join_kernel, sections),
        "join",
        jax.ShapeDtypeStruct((sections * count + EXTRA, width), BF16),
        [SMEM] + [WHOLE] * (2 * sections),
        WHOLE,
        [VMEM((EXTRA, width), F32)],
    )(place, *signals, *points)


def sources_kernel(offsets, first, sections, place_ref, *refs):
    refs = list(refs)

    def take(number):
        taken = refs[:number]
        del refs[:number]
        return taken

    parts = len(offsets)
    chunks = take(parts)
    source_ref, panel_ref = take(2)
    loading_in, thick_in = (None, None) if first else take(2)
    final = sections is not None
    if final:
        corner_ref, slot_ref, ids_ref = take(3)
        node_ref, head_ref = take(2)
        messages = take(sections)
        loading_ref, thick_ref = take(2)
    else:
        loading_ref, thick_ref = take(2)
    low_ref, high_ref, pair_ref, mass_ref, window_ref = take(5)

    blocks, span = source_ref.shape[1:3]
    panels = panel_ref.shape[0] * BLK
    observers = parts * span
    points = []
    for number, chunk in enumerate(chunks):
        low_ref[number * span : (number + 1) * span, :] = chunk[:span, :128].astype(F32)
        high_ref[number * span : (number + 1) * span, :] = chunk[:span, 128:].astype(F32)
        points.append(chunk[span : span + EXTRA, :].astype(F32) * 0.25)

    lanes = lax.broadcasted_iota(jnp.int32, (128, 128), 1)
    for block in range(blocks):
        for number, offset in enumerate(offsets):
            group = place_ref[2] ^ offset
            for piece in range(span // 128):
                here = number * span + piece * 128
                source = source_ref[group, block, piece * 128 : (piece + 1) * 128, :]
                at = source & 127
                low = jnp.take_along_axis(low_ref[here : here + 128, :], at, axis=1, mode="promise_in_bounds")
                high = jnp.take_along_axis(high_ref[here : here + 128, :], at, axis=1, mode="promise_in_bounds")
                current = jnp.where(source < 128, low, high)
                following = pltpu.roll(jnp.where(lanes == 0, high, current), 127, 1)
                window_ref[block, here : here + 128, :] = current.astype(BF16)
                window_ref[block, observers + here : observers + here + 128, :] = (following - current).astype(BF16)

                at_x, at_y, at_z = (points[number][i : i + 1, piece * 128 : piece * 128 + 128] for i in range(3))
                for strip in range(BLK // 16):
                    rows = slice(strip * 16, strip * 16 + 16)
                    delta_x = at_x - panel_ref[block, 0, rows, :]
                    delta_y = at_y - panel_ref[block, 1, rows, :]
                    delta_z = at_z - panel_ref[block, 2, rows, :]
                    inverse = lax.rsqrt(delta_x * delta_x + delta_y * delta_y + delta_z * delta_z)
                    flux = (
                        panel_ref[block, 3, rows, :] * delta_x
                        + panel_ref[block, 4, rows, :] * delta_y
                        + panel_ref[block, 5, rows, :] * delta_z
                    )
                    far = flux * inverse * inverse
                    pair_ref[block, rows, here : here + 128] = (far * inverse).astype(BF16)
                    pair_ref[block, rows, observers + here : observers + here + 128] = far.astype(BF16)
                    mass_ref[block, rows, here : here + 128] = (panel_ref[block, 6, rows, :] * inverse).astype(BF16)
        rows = slice(block * BLK, (block + 1) * BLK)
        loading = jnp.dot(pair_ref[block], window_ref[block], preferred_element_type=F32)
        thick = jnp.dot(mass_ref[block], window_ref[block, observers:, :], preferred_element_type=F32)
        if not first:
            loading = loading + loading_in[rows, :]
            thick = thick + thick_in[rows, :]
        if final:
            alive = block * BLK + lax.broadcasted_iota(jnp.int32, (BLK, TW), 0) < place_ref[1]
            loading = jnp.where(alive, loading, 0.0).astype(BF16)
            thick = jnp.where(alive, thick, 0.0).astype(BF16)
        loading_ref[rows, :] = loading
        thick_ref[rows, :] = thick

    if final:
        nodes = jnp.dot(corner_ref[...], loading_ref[...], preferred_element_type=F32)
        head_ref[...] = nodes[:HEAD]
        node_ref[...] = nodes[:NODE_DEV]
        cap = slot_ref.shape[0] // sections
        slots = jnp.dot(slot_ref[...], thick_ref[...], preferred_element_type=F32).astype(BF16)
        for away, message_ref in enumerate(messages):
            message_ref[:cap, :] = slots[away * cap : (away + 1) * cap]
            message_ref[cap : cap + EXTRA, :] = jnp.broadcast_to(ids_ref[away : away + 1, :], (EXTRA, 128)).astype(BF16)
            if away == 1:
                message_ref[cap + EXTRA :, :] = nodes[NODE_DEV:].astype(BF16)


def sources(offsets, place, chunks, source, panel_values, sums, matrices=None, sections=None):
    blocks, span = source.shape[1:3]
    panels = panel_values.shape[0] * BLK
    observers = len(offsets) * span
    first = sums is None
    operands = [place, *chunks, source, panel_values] + ([] if first else list(sums))
    in_specs = [SMEM] + [WHOLE] * (len(operands) - 1)
    scratch = [
        VMEM((observers, 128), F32),
        VMEM((observers, 128), F32),
        VMEM((blocks, BLK, 2 * observers), BF16),
        VMEM((blocks, BLK, observers), BF16),
        VMEM((blocks, 2 * observers, TW), BF16),
    ]
    aliases = {}
    if matrices is None:
        out_shape = [jax.ShapeDtypeStruct((panels, TW), F32)] * 2
        if not first:
            aliases = {len(operands) - 2: 0, len(operands) - 1: 1}
    else:
        operands += list(matrices)
        in_specs += [WHOLE] * 3
        cap = 2 * CELL_DEV // sections
        out_shape = [jax.ShapeDtypeStruct((NODE_DEV, TW), F32), jax.ShapeDtypeStruct((HEAD, TW), F32)]
        for away in range(sections):
            rows = cap + EXTRA + (HEAD if away == 1 else 0)
            out_shape.append(jax.ShapeDtypeStruct((rows, TW), BF16))
        scratch = [VMEM((panels, TW), BF16)] * 2 + scratch
    return call(
        functools.partial(sources_kernel, offsets, first, sections),
        "sources",
        out_shape,
        in_specs,
        [WHOLE] * len(out_shape),
        scratch,
        aliases,
        work=3_000_000_000,
    )(*operands)


def finish_kernel(*refs):
    sections = len(refs) - 8
    messages = refs[:sections]
    head_ref, _, node_ref, cell_ref, rows_ref, top_ref, total_ref, sems = refs[sections:]
    rim_rows = messages[1].shape[0] - HEAD
    cap = rim_rows - EXTRA
    per = 128 // cap
    top_ref[...] = head_ref[...] + messages[1][rim_rows:, :].astype(F32)
    top_copy = pltpu.make_async_copy(top_ref, node_ref.at[pl.ds(0, HEAD), :], sems.at[0])
    top_copy.start()
    total = jnp.zeros((CELL_DEV, TW), F32)
    cell = lax.broadcasted_iota(jnp.int32, (CELL_DEV, 128), 0).astype(F32)
    for group in range(sections // per):
        ids = jnp.zeros((EXTRA, 128), F32)
        for inner in range(per):
            message = messages[group * per + inner]
            ids = ids + message[cap : cap + EXTRA, :].astype(F32)
            rows_ref[group * 128 + inner * cap : group * 128 + (inner + 1) * cap, :] = message[:cap, :]
        match = jnp.where(ids[:1] == cell, 1.0, 0.0).astype(BF16)
        total = total + jnp.dot(match, rows_ref[group * 128 : (group + 1) * 128, :], preferred_element_type=F32)
    total_ref[...] = total
    cell_copy = pltpu.make_async_copy(total_ref, cell_ref, sems.at[1])
    cell_copy.start()
    top_copy.wait()
    cell_copy.wait()


def finish(messages, head, nodes):
    sections = len(messages)
    cap = messages[0].shape[0] - EXTRA
    return call(
        finish_kernel,
        "finish",
        (
            jax.ShapeDtypeStruct((NODE_DEV, TW), F32),
            jax.ShapeDtypeStruct((CELL_DEV, TW), F32),
        ),
        [WHOLE] * (sections + 1) + [PLACE],
        [PLACE] * 2,
        [VMEM((sections * cap, TW), BF16), VMEM((HEAD, TW), F32), VMEM((CELL_DEV, TW), F32), COPY((2,))],
        {sections + 1: 0},
    )(*messages, head, nodes)


def swapped(array, axis, bit):
    peers = lax.axis_size(axis)
    return lax.ppermute(array, axis, [(i, i ^ bit) for i in range(peers)])


def shifted(array, axis, by):
    peers = lax.axis_size(axis)
    return lax.ppermute(array, axis, [(i, (i + by) % peers) for i in range(peers)])


def section_chunk(place, signals, xyz):
    count, width = signals.shape
    sections = lax.axis_size("sect")
    if count % 16 == 0:
        turned = xyz.T
        pieces = [signals] + [shifted(signals, "sect", by) for by in range(1, sections)]
        points = [turned] + [shifted(turned, "sect", by) for by in range(1, sections)]
        return join(sections, place, pieces, points)
    extra = jnp.zeros((EXTRA, width), BF16)
    extra = lax.dynamic_update_slice(extra, xyz.T, (0, lax.axis_index("sect") * count))
    payload = jnp.concatenate([signals, extra], 0)
    everyone = jnp.broadcast_to(payload[None], (sections,) + payload.shape)
    received = lax.all_to_all(everyone, "sect", split_axis=0, concat_axis=0, tiled=True)
    return jnp.concatenate(
        [received[:, :count].reshape(sections * count, -1), received[:, count:].astype(F32).sum(0).astype(BF16)], 0
    )


def per_device(signals, observer_xyz, panel_geometry, delays, counts, connectivity, owners):
    sections = lax.axis_size("sect")
    groups = lax.axis_size("azim")
    place = jnp.stack([lax.axis_index("sect"), counts[0], lax.axis_index("azim")]).astype(jnp.int32)
    chunks = {0: section_chunk(place, signals, observer_xyz)}
    bit = groups // 2
    while bit:
        for offset in list(chunks):
            chunks[offset ^ bit] = swapped(chunks[offset], "azim", bit)
        bit //= 2
    order = list(chunks)
    corners, slots, ids, source, panel_values = route(
        sections, groups, place, connectivity, owners, delays, panel_geometry
    )
    sums = None
    half = groups // 2 + 1
    for offsets in (order[:1], order[1:half]):
        sums = sources(offsets, place, [chunks[o] for o in offsets], source, panel_values, sums)
    offsets = order[half:]
    nodes, head, *messages = sources(
        offsets, place, [chunks[o] for o in offsets], source, panel_values, sums, (corners, slots, ids), sections
    )
    messages = messages[:1] + [shifted(m, "sect", by) for by, m in enumerate(messages) if by]
    return finish(messages, head, nodes)


def solution(mesh):
    in_specs = (
        P(("azim", "sect"), None),
        P(("azim", "sect"), None),
        P(None, ("azim", "sect")),
        P(("azim", "sect"), None),
        P(("azim", "sect")),
        P(None, ("azim", "sect")),
        P(("azim", "sect")),
    )
    out_specs = (P(("azim", "sect"), None), P(("azim", "sect"), None))
    return jax.shard_map(
        per_device, mesh=mesh, in_specs=in_specs, out_specs=out_specs, check_vma=False
    )
```

```python
import functools

import jax
import jax.numpy as jnp
from jax import lax
from jax.experimental import pallas as pl
from jax.experimental.pallas import tpu as pltpu
from jax.sharding import PartitionSpec as P

NPU = 128
BLK = 128
TW = 128
CELL_DEV = 256
NODE_DEV = 1032
RIM = NPU + 1
HEAD = 136
NODE_ROWS = 1168
EXTRA = 16
F32 = jnp.float32
BF16 = jnp.bfloat16
VMEM = pltpu.VMEM
SMEM = pl.BlockSpec(memory_space=pltpu.SMEM)
WHOLE = pl.BlockSpec(memory_space=pltpu.VMEM)
PLACE = pl.BlockSpec(memory_space=pl.ANY)
FAR = pl.BlockSpec(memory_space=pltpu.HBM)
COPY = pltpu.SemaphoreType.DMA


def call(kernel, name, out_shape, in_specs, out_specs, scratch_shapes=(), aliases=None, work=1_000_000):
    return pl.pallas_call(
        kernel,
        out_shape=out_shape,
        in_specs=in_specs,
        out_specs=out_specs,
        scratch_shapes=list(scratch_shapes),
        input_output_aliases=aliases or {},
        compiler_params=pltpu.CompilerParams(vmem_limit_bytes=24 * 1024 * 1024),
        cost_estimate=pl.CostEstimate(flops=work, bytes_accessed=4_000_000, transcendentals=0),
        name=name,
    )


def fetch(pairs, sems):
    copies = [pltpu.make_async_copy(source, target, sems.at[i]) for i, (source, target) in enumerate(pairs)]
    for copy in copies:
        copy.start()
    for copy in copies:
        copy.wait()


def window_kernel(sections, paired, place_ref, delay_at, source_ref, delay_ref, sems):
    fetch([(delay_at, delay_ref)], sems)
    groups, blocks, span, _ = source_ref.shape
    count = span // sections
    piece_rows = count if paired else 128
    lanes = lax.broadcasted_iota(jnp.int32, (piece_rows, 128), 1)
    for piece in range(groups * span // 128):
        columns = delay_ref[:, piece * 128 : (piece + 1) * 128].T
        for part in range(128 // piece_rows):
            row = piece * 128 + part * piece_rows
            begin = row % span
            if paired:
                apart = place_ref[0] ^ (begin // count)
                begin = pl.multiple_of((apart // 2 + apart % 2 * (sections // 2)) * count, count)
            for block in range(blocks):
                column = columns[part * piece_rows : (part + 1) * piece_rows, block : block + 1]
                source_ref[row // span, block, pl.ds(begin, piece_rows), :] = (
                    jnp.broadcast_to(column, (piece_rows, 128)) + lanes
                )


def window_index(sections, groups, paired, place, delays):
    blocks, observers = delays.shape
    return call(
        functools.partial(window_kernel, sections, paired),
        "windows",
        jax.ShapeDtypeStruct((groups, blocks, observers // groups, 128), jnp.int32),
        [SMEM, FAR],
        WHOLE,
        [VMEM(delays.shape, jnp.int32), COPY((1,))],
        work=2_000_000_000,
    )(place, delays)


def column_kernel(
    sections, place_ref, geometry_at, owner_at, panel_ref, slot_ref, ids_ref, geometry_ref, owner_ref, sems
):
    fetch([(geometry_at, geometry_ref), (owner_at, owner_ref)], sems)
    panels = geometry_ref.shape[1]
    for block in range(panels // BLK):
        values = geometry_ref[:, block * BLK : (block + 1) * BLK]
        columns = jnp.concatenate([values, values[:1]], 0).T
        for part in range(7):
            column = columns[:, part : part + 1] * (0.25 if part < 3 else 1.0)
            panel_ref[block, part] = jnp.broadcast_to(column, (BLK, 128))

    cap = slot_ref.shape[0] // sections
    padded = ids_ref.shape[0]
    section = place_ref[0]
    live = place_ref[1]
    owner = owner_ref[...]
    dest = owner // CELL_DEV
    lane = lax.broadcasted_iota(jnp.int32, (padded, panels), 1)
    mine = dest == lax.broadcasted_iota(jnp.int32, (padded, panels), 0)
    count = jnp.where(mine, 1, 0)
    span = 1
    while span < panels:
        count = count + jnp.where(lane >= span, pltpu.roll(count, span, 1), 0)
        span *= 2
    before = jnp.sum(jnp.where(mine, count - 1, 0), axis=0, keepdims=True)
    rank = before // 4
    slot = dest * cap + rank

    def slot_rows(step, carried):
        row = pl.multiple_of(step * 16, 16)
        number = row + lax.broadcasted_iota(jnp.int32, (16, panels), 0)
        panel = lax.broadcasted_iota(jnp.int32, (16, panels), 1)
        number = jnp.where(panel < live, number, -1)
        slot_ref[pl.ds(row, 16), :] = jnp.where(slot == number, 1.0, 0.0).astype(BF16)
        return carried

    lax.fori_loop(0, slot_ref.shape[0] // 16, slot_rows, 0)

    at_lane = rank + section * cap % 128 == lax.broadcasted_iota(jnp.int32, (128, panels), 0)
    at_lane = jnp.where(at_lane, 1.0, 0.0).astype(BF16)
    cell = jnp.where(mine & (lane % 4 == 0), owner % CELL_DEV, 0).astype(F32).astype(BF16)
    ids_ref[...] = lax.dot_general(cell, at_lane, (((1,), (1,)), ((), ())), preferred_element_type=F32)


def panel_columns(sections, place, geometry, owners):
    panels = geometry.shape[1]
    cap = 2 * CELL_DEV // sections
    padded = -(-sections // EXTRA) * EXTRA
    return call(
        functools.partial(column_kernel, sections),
        "columns",
        (
            jax.ShapeDtypeStruct((panels // BLK, 7, BLK, 128), F32),
            jax.ShapeDtypeStruct((sections * cap, panels), BF16),
            jax.ShapeDtypeStruct((padded, 128), F32),
        ),
        [SMEM, FAR, FAR],
        [WHOLE] * 3,
        [VMEM(geometry.shape, F32), VMEM((1, panels), jnp.int32), COPY((2,))],
        work=2_000_000_000,
    )(place, geometry, owners.reshape(1, panels))


def corner_kernel(place_ref, conn_at, corner_ref, conn_ref, sems):
    fetch([(conn_at, conn_ref)], sems)
    panels = conn_ref.shape[1]
    live = place_ref[1]

    def corner_rows(step, carried):
        row = pl.multiple_of(step * 16, 16)
        node = row + lax.broadcasted_iota(jnp.int32, (16, panels), 0)
        panel = lax.broadcasted_iota(jnp.int32, (16, panels), 1)
        node = jnp.where(panel < live, node, -1)
        total = jnp.zeros((16, panels), F32)
        for corner in range(4):
            total = total + jnp.where(conn_ref[corner : corner + 1, :] == node, 0.25, 0.0)
        corner_ref[pl.ds(row, 16), :] = total.astype(BF16)
        return carried

    lax.fori_loop(0, NODE_ROWS // 16, corner_rows, 0)


def corner_matrix(place, connectivity):
    return call(
        corner_kernel,
        "corners",
        jax.ShapeDtypeStruct((NODE_ROWS, connectivity.shape[1]), BF16),
        [SMEM, FAR],
        WHOLE,
        [VMEM(connectivity.shape, jnp.int32), COPY((1,))],
        work=2_000_000_000,
    )(place, connectivity)


def first_join_kernel(mine_ref, other_ref, my_points_ref, other_points_ref, chunk_ref, wide_ref):
    count = mine_ref.shape[0]
    chunk_ref[:count, :] = mine_ref[...]
    chunk_ref[count : 2 * count, :] = other_ref[...]
    wide_ref[...] = jnp.zeros_like(wide_ref)
    wide_ref[:3, :count] = other_points_ref[...].astype(F32)
    moved = pltpu.roll(wide_ref[...], count, 1)
    wide_ref[:3, :count] = my_points_ref[...].astype(F32)
    wide_ref[3:, :count] = jnp.zeros((EXTRA - 3, count), F32)
    chunk_ref[2 * count :, :] = (moved + wide_ref[...]).astype(BF16)


def join_kernel(mine_ref, other_ref, chunk_ref):
    span = mine_ref.shape[0] - EXTRA
    chunk_ref[:span, :] = mine_ref[:span, :]
    chunk_ref[span : 2 * span, :] = other_ref[:span, :]
    moved = pltpu.roll(other_ref[span:, :].astype(F32), span, 1)
    chunk_ref[2 * span :, :] = (mine_ref[span:, :].astype(F32) + moved).astype(BF16)


def sources_kernel(offsets, first, final, place_ref, *refs):
    refs = list(refs)

    def take(number):
        taken = refs[:number]
        del refs[:number]
        return taken

    parts = len(offsets)
    chunks = take(parts)
    source_ref, panel_ref = take(2)
    loading_in, thick_in = (None, None) if first else take(2)
    if final:
        corner_ref, node_ref, head_ref, rim_ref, thick_ref, loading_ref = take(6)
    else:
        loading_ref, thick_ref = take(2)
    low_ref, high_ref, pair_ref, mass_ref, window_ref = take(5)

    blocks, span = source_ref.shape[1:3]
    panels = panel_ref.shape[0] * BLK
    observers = parts * span
    points = []
    for number, chunk in enumerate(chunks):
        low_ref[number * span : (number + 1) * span, :] = chunk[:span, :128].astype(F32)
        high_ref[number * span : (number + 1) * span, :] = chunk[:span, 128:].astype(F32)
        points.append(chunk[span : span + EXTRA, :].astype(F32) * 0.25)

    lanes = lax.broadcasted_iota(jnp.int32, (128, 128), 1)
    for block in range(blocks):
        for number, offset in enumerate(offsets):
            group = place_ref[2] ^ offset
            for piece in range(span // 128):
                here = number * span + piece * 128
                source = source_ref[group, block, piece * 128 : (piece + 1) * 128, :]
                at = source & 127
                low = jnp.take_along_axis(low_ref[here : here + 128, :], at, axis=1, mode="promise_in_bounds")
                high = jnp.take_along_axis(high_ref[here : here + 128, :], at, axis=1, mode="promise_in_bounds")
                current = jnp.where(source < 128, low, high)
                following = pltpu.roll(jnp.where(lanes == 0, high, current), 127, 1)
                window_ref[block, here : here + 128, :] = current.astype(BF16)
                window_ref[block, observers + here : observers + here + 128, :] = (following - current).astype(BF16)

                at_x, at_y, at_z = (points[number][i : i + 1, piece * 128 : piece * 128 + 128] for i in range(3))
                for strip in range(BLK // 16):
                    rows = slice(strip * 16, strip * 16 + 16)
                    delta_x = at_x - panel_ref[block, 0, rows, :]
                    delta_y = at_y - panel_ref[block, 1, rows, :]
                    delta_z = at_z - panel_ref[block, 2, rows, :]
                    inverse = lax.rsqrt(delta_x * delta_x + delta_y * delta_y + delta_z * delta_z)
                    flux = (
                        panel_ref[block, 3, rows, :] * delta_x
                        + panel_ref[block, 4, rows, :] * delta_y
                        + panel_ref[block, 5, rows, :] * delta_z
                    )
                    far = flux * inverse * inverse
                    pair_ref[block, rows, here : here + 128] = (far * inverse).astype(BF16)
                    pair_ref[block, rows, observers + here : observers + here + 128] = far.astype(BF16)
                    mass_ref[block, rows, here : here + 128] = (panel_ref[block, 6, rows, :] * inverse).astype(BF16)
        rows = slice(block * BLK, (block + 1) * BLK)
        loading = jnp.dot(pair_ref[block], window_ref[block], preferred_element_type=F32)
        thick = jnp.dot(mass_ref[block], window_ref[block, observers:, :], preferred_element_type=F32)
        if not first:
            loading = loading + loading_in[rows, :]
            thick = thick + thick_in[rows, :]
        if final:
            alive = block * BLK + lax.broadcasted_iota(jnp.int32, (BLK, TW), 0) < place_ref[1]
            loading = jnp.where(alive, loading, 0.0).astype(BF16)
            thick = jnp.where(alive, thick, 0.0).astype(BF16)
        loading_ref[rows, :] = loading
        thick_ref[rows, :] = thick

    if final:
        nodes = jnp.dot(corner_ref[...], loading_ref[...], preferred_element_type=F32)
        head_ref[...] = nodes[:HEAD]
        rim_ref[...] = nodes[NODE_DEV:].astype(BF16)
        node_ref[...] = nodes[:NODE_DEV]


def sources(offsets, place, chunks, source, panel_values, sums, corners=None):
    blocks, span = source.shape[1:3]
    panels = panel_values.shape[0] * BLK
    observers = len(offsets) * span
    first = sums is None
    operands = [place, *chunks, source, panel_values] + ([] if first else list(sums))
    in_specs = [SMEM] + [WHOLE] * (len(operands) - 1)
    scratch = [
        VMEM((observers, 128), F32),
        VMEM((observers, 128), F32),
        VMEM((blocks, BLK, 2 * observers), BF16),
        VMEM((blocks, BLK, observers), BF16),
        VMEM((blocks, 2 * observers, TW), BF16),
    ]
    aliases = {}
    if corners is None:
        out_shape = [jax.ShapeDtypeStruct((panels, TW), F32)] * 2
        if not first:
            aliases = {len(operands) - 2: 0, len(operands) - 1: 1}
    else:
        operands.append(corners)
        in_specs.append(WHOLE)
        out_shape = [
            jax.ShapeDtypeStruct((NODE_DEV, TW), F32),
            jax.ShapeDtypeStruct((HEAD, TW), F32),
            jax.ShapeDtypeStruct((HEAD, TW), BF16),
            jax.ShapeDtypeStruct((panels, TW), BF16),
        ]
        scratch = [VMEM((panels, TW), BF16)] + scratch
    return call(
        functools.partial(sources_kernel, offsets, first, corners is not None),
        "sources",
        out_shape,
        in_specs,
        [WHOLE] * len(out_shape),
        scratch,
        aliases,
        work=3_000_000_000,
    )(*operands)


def slot_kernel(slot_ref, ids_ref, thick_ref, message_ref):
    sections = message_ref.shape[0]
    cap = slot_ref.shape[0] // sections
    slots = jnp.dot(slot_ref[...], thick_ref[...], preferred_element_type=F32).astype(BF16)
    for section in range(sections):
        message_ref[section, :cap, :] = slots[section * cap : (section + 1) * cap]
        ids = jnp.broadcast_to(ids_ref[section : section + 1, :], (EXTRA, 128))
        message_ref[section, cap:, :] = ids.astype(BF16)


def slot_messages(sections, slots, ids, thick):
    cap = 2 * CELL_DEV // sections
    return call(
        slot_kernel,
        "slots",
        jax.ShapeDtypeStruct((sections, cap + EXTRA, TW), BF16),
        [WHOLE] * 3,
        WHOLE,
    )(slots, ids, thick)


def finish_kernel(message_ref, rim_ref, head_ref, _, node_ref, cell_ref, rows_ref, top_ref, total_ref, sems):
    sections = message_ref.shape[0]
    cap = message_ref.shape[1] - EXTRA
    per = 128 // cap
    top_ref[...] = head_ref[...] + rim_ref[...].astype(F32)
    top_copy = pltpu.make_async_copy(top_ref, node_ref.at[pl.ds(0, HEAD), :], sems.at[0])
    top_copy.start()
    total = jnp.zeros((CELL_DEV, TW), F32)
    cell = lax.broadcasted_iota(jnp.int32, (CELL_DEV, 128), 0).astype(F32)
    for group in range(sections // per):
        ids = jnp.zeros((EXTRA, 128), F32)
        for inner in range(per):
            section = group * per + inner
            ids = ids + message_ref[section, cap:, :].astype(F32)
            rows_ref[section * cap : (section + 1) * cap, :] = message_ref[section, :cap, :]
        match = jnp.where(ids[:1] == cell, 1.0, 0.0).astype(BF16)
        total = total + jnp.dot(match, rows_ref[group * 128 : (group + 1) * 128, :], preferred_element_type=F32)
    total_ref[...] = total
    cell_copy = pltpu.make_async_copy(total_ref, cell_ref, sems.at[1])
    cell_copy.start()
    top_copy.wait()
    cell_copy.wait()


def finish(message, rim, head, nodes):
    sections = message.shape[0]
    cap = message.shape[1] - EXTRA
    return call(
        finish_kernel,
        "finish",
        (
            jax.ShapeDtypeStruct((NODE_DEV, TW), F32),
            jax.ShapeDtypeStruct((CELL_DEV, TW), F32),
        ),
        [WHOLE] * 3 + [PLACE],
        [PLACE] * 2,
        [VMEM((sections * cap, TW), BF16), VMEM((HEAD, TW), F32), VMEM((CELL_DEV, TW), F32), COPY((2,))],
        {3: 0},
    )(message, rim, head, nodes)


def swapped(array, axis, bit):
    peers = lax.axis_size(axis)
    return lax.ppermute(array, axis, [(i, i ^ bit) for i in range(peers)])


def joined(mine, other):
    span = mine.shape[0] - EXTRA
    shape = jax.ShapeDtypeStruct((2 * span + EXTRA, mine.shape[1]), BF16)
    return call(join_kernel, "join", shape, [WHOLE] * 2, WHOLE)(mine, other)


def paired_chunk(signals, xyz, sections, local):
    count, width = signals.shape
    turned = xyz.T
    bit = 2
    other, other_points = swapped(signals, "sect", bit), swapped(turned, "sect", bit)
    shape = jax.ShapeDtypeStruct((2 * count + EXTRA, width), BF16)
    done = [local[0]()]
    chunk = call(first_join_kernel, "pair", shape, [WHOLE] * 4, WHOLE, [VMEM((EXTRA, width), F32)])(
        signals, other, turned, other_points
    )
    for step in range(2, sections.bit_length()):
        bit = bit * 2 if bit * 2 < sections else 1
        other = swapped(chunk, "sect", bit)
        done.append(local[step - 1](chunk) if step <= len(local) else None)
        chunk = joined(chunk, other)
    return chunk, done


def spread_chunk(signals, xyz, sections):
    count, width = signals.shape
    extra = jnp.zeros((EXTRA, width), BF16)
    extra = lax.dynamic_update_slice(extra, xyz.T, (0, lax.axis_index("sect") * count))
    payload = jnp.concatenate([signals, extra], 0)
    everyone = jnp.broadcast_to(payload[None], (sections,) + payload.shape)
    received = lax.all_to_all(everyone, "sect", split_axis=0, concat_axis=0, tiled=True)
    return jnp.concatenate(
        [received[:, :count].reshape(sections * count, -1), received[:, count:].astype(F32).sum(0).astype(BF16)], 0
    )


def per_device(signals, observer_xyz, panel_geometry, delays, counts, connectivity, owners):
    sections = lax.axis_size("sect")
    groups = lax.axis_size("azim")
    place = jnp.stack([lax.axis_index("sect"), counts[0], lax.axis_index("azim")]).astype(jnp.int32)
    paired = sections == 8 and signals.shape[0] % 16 == 0

    def windows():
        return window_index(sections, groups, paired, place, delays)

    def columns(after=None):
        geometry = panel_geometry
        if after is not None:
            geometry, _ = lax.optimization_barrier((geometry, after))
        return panel_columns(sections, place, geometry, owners)

    def corners(after=None):
        nodes = connectivity
        if after is not None:
            nodes, _ = lax.optimization_barrier((nodes, after))
        return corner_matrix(place, nodes)

    if paired:
        chunk, done = paired_chunk(signals, observer_xyz, sections, (windows, columns, corners))
        source, (panel_values, slots, ids), corner_values = done
    else:
        chunk = spread_chunk(signals, observer_xyz, sections)
        source, (panel_values, slots, ids), corner_values = windows(), columns(), corners()
    chunks = {0: chunk}
    bit = groups // 2
    while bit:
        for offset in list(chunks):
            chunks[offset ^ bit] = swapped(chunks[offset], "azim", bit)
        bit //= 2
    sums = None
    for offsets in ([0], [1]):
        sums = sources(offsets, place, [chunks[o] for o in offsets], source, panel_values, sums)
    offsets = [o for o in chunks if o > 1]
    nodes, head, rim, thick = sources(
        offsets, place, [chunks[o] for o in offsets], source, panel_values, sums, corner_values
    )
    rim = lax.ppermute(rim, "sect", [(i, (i + 1) % sections) for i in range(sections)])
    message = slot_messages(sections, slots, ids, thick)
    message = lax.all_to_all(message, "sect", split_axis=0, concat_axis=0, tiled=True)
    return finish(message, rim, head, nodes)


def solution(mesh):
    in_specs = (
        P(("azim", "sect"), None),
        P(("azim", "sect"), None),
        P(None, ("azim", "sect")),
        P(("azim", "sect"), None),
        P(("azim", "sect")),
        P(None, ("azim", "sect")),
        P(("azim", "sect")),
    )
    out_specs = (P(("azim", "sect"), None), P(("azim", "sect"), None))
    return jax.shard_map(
        per_device, mesh=mesh, in_specs=in_specs, out_specs=out_specs, check_vma=False
    )
```

```python
import functools

import jax
import jax.numpy as jnp
from jax import lax
from jax.experimental import pallas as pl
from jax.experimental.pallas import tpu as pltpu
from jax.sharding import PartitionSpec as P

NPU = 128
BLK = 128
TW = 128
CELL_DEV = 256
NODE_DEV = 1032
RIM = NPU + 1
HEAD = 136
NODE_ROWS = 1168
EXTRA = 16
F32 = jnp.float32
BF16 = jnp.bfloat16
VMEM = pltpu.VMEM
SMEM = pl.BlockSpec(memory_space=pltpu.SMEM)
WHOLE = pl.BlockSpec(memory_space=pltpu.VMEM)
PLACE = pl.BlockSpec(memory_space=pl.ANY)
COPY = pltpu.SemaphoreType.DMA


def call(kernel, name, out_shape, in_specs, out_specs, scratch_shapes=(), aliases=None, work=1_000_000):
    return pl.pallas_call(
        kernel,
        out_shape=out_shape,
        in_specs=in_specs,
        out_specs=out_specs,
        scratch_shapes=list(scratch_shapes),
        input_output_aliases=aliases or {},
        compiler_params=pltpu.CompilerParams(vmem_limit_bytes=24 * 1024 * 1024),
        cost_estimate=pl.CostEstimate(flops=work, bytes_accessed=4_000_000, transcendentals=0),
        name=name,
    )


def window_kernel(sections, paired, delay_ref, source_ref):
    groups, blocks, span, _ = source_ref.shape
    count = span // sections
    piece_rows = count if paired else 128
    padded = -(-blocks // 16) * 16
    delay = delay_ref[...].astype(F32)
    delay = jnp.concatenate([delay, jnp.zeros((padded - blocks, delay.shape[1]), F32)], 0).astype(BF16)
    spread = (padded, blocks * 128)
    spread = lax.broadcasted_iota(jnp.int32, spread, 1) // 128 == lax.broadcasted_iota(jnp.int32, spread, 0)
    spread = jnp.where(spread, 1.0, 0.0).astype(BF16)
    lanes = lax.broadcasted_iota(jnp.int32, (128, 128), 1)
    for piece in range(groups * span // 128):
        columns = lax.dot_general(
            delay[:, piece * 128 : (piece + 1) * 128], spread, (((0,), (0,)), ((), ())), preferred_element_type=F32
        )
        for block in range(blocks):
            source = columns[:, block * 128 : (block + 1) * 128].astype(jnp.int32) + lanes
            for part in range(128 // piece_rows):
                row = piece * 128 + part * piece_rows
                begin = row % span
                if paired:
                    apart = lax.axis_index("sect") ^ (begin // count)
                    begin = pl.multiple_of((apart // 2 + apart % 2 * (sections // 2)) * count, count)
                source_ref[row // span, block, pl.ds(begin, piece_rows), :] = source[
                    part * piece_rows : (part + 1) * piece_rows
                ]


def window_index(sections, groups, paired, delays):
    blocks, observers = delays.shape
    return call(
        functools.partial(window_kernel, sections, paired),
        "windows",
        jax.ShapeDtypeStruct((groups, blocks, observers // groups, 128), jnp.int32),
        [WHOLE],
        WHOLE,
        work=2_000_000_000,
    )(delays)


def column_kernel(sections, count_ref, geometry_ref, owner_ref, panel_ref, slot_ref, ids_ref):
    panels = geometry_ref.shape[1]
    spread = (32, 7 * 128)
    number = lax.broadcasted_iota(jnp.int32, spread, 0)
    spread = (lax.broadcasted_iota(jnp.int32, spread, 1) // 128 == number % 8) & (number < 24)
    spread = jnp.where(spread, 1.0, 0.0).astype(BF16)
    scale = jnp.where(lax.broadcasted_iota(jnp.int32, (8, BLK), 0) < 3, 0.25, 1.0)
    for block in range(panels // BLK):
        values = geometry_ref[:, block * BLK : (block + 1) * BLK]
        values = jnp.concatenate([values, values[:1]], 0) * scale
        high = values.astype(BF16).astype(F32)
        middle = (values - high).astype(BF16).astype(F32)
        parts = jnp.concatenate([high, middle, values - high - middle, jnp.zeros_like(values)], 0).astype(BF16)
        columns = lax.dot_general(parts, spread, (((0,), (0,)), ((), ())), preferred_element_type=F32)
        for part in range(7):
            panel_ref[block, part] = columns[:, part * 128 : (part + 1) * 128]

    cap = slot_ref.shape[0] // sections
    padded = ids_ref.shape[0]
    owner = owner_ref[...]
    dest = owner // CELL_DEV
    lane = lax.broadcasted_iota(jnp.int32, (padded, panels), 1)
    mine = dest == lax.broadcasted_iota(jnp.int32, (padded, panels), 0)
    ones = jnp.where(mine, 1.0, 0.0).astype(BF16)
    square = (128, 128)
    upto = lax.broadcasted_iota(jnp.int32, square, 0) <= lax.broadcasted_iota(jnp.int32, square, 1)
    upto = jnp.where(upto, 1.0, 0.0).astype(BF16)
    every = jnp.ones(square, BF16)
    carry = jnp.zeros((padded, 128), F32)
    counts = []
    for begin in range(0, panels, 128):
        piece = ones[:, begin : begin + 128]
        counts.append(carry + jnp.dot(piece, upto, preferred_element_type=F32))
        carry = carry + jnp.dot(piece, every, preferred_element_type=F32)
    count = jnp.concatenate(counts, 1).astype(jnp.int32)
    before = jnp.sum(jnp.where(mine, count - 1, 0), axis=0, keepdims=True)
    rank = before // 4
    slot = jnp.where(lane[:1] < count_ref[0], dest * cap + rank, -1)
    slot = jnp.broadcast_to(slot, (16, panels)).astype(jnp.int16)
    number = lax.broadcasted_iota(jnp.int16, (16, panels), 0)
    one, zero = jnp.array(1, BF16), jnp.array(0, BF16)
    for row in range(0, slot_ref.shape[0], 16):
        slot_ref[row : row + 16, :] = jnp.where(slot == number + jnp.int16(row), one, zero)

    at_lane = rank + lax.axis_index("sect") * cap % 128 == lax.broadcasted_iota(jnp.int32, (128, panels), 0)
    at_lane = jnp.where(at_lane, 1.0, 0.0).astype(BF16)
    cell = jnp.where(mine & (lane % 4 == 0), owner % CELL_DEV, 0).astype(F32).astype(BF16)
    ids_ref[...] = lax.dot_general(cell, at_lane, (((1,), (1,)), ((), ())), preferred_element_type=F32)


def panel_columns(sections, counts, geometry, owners):
    panels = geometry.shape[1]
    cap = 2 * CELL_DEV // sections
    padded = -(-sections // EXTRA) * EXTRA
    return call(
        functools.partial(column_kernel, sections),
        "columns",
        (
            jax.ShapeDtypeStruct((panels // BLK, 7, BLK, 128), F32),
            jax.ShapeDtypeStruct((sections * cap, panels), BF16),
            jax.ShapeDtypeStruct((padded, 128), F32),
        ),
        [SMEM, WHOLE, WHOLE],
        [WHOLE] * 3,
        work=2_000_000_000,
    )(counts, geometry, owners.reshape(1, panels))


def corner_kernel(count_ref, conn_ref, corner_ref):
    panels = conn_ref.shape[1]
    live = lax.broadcasted_iota(jnp.int32, (16, panels), 1) < count_ref[0]
    corners = [
        jnp.where(live, jnp.broadcast_to(conn_ref[i : i + 1, :], (16, panels)), -1).astype(jnp.int16) for i in range(4)
    ]
    number = lax.broadcasted_iota(jnp.int16, (16, panels), 0)
    share, zero = jnp.array(0.25, BF16), jnp.array(0, BF16)
    for row in range(0, NODE_ROWS, 16):
        node = number + jnp.int16(row)
        total = jnp.where(corners[0] == node, share, zero)
        for corner in corners[1:]:
            total = total + jnp.where(corner == node, share, zero)
        corner_ref[row : row + 16, :] = total


def corner_matrix(counts, connectivity):
    return call(
        corner_kernel,
        "corners",
        jax.ShapeDtypeStruct((NODE_ROWS, connectivity.shape[1]), BF16),
        [SMEM, WHOLE],
        WHOLE,
        work=2_000_000_000,
    )(counts, connectivity)


def first_join_kernel(mine_ref, other_ref, my_points_ref, other_points_ref, chunk_ref, wide_ref):
    count = mine_ref.shape[0]
    chunk_ref[:count, :] = mine_ref[...]
    chunk_ref[count : 2 * count, :] = other_ref[...]
    wide_ref[...] = jnp.zeros_like(wide_ref)
    wide_ref[:3, :count] = other_points_ref[...].astype(F32)
    moved = pltpu.roll(wide_ref[...], count, 1)
    wide_ref[:3, :count] = my_points_ref[...].astype(F32)
    wide_ref[3:, :count] = jnp.zeros((EXTRA - 3, count), F32)
    chunk_ref[2 * count :, :] = (moved + wide_ref[...]).astype(BF16)


def join_kernel(mine_ref, other_ref, chunk_ref):
    span = mine_ref.shape[0] - EXTRA
    chunk_ref[:span, :] = mine_ref[:span, :]
    chunk_ref[span : 2 * span, :] = other_ref[:span, :]
    moved = pltpu.roll(other_ref[span:, :].astype(F32), span, 1)
    chunk_ref[2 * span :, :] = (mine_ref[span:, :].astype(F32) + moved).astype(BF16)


def sources_kernel(offsets, first, last, count_ref, *refs):
    refs = list(refs)

    def take(number):
        taken = refs[:number]
        del refs[:number]
        return taken

    parts = len(offsets)
    chunks = take(parts)
    source_ref, panel_ref = take(2)
    if last:
        thick_in, slot_ref, ids_ref, pair_ref, window_ref, message_ref, thick_ref = take(7)
        low_ref, high_ref, mass_ref = take(3)
    else:
        loading_in, thick_in = (None, None) if first else take(2)
        loading_ref, thick_ref = take(2)
        low_ref, high_ref, mass_ref, pair_ref, window_ref = take(5)

    blocks, span = source_ref.shape[1:3]
    observers = parts * span
    points = []
    for number, chunk in enumerate(chunks):
        low_ref[number * span : (number + 1) * span, :] = chunk[:span, :128].astype(F32)
        high_ref[number * span : (number + 1) * span, :] = chunk[:span, 128:].astype(F32)
        points.append(chunk[span : span + EXTRA, :].astype(F32) * 0.25)

    lanes = lax.broadcasted_iota(jnp.int32, (128, 128), 1)
    for block in range(blocks):
        for number, offset in enumerate(offsets):
            group = lax.axis_index("azim") ^ offset
            for piece in range(span // 128):
                here = number * span + piece * 128
                source = source_ref[group, block, piece * 128 : (piece + 1) * 128, :]
                at = source & 127
                low = jnp.take_along_axis(low_ref[here : here + 128, :], at, axis=1, mode="promise_in_bounds")
                high = jnp.take_along_axis(high_ref[here : here + 128, :], at, axis=1, mode="promise_in_bounds")
                current = jnp.where(source < 128, low, high)
                following = pltpu.roll(jnp.where(lanes == 0, high, current).astype(BF16), 127, 1)
                current = current.astype(BF16)
                window_ref[block, here : here + 128, :] = current
                window_ref[block, observers + here : observers + here + 128, :] = following - current

                at_x, at_y, at_z = (points[number][i : i + 1, piece * 128 : piece * 128 + 128] for i in range(3))
                for strip in range(BLK // 16):
                    rows = slice(strip * 16, strip * 16 + 16)
                    delta_x = at_x - panel_ref[block, 0, rows, :]
                    delta_y = at_y - panel_ref[block, 1, rows, :]
                    delta_z = at_z - panel_ref[block, 2, rows, :]
                    inverse = lax.rsqrt(delta_x * delta_x + delta_y * delta_y + delta_z * delta_z)
                    flux = (
                        panel_ref[block, 3, rows, :] * delta_x
                        + panel_ref[block, 4, rows, :] * delta_y
                        + panel_ref[block, 5, rows, :] * delta_z
                    )
                    far = flux * inverse * inverse
                    pair_ref[block, rows, here : here + 128] = (far * inverse).astype(BF16)
                    pair_ref[block, rows, observers + here : observers + here + 128] = far.astype(BF16)
                    mass_ref[block, rows, here : here + 128] = (panel_ref[block, 6, rows, :] * inverse).astype(BF16)
        rows = slice(block * BLK, (block + 1) * BLK)
        thick = jnp.dot(mass_ref[block], window_ref[block, observers:, :], preferred_element_type=F32)
        if not first:
            thick = thick + thick_in[rows, :]
        if last:
            alive = block * BLK + lax.broadcasted_iota(jnp.int32, (BLK, TW), 0) < count_ref[0]
            thick_ref[rows, :] = jnp.where(alive, thick, 0.0).astype(BF16)
            continue
        thick_ref[rows, :] = thick
        loading = jnp.dot(pair_ref[block], window_ref[block], preferred_element_type=F32)
        loading_ref[rows, :] = loading if first else loading + loading_in[rows, :]

    if last:
        sections = message_ref.shape[0]
        cap = slot_ref.shape[0] // sections
        slots = jnp.dot(slot_ref[...], thick_ref[...], preferred_element_type=F32).astype(BF16)
        for section in range(sections):
            message_ref[section, :cap, :] = slots[section * cap : (section + 1) * cap]
            ids = jnp.broadcast_to(ids_ref[section : section + 1, :], (EXTRA, 128))
            message_ref[section, cap:, :] = ids.astype(BF16)


def sources(offsets, counts, chunks, source, panel_values, sums=(), slots=None, sections=None):
    blocks, span = source.shape[1:3]
    panels = panel_values.shape[0] * BLK
    observers = len(offsets) * span
    last = slots is not None
    operands = [counts, *chunks, source, panel_values, *sums]
    scratch = [
        VMEM((observers, 128), F32),
        VMEM((observers, 128), F32),
        VMEM((blocks, BLK, observers), BF16),
    ]
    pair, window = (blocks, BLK, 2 * observers), (blocks, 2 * observers, TW)
    aliases = {}
    if last:
        operands += slots
        cap = 2 * CELL_DEV // sections
        out_shape = [
            jax.ShapeDtypeStruct(pair, BF16),
            jax.ShapeDtypeStruct(window, BF16),
            jax.ShapeDtypeStruct((sections, cap + EXTRA, TW), BF16),
        ]
        scratch = [VMEM((panels, TW), BF16)] + scratch
    else:
        out_shape = [jax.ShapeDtypeStruct((panels, TW), F32)] * 2
        scratch += [VMEM(pair, BF16), VMEM(window, BF16)]
        if sums:
            aliases = {len(operands) - 2: 0, len(operands) - 1: 1}
    return call(
        functools.partial(sources_kernel, offsets, not sums, last),
        "sources",
        out_shape,
        [SMEM] + [WHOLE] * (len(operands) - 1),
        [WHOLE] * len(out_shape),
        scratch,
        aliases,
        work=3_000_000_000,
    )(*operands)


def loading_kernel(count_ref, pair_ref, window_ref, sum_ref, corner_ref, loading_ref, rim_ref):
    for block in range(pair_ref.shape[0]):
        rows = slice(block * BLK, (block + 1) * BLK)
        loading = sum_ref[rows, :] + jnp.dot(pair_ref[block], window_ref[block], preferred_element_type=F32)
        alive = block * BLK + lax.broadcasted_iota(jnp.int32, (BLK, TW), 0) < count_ref[0]
        loading_ref[rows, :] = jnp.where(alive, loading, 0.0).astype(BF16)
    rim = jnp.dot(corner_ref[NODE_DEV - 8 :, :], loading_ref[...], preferred_element_type=F32)
    rim_ref[...] = rim[8:].astype(BF16)


def loading_sums(counts, pair, window, sums, corners):
    panels = sums.shape[0]
    return call(
        loading_kernel,
        "loading",
        (jax.ShapeDtypeStruct((panels, TW), BF16), jax.ShapeDtypeStruct((HEAD, TW), BF16)),
        [SMEM] + [WHOLE] * 4,
        [WHOLE] * 2,
        work=2_000_000_000,
    )(counts, pair, window, sums, corners)


def node_kernel(corner_ref, loading_ref, node_ref, head_ref):
    nodes = jnp.dot(corner_ref[: NODE_DEV + 8, :], loading_ref[...], preferred_element_type=F32)
    head_ref[...] = nodes[:HEAD]
    node_ref[...] = nodes[:NODE_DEV]


def node_sums(corners, loading):
    return call(
        node_kernel,
        "nodes",
        (jax.ShapeDtypeStruct((NODE_DEV, TW), F32), jax.ShapeDtypeStruct((HEAD, TW), F32)),
        [WHOLE] * 2,
        [WHOLE] * 2,
        work=2_000_000_000,
    )(corners, loading)


def finish_kernel(message_ref, rim_ref, head_ref, _, node_ref, cell_ref, rows_ref, top_ref, total_ref, sems):
    sections = message_ref.shape[0]
    cap = message_ref.shape[1] - EXTRA
    per = 128 // cap
    top_ref[...] = head_ref[...] + rim_ref[...].astype(F32)
    top_copy = pltpu.make_async_copy(top_ref, node_ref.at[pl.ds(0, HEAD), :], sems.at[0])
    top_copy.start()
    total = jnp.zeros((CELL_DEV, TW), F32)
    cell = lax.broadcasted_iota(jnp.int32, (CELL_DEV, 128), 0).astype(F32)
    for group in range(sections // per):
        ids = jnp.zeros((EXTRA, 128), F32)
        for inner in range(per):
            section = group * per + inner
            ids = ids + message_ref[section, cap:, :].astype(F32)
            rows_ref[section * cap : (section + 1) * cap, :] = message_ref[section, :cap, :]
        match = jnp.where(ids[:1] == cell, 1.0, 0.0).astype(BF16)
        total = total + jnp.dot(match, rows_ref[group * 128 : (group + 1) * 128, :], preferred_element_type=F32)
    total_ref[...] = total
    cell_copy = pltpu.make_async_copy(total_ref, cell_ref, sems.at[1])
    cell_copy.start()
    top_copy.wait()
    cell_copy.wait()


def finish(message, rim, head, nodes):
    sections = message.shape[0]
    cap = message.shape[1] - EXTRA
    return call(
        finish_kernel,
        "finish",
        (
            jax.ShapeDtypeStruct((NODE_DEV, TW), F32),
            jax.ShapeDtypeStruct((CELL_DEV, TW), F32),
        ),
        [WHOLE] * 3 + [PLACE],
        [PLACE] * 2,
        [VMEM((sections * cap, TW), BF16), VMEM((HEAD, TW), F32), VMEM((CELL_DEV, TW), F32), COPY((2,))],
        {3: 0},
    )(message, rim, head, nodes)


def swapped(array, axis, bit):
    peers = lax.axis_size(axis)
    return lax.ppermute(array, axis, [(i, i ^ bit) for i in range(peers)])


def joined(mine, other):
    span = mine.shape[0] - EXTRA
    shape = jax.ShapeDtypeStruct((2 * span + EXTRA, mine.shape[1]), BF16)
    return call(join_kernel, "join", shape, [WHOLE] * 2, WHOLE)(mine, other)


def paired_chunk(signals, xyz, sections, local):
    count, width = signals.shape
    turned = xyz.T
    bit = 2
    other, other_points = swapped(signals, "sect", bit), swapped(turned, "sect", bit)
    shape = jax.ShapeDtypeStruct((2 * count + EXTRA, width), BF16)
    done = [local[0]()]
    chunk = call(first_join_kernel, "pair", shape, [WHOLE] * 4, WHOLE, [VMEM((EXTRA, width), F32)])(
        signals, other, turned, other_points
    )
    for step in range(2, sections.bit_length()):
        bit = bit * 2 if bit * 2 < sections else 1
        other = swapped(chunk, "sect", bit)
        done.append(local[step - 1](chunk) if step <= len(local) else None)
        chunk = joined(chunk, other)
    return chunk, done


def spread_chunk(signals, xyz, sections):
    count, width = signals.shape
    extra = jnp.zeros((EXTRA, width), BF16)
    extra = lax.dynamic_update_slice(extra, xyz.T, (0, lax.axis_index("sect") * count))
    payload = jnp.concatenate([signals, extra], 0)
    everyone = jnp.broadcast_to(payload[None], (sections,) + payload.shape)
    received = lax.all_to_all(everyone, "sect", split_axis=0, concat_axis=0, tiled=True)
    return jnp.concatenate(
        [received[:, :count].reshape(sections * count, -1), received[:, count:].astype(F32).sum(0).astype(BF16)], 0
    )


def per_device(signals, observer_xyz, panel_geometry, delays, counts, connectivity, owners):
    sections = lax.axis_size("sect")
    groups = lax.axis_size("azim")
    paired = sections == 8 and signals.shape[0] % 16 == 0

    def windows():
        return window_index(sections, groups, paired, delays)

    def columns(after=None):
        geometry = panel_geometry
        if after is not None:
            geometry, _ = lax.optimization_barrier((geometry, after))
        return panel_columns(sections, counts, geometry, owners)

    def corners(after=None):
        nodes = connectivity
        if after is not None:
            nodes, _ = lax.optimization_barrier((nodes, after))
        return corner_matrix(counts, nodes)

    if paired:
        chunk, done = paired_chunk(signals, observer_xyz, sections, (windows, columns, corners))
        source, (panel_values, slots, ids), corner_values = done
    else:
        chunk = spread_chunk(signals, observer_xyz, sections)
        source, (panel_values, slots, ids), corner_values = windows(), columns(), corners()
    chunks = {0: chunk}
    bit = groups // 2
    while bit:
        for offset in list(chunks):
            chunks[offset ^ bit] = swapped(chunks[offset], "azim", bit)
        bit //= 2
    sums = ()
    for offsets in ([0], [1]):
        sums = sources(offsets, counts, [chunks[o] for o in offsets], source, panel_values, sums)
    offsets = [o for o in chunks if o > 1]
    pair, window, message = sources(
        offsets, counts, [chunks[o] for o in offsets], source, panel_values, sums[1:], [slots, ids], sections
    )
    message = lax.all_to_all(message, "sect", split_axis=0, concat_axis=0, tiled=True)
    loading, rim = loading_sums(counts, pair, window, sums[0], corner_values)
    rim = lax.ppermute(rim, "sect", [(i, (i + 1) % sections) for i in range(sections)])
    nodes, head = node_sums(corner_values, loading)
    return finish(message, rim, head, nodes)


def solution(mesh):
    in_specs = (
        P(("azim", "sect"), None),
        P(("azim", "sect"), None),
        P(None, ("azim", "sect")),
        P(("azim", "sect"), None),
        P(("azim", "sect")),
        P(None, ("azim", "sect")),
        P(("azim", "sect")),
    )
    out_specs = (P(("azim", "sect"), None), P(("azim", "sect"), None))
    return jax.shard_map(
        per_device, mesh=mesh, in_specs=in_specs, out_specs=out_specs, check_vma=False
    )
```

```python
import functools

import jax
import jax.numpy as jnp
from jax import lax
from jax.experimental import pallas as pl
from jax.experimental.pallas import tpu as pltpu
from jax.sharding import PartitionSpec as P

NPU = 128
BLK = 128
TW = 128
CELL_DEV = 256
NODE_DEV = 1032
RIM = NPU + 1
HEAD = 136
NODE_ROWS = 1168
EXTRA = 16
F32 = jnp.float32
BF16 = jnp.bfloat16
VMEM = pltpu.VMEM
SMEM = pl.BlockSpec(memory_space=pltpu.SMEM)
WHOLE = pl.BlockSpec(memory_space=pltpu.VMEM)
PLACE = pl.BlockSpec(memory_space=pl.ANY)
COPY = pltpu.SemaphoreType.DMA


def call(kernel, name, out_shape, in_specs, out_specs, scratch_shapes=(), aliases=None, work=1_000_000):
    return pl.pallas_call(
        kernel,
        out_shape=out_shape,
        in_specs=in_specs,
        out_specs=out_specs,
        scratch_shapes=list(scratch_shapes),
        input_output_aliases=aliases or {},
        compiler_params=pltpu.CompilerParams(vmem_limit_bytes=24 * 1024 * 1024),
        cost_estimate=pl.CostEstimate(flops=work, bytes_accessed=4_000_000, transcendentals=0),
        name=name,
    )


def window_kernel(sections, paired, delay_ref, source_ref):
    groups, blocks, span, _ = source_ref.shape
    count = span // sections
    piece_rows = count if paired else 128
    padded = -(-blocks // 16) * 16
    delay = delay_ref[...].astype(F32)
    delay = jnp.concatenate([delay, jnp.zeros((padded - blocks, delay.shape[1]), F32)], 0).astype(BF16)
    spread = (padded, blocks * 128)
    spread = lax.broadcasted_iota(jnp.int32, spread, 1) // 128 == lax.broadcasted_iota(jnp.int32, spread, 0)
    spread = jnp.where(spread, 1.0, 0.0).astype(BF16)
    lanes = lax.broadcasted_iota(jnp.int32, (128, 128), 1)
    for piece in range(groups * span // 128):
        columns = lax.dot_general(
            delay[:, piece * 128 : (piece + 1) * 128], spread, (((0,), (0,)), ((), ())), preferred_element_type=F32
        )
        for block in range(blocks):
            source = columns[:, block * 128 : (block + 1) * 128].astype(jnp.int32) + lanes
            for part in range(128 // piece_rows):
                row = piece * 128 + part * piece_rows
                begin = row % span
                if paired:
                    apart = lax.axis_index("sect") ^ (begin // count)
                    begin = pl.multiple_of((apart // 2 + apart % 2 * (sections // 2)) * count, count)
                source_ref[row // span, block, pl.ds(begin, piece_rows), :] = source[
                    part * piece_rows : (part + 1) * piece_rows
                ]


def window_index(sections, groups, paired, delays):
    blocks, observers = delays.shape
    return call(
        functools.partial(window_kernel, sections, paired),
        "windows",
        jax.ShapeDtypeStruct((groups, blocks, observers // groups, 128), jnp.int32),
        [WHOLE],
        WHOLE,
        work=2_000_000_000,
    )(delays)


def column_kernel(sections, count_ref, geometry_ref, owner_ref, panel_ref, slot_ref, ids_ref):
    panels = geometry_ref.shape[1]
    spread = (32, 7 * 128)
    number = lax.broadcasted_iota(jnp.int32, spread, 0)
    spread = (lax.broadcasted_iota(jnp.int32, spread, 1) // 128 == number % 8) & (number < 24)
    spread = jnp.where(spread, 1.0, 0.0).astype(BF16)
    scale = jnp.where(lax.broadcasted_iota(jnp.int32, (8, BLK), 0) < 3, 0.25, 1.0)
    for block in range(panels // BLK):
        values = geometry_ref[:, block * BLK : (block + 1) * BLK]
        values = jnp.concatenate([values, values[:1]], 0) * scale
        high = values.astype(BF16).astype(F32)
        middle = (values - high).astype(BF16).astype(F32)
        parts = jnp.concatenate([high, middle, values - high - middle, jnp.zeros_like(values)], 0).astype(BF16)
        columns = lax.dot_general(parts, spread, (((0,), (0,)), ((), ())), preferred_element_type=F32)
        for part in range(7):
            panel_ref[block, part] = columns[:, part * 128 : (part + 1) * 128]

    cap = slot_ref.shape[0] // sections
    padded = ids_ref.shape[0]
    owner = owner_ref[...]
    dest = owner // CELL_DEV
    lane = lax.broadcasted_iota(jnp.int32, (padded, panels), 1)
    mine = dest == lax.broadcasted_iota(jnp.int32, (padded, panels), 0)
    ones = jnp.where(mine, 1.0, 0.0).astype(BF16)
    square = (128, 128)
    upto = lax.broadcasted_iota(jnp.int32, square, 0) <= lax.broadcasted_iota(jnp.int32, square, 1)
    upto = jnp.where(upto, 1.0, 0.0).astype(BF16)
    every = jnp.ones(square, BF16)
    carry = jnp.zeros((padded, 128), F32)
    counts = []
    for begin in range(0, panels, 128):
        piece = ones[:, begin : begin + 128]
        counts.append(carry + jnp.dot(piece, upto, preferred_element_type=F32))
        carry = carry + jnp.dot(piece, every, preferred_element_type=F32)
    count = jnp.concatenate(counts, 1).astype(jnp.int32)
    before = jnp.sum(jnp.where(mine, count - 1, 0), axis=0, keepdims=True)
    rank = before // 4
    slot = jnp.where(lane[:1] < count_ref[0], dest * cap + rank, -1)
    slot = jnp.broadcast_to(slot, (16, panels)).astype(jnp.int16)
    number = lax.broadcasted_iota(jnp.int16, (16, panels), 0)
    one, zero = jnp.array(1, BF16), jnp.array(0, BF16)
    for row in range(0, slot_ref.shape[0], 16):
        slot_ref[row : row + 16, :] = jnp.where(slot == number + jnp.int16(row), one, zero)

    at_lane = rank + lax.axis_index("sect") * cap % 128 == lax.broadcasted_iota(jnp.int32, (128, panels), 0)
    at_lane = jnp.where(at_lane, 1.0, 0.0).astype(BF16)
    cell = jnp.where(mine & (lane % 4 == 0), owner % CELL_DEV, 0).astype(F32).astype(BF16)
    ids_ref[...] = lax.dot_general(cell, at_lane, (((1,), (1,)), ((), ())), preferred_element_type=F32)


def panel_columns(sections, counts, geometry, owners):
    panels = geometry.shape[1]
    cap = 2 * CELL_DEV // sections
    padded = -(-sections // EXTRA) * EXTRA
    return call(
        functools.partial(column_kernel, sections),
        "columns",
        (
            jax.ShapeDtypeStruct((panels // BLK, 7, BLK, 128), F32),
            jax.ShapeDtypeStruct((sections * cap, panels), BF16),
            jax.ShapeDtypeStruct((padded, 128), F32),
        ),
        [SMEM, WHOLE, WHOLE],
        [WHOLE] * 3,
        work=2_000_000_000,
    )(counts, geometry, owners.reshape(1, panels))


def corner_kernel(count_ref, conn_ref, corner_ref):
    panels = conn_ref.shape[1]
    live = lax.broadcasted_iota(jnp.int32, (16, panels), 1) < count_ref[0]
    corners = [
        jnp.where(live, jnp.broadcast_to(conn_ref[i : i + 1, :], (16, panels)), -1).astype(jnp.int16) for i in range(4)
    ]
    number = lax.broadcasted_iota(jnp.int16, (16, panels), 0)
    share, zero = jnp.array(0.25, BF16), jnp.array(0, BF16)
    for row in range(0, NODE_ROWS, 16):
        node = number + jnp.int16(row)
        total = jnp.where(corners[0] == node, share, zero)
        for corner in corners[1:]:
            total = total + jnp.where(corner == node, share, zero)
        corner_ref[row : row + 16, :] = total


def corner_matrix(counts, connectivity):
    return call(
        corner_kernel,
        "corners",
        jax.ShapeDtypeStruct((NODE_ROWS, connectivity.shape[1]), BF16),
        [SMEM, WHOLE],
        WHOLE,
        work=2_000_000_000,
    )(counts, connectivity)


def first_join_kernel(*refs):
    *inputs, chunk_ref, wide_ref = refs
    parts = len(inputs) // 2
    count = inputs[0].shape[0]
    wide_ref[...] = jnp.zeros_like(wide_ref)
    total = jnp.zeros(wide_ref.shape, F32)
    for part in range(parts):
        chunk_ref[part * count : (part + 1) * count, :] = inputs[part][...]
        wide_ref[:3, :count] = inputs[parts + part][...].astype(F32)
        total = total + (pltpu.roll(wide_ref[...], part * count, 1) if part else wide_ref[...])
    chunk_ref[parts * count :, :] = total.astype(BF16)


def join_kernel(mine_ref, other_ref, chunk_ref):
    span = mine_ref.shape[0] - EXTRA
    chunk_ref[:span, :] = mine_ref[:span, :]
    chunk_ref[span : 2 * span, :] = other_ref[:span, :]
    moved = pltpu.roll(other_ref[span:, :].astype(F32), span, 1)
    chunk_ref[2 * span :, :] = (mine_ref[span:, :].astype(F32) + moved).astype(BF16)


def sources_kernel(places, first, last, count_ref, *refs):
    refs = list(refs)

    def take(number):
        taken = refs[:number]
        del refs[:number]
        return taken

    parts = len(places)
    chunks = take(parts)
    source_ref, panel_ref = take(2)
    if last:
        loading_in, thick_in, slot_ref, ids_ref, loading_ref, message_ref, thick_ref = take(7)
    else:
        loading_in, thick_in = (None, None) if first else take(2)
        loading_ref, thick_ref = take(2)
    low_ref, high_ref, mass_ref, pair_ref, window_ref = take(5)

    blocks = source_ref.shape[1]
    span = chunks[0].shape[0] - EXTRA
    observers = parts * span
    points = []
    for number, chunk in enumerate(chunks):
        low_ref[number * span : (number + 1) * span, :] = chunk[:span, :128].astype(F32)
        high_ref[number * span : (number + 1) * span, :] = chunk[:span, 128:].astype(F32)
        points.append(chunk[span : span + EXTRA, :].astype(F32) * 0.25)

    lanes = lax.broadcasted_iota(jnp.int32, (128, 128), 1)
    for block in range(blocks):
        for number, (offset, begin) in enumerate(places):
            group = lax.axis_index("azim") ^ offset
            for piece in range(span // 128):
                here = number * span + piece * 128
                source = source_ref[group, block, begin + piece * 128 : begin + (piece + 1) * 128, :]
                at = source & 127
                low = jnp.take_along_axis(low_ref[here : here + 128, :], at, axis=1, mode="promise_in_bounds")
                high = jnp.take_along_axis(high_ref[here : here + 128, :], at, axis=1, mode="promise_in_bounds")
                current = jnp.where(source < 128, low, high)
                following = pltpu.roll(jnp.where(lanes == 0, high, current).astype(BF16), 127, 1)
                current = current.astype(BF16)
                window_ref[block, here : here + 128, :] = current
                window_ref[block, observers + here : observers + here + 128, :] = following - current

                at_x, at_y, at_z = (points[number][i : i + 1, piece * 128 : piece * 128 + 128] for i in range(3))
                for strip in range(BLK // 16):
                    rows = slice(strip * 16, strip * 16 + 16)
                    delta_x = at_x - panel_ref[block, 0, rows, :]
                    delta_y = at_y - panel_ref[block, 1, rows, :]
                    delta_z = at_z - panel_ref[block, 2, rows, :]
                    inverse = lax.rsqrt(delta_x * delta_x + delta_y * delta_y + delta_z * delta_z)
                    flux = (
                        panel_ref[block, 3, rows, :] * delta_x
                        + panel_ref[block, 4, rows, :] * delta_y
                        + panel_ref[block, 5, rows, :] * delta_z
                    )
                    far = flux * inverse * inverse
                    pair_ref[block, rows, here : here + 128] = (far * inverse).astype(BF16)
                    pair_ref[block, rows, observers + here : observers + here + 128] = far.astype(BF16)
                    mass_ref[block, rows, here : here + 128] = (panel_ref[block, 6, rows, :] * inverse).astype(BF16)
        rows = slice(block * BLK, (block + 1) * BLK)
        thick = jnp.dot(mass_ref[block], window_ref[block, observers:, :], preferred_element_type=F32)
        loading = jnp.dot(pair_ref[block], window_ref[block], preferred_element_type=F32)
        if not first:
            thick = thick + thick_in[rows, :]
            loading = loading + loading_in[rows, :]
        if last:
            alive = block * BLK + lax.broadcasted_iota(jnp.int32, (BLK, TW), 0) < count_ref[0]
            thick = jnp.where(alive, thick, 0.0).astype(BF16)
            loading = jnp.where(alive, loading, 0.0).astype(BF16)
        thick_ref[rows, :] = thick
        loading_ref[rows, :] = loading

    if last:
        sections = message_ref.shape[0]
        cap = slot_ref.shape[0] // sections
        slots = jnp.dot(slot_ref[...], thick_ref[...], preferred_element_type=F32).astype(BF16)
        for section in range(sections):
            message_ref[section, :cap, :] = slots[section * cap : (section + 1) * cap]
            ids = jnp.broadcast_to(ids_ref[section : section + 1, :], (EXTRA, 128))
            message_ref[section, cap:, :] = ids.astype(BF16)


def sources(places, counts, chunks, source, panel_values, sums=(), slots=None, sections=None):
    blocks = source.shape[1]
    panels = panel_values.shape[0] * BLK
    observers = len(places) * (chunks[0].shape[0] - EXTRA)
    last = slots is not None
    operands = [counts, *chunks, source, panel_values, *sums]
    scratch = [
        VMEM((observers, 128), F32),
        VMEM((observers, 128), F32),
        VMEM((blocks, BLK, observers), BF16),
        VMEM((blocks, BLK, 2 * observers), BF16),
        VMEM((blocks, 2 * observers, TW), BF16),
    ]
    aliases = {}
    if last:
        operands += slots
        cap = 2 * CELL_DEV // sections
        out_shape = [
            jax.ShapeDtypeStruct((panels, TW), BF16),
            jax.ShapeDtypeStruct((sections, cap + EXTRA, TW), BF16),
        ]
        scratch = [VMEM((panels, TW), BF16)] + scratch
    else:
        out_shape = [jax.ShapeDtypeStruct((panels, TW), F32)] * 2
        if sums:
            aliases = {len(operands) - 2: 0, len(operands) - 1: 1}
    return call(
        functools.partial(sources_kernel, places, not sums, last),
        "sources",
        out_shape,
        [SMEM] + [WHOLE] * (len(operands) - 1),
        [WHOLE] * len(out_shape),
        scratch,
        aliases,
        work=3_000_000_000,
    )(*operands)


def rim_kernel(corner_ref, loading_ref, rim_ref):
    rim = jnp.dot(corner_ref[NODE_DEV - 8 :, :], loading_ref[...], preferred_element_type=F32)
    rim_ref[...] = rim[8:].astype(BF16)


def rim_sums(corners, loading):
    return call(
        rim_kernel, "rim", jax.ShapeDtypeStruct((HEAD, TW), BF16), [WHOLE] * 2, WHOLE, work=1_000_000_000
    )(corners, loading)


def node_kernel(corner_ref, loading_ref, node_ref, head_ref):
    nodes = jnp.dot(corner_ref[: NODE_DEV + 8, :], loading_ref[...], preferred_element_type=F32)
    head_ref[...] = nodes[:HEAD]
    node_ref[...] = nodes[:NODE_DEV]


def node_sums(corners, loading):
    return call(
        node_kernel,
        "nodes",
        (jax.ShapeDtypeStruct((NODE_DEV, TW), F32), jax.ShapeDtypeStruct((HEAD, TW), F32)),
        [WHOLE] * 2,
        [WHOLE] * 2,
        work=2_000_000_000,
    )(corners, loading)


def finish_kernel(message_ref, rim_ref, head_ref, _, node_ref, cell_ref, rows_ref, top_ref, total_ref, sems):
    sections = message_ref.shape[0]
    cap = message_ref.shape[1] - EXTRA
    per = 128 // cap
    top_ref[...] = head_ref[...] + rim_ref[...].astype(F32)
    top_copy = pltpu.make_async_copy(top_ref, node_ref.at[pl.ds(0, HEAD), :], sems.at[0])
    top_copy.start()
    total = jnp.zeros((CELL_DEV, TW), F32)
    cell = lax.broadcasted_iota(jnp.int32, (CELL_DEV, 128), 0).astype(F32)
    for group in range(sections // per):
        ids = jnp.zeros((EXTRA, 128), F32)
        for inner in range(per):
            section = group * per + inner
            ids = ids + message_ref[section, cap:, :].astype(F32)
            rows_ref[section * cap : (section + 1) * cap, :] = message_ref[section, :cap, :]
        match = jnp.where(ids[:1] == cell, 1.0, 0.0).astype(BF16)
        total = total + jnp.dot(match, rows_ref[group * 128 : (group + 1) * 128, :], preferred_element_type=F32)
    total_ref[...] = total
    cell_copy = pltpu.make_async_copy(total_ref, cell_ref, sems.at[1])
    cell_copy.start()
    top_copy.wait()
    cell_copy.wait()


def finish(message, rim, head, nodes):
    sections = message.shape[0]
    cap = message.shape[1] - EXTRA
    return call(
        finish_kernel,
        "finish",
        (
            jax.ShapeDtypeStruct((NODE_DEV, TW), F32),
            jax.ShapeDtypeStruct((CELL_DEV, TW), F32),
        ),
        [WHOLE] * 3 + [PLACE],
        [PLACE] * 2,
        [VMEM((sections * cap, TW), BF16), VMEM((HEAD, TW), F32), VMEM((CELL_DEV, TW), F32), COPY((2,))],
        {3: 0},
    )(message, rim, head, nodes)


def swapped(array, axis, bit):
    peers = lax.axis_size(axis)
    return lax.ppermute(array, axis, [(i, i ^ bit) for i in range(peers)])


def joined(mine, other):
    span = mine.shape[0] - EXTRA
    shape = jax.ShapeDtypeStruct((2 * span + EXTRA, mine.shape[1]), BF16)
    return call(join_kernel, "join", shape, [WHOLE] * 2, WHOLE)(mine, other)


def half_chunk(signals, xyz, sections):
    count, width = signals.shape
    turned = xyz.T
    pieces, points = [signals], [turned]
    for apart in range(2, sections, 2):
        pieces.append(swapped(signals, "sect", apart))
        points.append(swapped(turned, "sect", apart))
    shape = jax.ShapeDtypeStruct((len(pieces) * count + EXTRA, width), BF16)
    return call(
        first_join_kernel, "first", shape, [WHOLE] * (2 * len(pieces)), WHOLE, [VMEM((EXTRA, width), F32)]
    )(*pieces, *points)


def after(array, other):
    return lax.optimization_barrier((array, other))[0]


def spread_chunk(signals, xyz, sections):
    count, width = signals.shape
    extra = jnp.zeros((EXTRA, width), BF16)
    extra = lax.dynamic_update_slice(extra, xyz.T, (0, lax.axis_index("sect") * count))
    payload = jnp.concatenate([signals, extra], 0)
    everyone = jnp.broadcast_to(payload[None], (sections,) + payload.shape)
    received = lax.all_to_all(everyone, "sect", split_axis=0, concat_axis=0, tiled=True)
    return jnp.concatenate(
        [received[:, :count].reshape(sections * count, -1), received[:, count:].astype(F32).sum(0).astype(BF16)], 0
    )


def per_device(signals, observer_xyz, panel_geometry, delays, counts, connectivity, owners):
    sections = lax.axis_size("sect")
    groups = lax.axis_size("azim")
    count = signals.shape[0]
    paired = count % 16 == 0 and sections % 2 == 0 and sections // 2 * count == 128

    source = window_index(sections, groups, paired, delays)
    panel_values, slots, ids = panel_columns(sections, counts, panel_geometry, owners)

    def add(sums, places, chunks, *rest):
        return sources(places, counts, chunks, source, panel_values, sums, *rest)

    if paired:
        half = half_chunk(signals, observer_xyz, sections)
        other = swapped(half, "sect", 1)
        corners = corner_matrix(counts, after(connectivity, half))
        sums = add((), [(0, 0)], [half])
        chunk = joined(half, other)
    else:
        chunk = spread_chunk(signals, observer_xyz, sections)
        corners = corner_matrix(counts, connectivity)
    near = swapped(chunk, "azim", 1)
    chunks = {0: chunk}
    bit = groups // 2
    while bit > 1:
        for offset in list(chunks):
            chunks[offset ^ bit] = swapped(chunks[offset], "azim", bit)
        bit //= 2
    if paired:
        sums = add(sums, [(0, 128)], [other])
    else:
        sums = add((), [(0, 0)], [chunk])
    sums = add(sums, [(1, 0)], [near])
    rest = [offset for offset in chunks if offset]
    for offset in rest:
        chunks[offset] = after(chunks[offset], sums[0])
        chunks[offset ^ 1] = swapped(chunks[offset], "azim", 1)
    sums = add(sums, [(o, 0) for o in rest], [chunks[o] for o in rest])
    rest = [offset ^ 1 for offset in rest]
    loading, message = add(sums, [(o, 0) for o in rest], [chunks[o] for o in rest], [slots, ids], sections)
    message = lax.all_to_all(message, "sect", split_axis=0, concat_axis=0, tiled=True)
    rim = rim_sums(corners, loading)
    rim = lax.ppermute(rim, "sect", [(i, (i + 1) % sections) for i in range(sections)])
    nodes, head = node_sums(corners, loading)
    return finish(message, rim, head, nodes)


def solution(mesh):
    in_specs = (
        P(("azim", "sect"), None),
        P(("azim", "sect"), None),
        P(None, ("azim", "sect")),
        P(("azim", "sect"), None),
        P(("azim", "sect")),
        P(None, ("azim", "sect")),
        P(("azim", "sect")),
    )
    out_specs = (P(("azim", "sect"), None), P(("azim", "sect"), None))
    return jax.shard_map(
        per_device, mesh=mesh, in_specs=in_specs, out_specs=out_specs, check_vma=False
    )
```

```python
import functools

import jax
import jax.numpy as jnp
from jax import lax
from jax.experimental import pallas as pl
from jax.experimental.pallas import tpu as pltpu
from jax.sharding import PartitionSpec as P

NPU = 128
BLK = 128
TW = 128
CELL_DEV = 256
NODE_DEV = 1032
RIM = NPU + 1
HEAD = 136
NODE_ROWS = 1168
EXTRA = 16
FIXED = 32000.0
F32 = jnp.float32
BF16 = jnp.bfloat16
VMEM = pltpu.VMEM
SMEM = pl.BlockSpec(memory_space=pltpu.SMEM)
WHOLE = pl.BlockSpec(memory_space=pltpu.VMEM)
PLACE = pl.BlockSpec(memory_space=pl.ANY)
COPY = pltpu.SemaphoreType.DMA


def call(kernel, name, out_shape, in_specs, out_specs, scratch_shapes=(), aliases=None, work=1_000_000):
    return pl.pallas_call(
        kernel,
        out_shape=out_shape,
        in_specs=in_specs,
        out_specs=out_specs,
        scratch_shapes=list(scratch_shapes),
        input_output_aliases=aliases or {},
        compiler_params=pltpu.CompilerParams(vmem_limit_bytes=24 * 1024 * 1024),
        cost_estimate=pl.CostEstimate(flops=work, bytes_accessed=4_000_000, transcendentals=0),
        name=name,
    )


def window_kernel(sections, paired, delay_ref, source_ref):
    groups, blocks, span, _ = source_ref.shape
    count = span // sections
    piece_rows = count if paired else 128
    padded = -(-blocks // 16) * 16
    delay = delay_ref[...].astype(F32)
    delay = jnp.concatenate([delay, jnp.zeros((padded - blocks, delay.shape[1]), F32)], 0).astype(BF16)
    spread = (padded, blocks * 128)
    spread = lax.broadcasted_iota(jnp.int32, spread, 1) // 128 == lax.broadcasted_iota(jnp.int32, spread, 0)
    spread = jnp.where(spread, 1.0, 0.0).astype(BF16)
    lanes = lax.broadcasted_iota(jnp.int32, (128, 128), 1)
    for piece in range(groups * span // 128):
        columns = lax.dot_general(
            delay[:, piece * 128 : (piece + 1) * 128], spread, (((0,), (0,)), ((), ())), preferred_element_type=F32
        )
        for block in range(blocks):
            source = columns[:, block * 128 : (block + 1) * 128].astype(jnp.int32) + lanes
            for part in range(128 // piece_rows):
                row = piece * 128 + part * piece_rows
                begin = row % span
                if paired:
                    apart = lax.axis_index("sect") ^ (begin // count)
                    begin = pl.multiple_of((apart // 2 + apart % 2 * (sections // 2)) * count, count)
                source_ref[row // span, block, pl.ds(begin, piece_rows), :] = source[
                    part * piece_rows : (part + 1) * piece_rows
                ]


def window_index(sections, groups, paired, delays):
    blocks, observers = delays.shape
    return call(
        functools.partial(window_kernel, sections, paired),
        "windows",
        jax.ShapeDtypeStruct((groups, blocks, observers // groups, 128), jnp.int32),
        [WHOLE],
        WHOLE,
        work=2_000_000_000,
    )(delays)


def column_kernel(sections, count_ref, geometry_ref, owner_ref, panel_ref, slot_ref, ids_ref):
    panels = geometry_ref.shape[1]
    spread = (32, 7 * 128)
    number = lax.broadcasted_iota(jnp.int32, spread, 0)
    spread = (lax.broadcasted_iota(jnp.int32, spread, 1) // 128 == number % 8) & (number < 24)
    spread = jnp.where(spread, 1.0, 0.0).astype(BF16)
    scale = jnp.where(lax.broadcasted_iota(jnp.int32, (8, BLK), 0) < 3, 0.25, 1.0)
    for block in range(panels // BLK):
        values = geometry_ref[:, block * BLK : (block + 1) * BLK]
        values = jnp.concatenate([values, values[:1]], 0) * scale
        high = values.astype(BF16).astype(F32)
        middle = (values - high).astype(BF16).astype(F32)
        parts = jnp.concatenate([high, middle, values - high - middle, jnp.zeros_like(values)], 0).astype(BF16)
        columns = lax.dot_general(parts, spread, (((0,), (0,)), ((), ())), preferred_element_type=F32)
        for part in range(7):
            panel_ref[block, part] = columns[:, part * 128 : (part + 1) * 128]

    cap = slot_ref.shape[0] // sections
    padded = ids_ref.shape[0]
    owner = owner_ref[...]
    dest = owner // CELL_DEV
    lane = lax.broadcasted_iota(jnp.int32, (padded, panels), 1)
    mine = dest == lax.broadcasted_iota(jnp.int32, (padded, panels), 0)
    ones = jnp.where(mine, 1.0, 0.0).astype(BF16)
    square = (128, 128)
    upto = lax.broadcasted_iota(jnp.int32, square, 0) <= lax.broadcasted_iota(jnp.int32, square, 1)
    upto = jnp.where(upto, 1.0, 0.0).astype(BF16)
    every = jnp.ones(square, BF16)
    carry = jnp.zeros((padded, 128), F32)
    counts = []
    for begin in range(0, panels, 128):
        piece = ones[:, begin : begin + 128]
        counts.append(carry + jnp.dot(piece, upto, preferred_element_type=F32))
        carry = carry + jnp.dot(piece, every, preferred_element_type=F32)
    count = jnp.concatenate(counts, 1).astype(jnp.int32)
    before = jnp.sum(jnp.where(mine, count - 1, 0), axis=0, keepdims=True)
    rank = before // 4
    slot = jnp.where(lane[:1] < count_ref[0], dest * cap + rank, -1)
    slot = jnp.broadcast_to(slot, (16, panels)).astype(jnp.int16)
    number = lax.broadcasted_iota(jnp.int16, (16, panels), 0)
    one, zero = jnp.array(1, BF16), jnp.array(0, BF16)
    for row in range(0, slot_ref.shape[0], 16):
        slot_ref[row : row + 16, :] = jnp.where(slot == number + jnp.int16(row), one, zero)

    at_lane = rank + lax.axis_index("sect") * cap % 128 == lax.broadcasted_iota(jnp.int32, (128, panels), 0)
    at_lane = jnp.where(at_lane, 1.0, 0.0).astype(BF16)
    cell = jnp.where(mine & (lane % 4 == 0), owner % CELL_DEV, 0).astype(F32).astype(BF16)
    ids_ref[...] = lax.dot_general(cell, at_lane, (((1,), (1,)), ((), ())), preferred_element_type=F32)


def panel_columns(sections, counts, geometry, owners):
    panels = geometry.shape[1]
    cap = 2 * CELL_DEV // sections
    padded = -(-sections // EXTRA) * EXTRA
    return call(
        functools.partial(column_kernel, sections),
        "columns",
        (
            jax.ShapeDtypeStruct((panels // BLK, 7, BLK, 128), F32),
            jax.ShapeDtypeStruct((sections * cap, panels), BF16),
            jax.ShapeDtypeStruct((padded, 128), F32),
        ),
        [SMEM, WHOLE, WHOLE],
        [WHOLE] * 3,
        work=2_000_000_000,
    )(counts, geometry, owners.reshape(1, panels))


def corner_kernel(count_ref, conn_ref, corner_ref):
    panels = conn_ref.shape[1]
    live = lax.broadcasted_iota(jnp.int32, (16, panels), 1) < count_ref[0]
    corners = [
        jnp.where(live, jnp.broadcast_to(conn_ref[i : i + 1, :], (16, panels)), -1).astype(jnp.int16) for i in range(4)
    ]
    number = lax.broadcasted_iota(jnp.int16, (16, panels), 0)
    share, zero = jnp.array(0.25, BF16), jnp.array(0, BF16)
    for row in range(0, NODE_ROWS, 16):
        node = number + jnp.int16(row)
        total = jnp.where(corners[0] == node, share, zero)
        for corner in corners[1:]:
            total = total + jnp.where(corner == node, share, zero)
        corner_ref[row : row + 16, :] = total


def corner_matrix(counts, connectivity):
    return call(
        corner_kernel,
        "corners",
        jax.ShapeDtypeStruct((NODE_ROWS, connectivity.shape[1]), BF16),
        [SMEM, WHOLE],
        WHOLE,
        work=2_000_000_000,
    )(counts, connectivity)


def first_join_kernel(*refs):
    *inputs, chunk_ref, wide_ref = refs
    parts = len(inputs) // 2
    count = inputs[0].shape[0]
    wide_ref[...] = jnp.zeros_like(wide_ref)
    total = jnp.zeros(wide_ref.shape, F32)
    for part in range(parts):
        chunk_ref[part * count : (part + 1) * count, :] = inputs[part][...]
        wide_ref[:3, :count] = inputs[parts + part][...].astype(F32)
        total = total + (pltpu.roll(wide_ref[...], part * count, 1) if part else wide_ref[...])
    chunk_ref[parts * count :, :] = total.astype(BF16)


def join_kernel(mine_ref, other_ref, chunk_ref):
    span = mine_ref.shape[0] - EXTRA
    chunk_ref[:span, :] = mine_ref[:span, :]
    chunk_ref[span : 2 * span, :] = other_ref[:span, :]
    moved = pltpu.roll(other_ref[span:, :].astype(F32), span, 1)
    chunk_ref[2 * span :, :] = (mine_ref[span:, :].astype(F32) + moved).astype(BF16)


def sources_kernel(places, first, last, count_ref, *refs):
    refs = list(refs)

    def take(number):
        taken = refs[:number]
        del refs[:number]
        return taken

    parts = len(places)
    chunks = take(parts)
    source_ref, panel_ref = take(2)
    if last:
        loading_in, thick_in, slot_ref, ids_ref, corner_ref = take(5)
        loading_ref, message_ref, rim_ref, thick_ref = take(4)
    else:
        loading_in, thick_in = (None, None) if first else take(2)
        loading_ref, thick_ref = take(2)
    code_ref, scale_ref, mass_ref, pair_ref, window_ref = take(5)

    blocks = source_ref.shape[1]
    span = chunks[0].shape[0] - EXTRA
    observers = parts * span
    points = []
    for number, chunk in enumerate(chunks):
        low = chunk[:span, :128].astype(F32)
        high = chunk[:span, 128:].astype(F32)
        most = jnp.max(jnp.maximum(jnp.abs(low), jnp.abs(high)), axis=1, keepdims=True)
        most = jnp.maximum(jnp.broadcast_to(most, (span, 128)), 1e-30)
        low = jnp.floor(low * (FIXED / most) + 0.5).astype(jnp.int32)
        high = jnp.floor(high * (FIXED / most) + 0.5).astype(jnp.int32)
        code_ref[number * span : (number + 1) * span, :] = (high << 16) | (low & 0xFFFF)
        scale_ref[number * span : (number + 1) * span, :] = most * (1 / (FIXED * 65536))
        points.append(chunk[span : span + EXTRA, :].astype(F32) * 0.25)

    lanes = lax.broadcasted_iota(jnp.int32, (128, 128), 1)
    for block in range(blocks):
        for number, (offset, begin) in enumerate(places):
            group = lax.axis_index("azim") ^ offset
            for piece in range(span // 128):
                here = number * span + piece * 128
                source = source_ref[group, block, begin + piece * 128 : begin + (piece + 1) * 128, :]
                at = source & 127
                code = jnp.take_along_axis(code_ref[here : here + 128, :], at, axis=1, mode="promise_in_bounds")
                scale = scale_ref[here : here + 128, :]
                current = jnp.where(source < 128, code << 16, code)
                following = (jnp.where(lanes == 0, code, current).astype(F32) * scale).astype(BF16)
                following = pltpu.roll(following, 127, 1)
                current = (current.astype(F32) * scale).astype(BF16)
                window_ref[block, here : here + 128, :] = current
                window_ref[block, observers + here : observers + here + 128, :] = following - current

                at_x, at_y, at_z = (points[number][i : i + 1, piece * 128 : piece * 128 + 128] for i in range(3))
                for strip in range(BLK // 16):
                    rows = slice(strip * 16, strip * 16 + 16)
                    delta_x = at_x - panel_ref[block, 0, rows, :]
                    delta_y = at_y - panel_ref[block, 1, rows, :]
                    delta_z = at_z - panel_ref[block, 2, rows, :]
                    inverse = lax.rsqrt(delta_x * delta_x + delta_y * delta_y + delta_z * delta_z)
                    flux = (
                        panel_ref[block, 3, rows, :] * delta_x
                        + panel_ref[block, 4, rows, :] * delta_y
                        + panel_ref[block, 5, rows, :] * delta_z
                    )
                    far = flux * inverse * inverse
                    pair_ref[block, rows, here : here + 128] = (far * inverse).astype(BF16)
                    pair_ref[block, rows, observers + here : observers + here + 128] = far.astype(BF16)
                    mass_ref[block, rows, here : here + 128] = (panel_ref[block, 6, rows, :] * inverse).astype(BF16)
        rows = slice(block * BLK, (block + 1) * BLK)
        thick = jnp.dot(mass_ref[block], window_ref[block, observers:, :], preferred_element_type=F32)
        loading = jnp.dot(pair_ref[block], window_ref[block], preferred_element_type=F32)
        if not first:
            thick = thick + thick_in[rows, :]
            loading = loading + loading_in[rows, :]
        if last:
            alive = block * BLK + lax.broadcasted_iota(jnp.int32, (BLK, TW), 0) < count_ref[0]
            thick = jnp.where(alive, thick, 0.0).astype(BF16)
            loading = jnp.where(alive, loading, 0.0).astype(BF16)
        thick_ref[rows, :] = thick
        loading_ref[rows, :] = loading

    if last:
        sections = message_ref.shape[0]
        cap = slot_ref.shape[0] // sections
        slots = jnp.dot(slot_ref[...], thick_ref[...], preferred_element_type=F32).astype(BF16)
        for section in range(sections):
            message_ref[section, :cap, :] = slots[section * cap : (section + 1) * cap]
            ids = jnp.broadcast_to(ids_ref[section : section + 1, :], (EXTRA, 128))
            message_ref[section, cap:, :] = ids.astype(BF16)
        rim = jnp.dot(corner_ref[NODE_DEV - 8 :, :], loading_ref[...], preferred_element_type=F32)
        rim_ref[...] = rim[8:].astype(BF16)


def sources(places, counts, chunks, source, panel_values, sums=(), slots=None, sections=None):
    blocks = source.shape[1]
    panels = panel_values.shape[0] * BLK
    observers = len(places) * (chunks[0].shape[0] - EXTRA)
    last = slots is not None
    operands = [counts, *chunks, source, panel_values, *sums]
    scratch = [
        VMEM((observers, 128), jnp.int32),
        VMEM((observers, 128), F32),
        VMEM((blocks, BLK, observers), BF16),
        VMEM((blocks, BLK, 2 * observers), BF16),
        VMEM((blocks, 2 * observers, TW), BF16),
    ]
    aliases = {}
    if last:
        operands += slots
        cap = 2 * CELL_DEV // sections
        out_shape = [
            jax.ShapeDtypeStruct((panels, TW), BF16),
            jax.ShapeDtypeStruct((sections, cap + EXTRA, TW), BF16),
            jax.ShapeDtypeStruct((HEAD, TW), BF16),
        ]
        scratch = [VMEM((panels, TW), BF16)] + scratch
    else:
        out_shape = [jax.ShapeDtypeStruct((panels, TW), F32)] * 2
        if sums:
            aliases = {len(operands) - 2: 0, len(operands) - 1: 1}
    return call(
        functools.partial(sources_kernel, places, not sums, last),
        "sources",
        out_shape,
        [SMEM] + [WHOLE] * (len(operands) - 1),
        [WHOLE] * len(out_shape),
        scratch,
        aliases,
        work=3_000_000_000,
    )(*operands)


def node_kernel(corner_ref, loading_ref, node_ref, head_ref):
    nodes = jnp.dot(corner_ref[: NODE_DEV + 8, :], loading_ref[...], preferred_element_type=F32)
    head_ref[...] = nodes[:HEAD]
    node_ref[...] = nodes[:NODE_DEV]


def node_sums(corners, loading):
    return call(
        node_kernel,
        "nodes",
        (jax.ShapeDtypeStruct((NODE_DEV, TW), F32), jax.ShapeDtypeStruct((HEAD, TW), F32)),
        [WHOLE] * 2,
        [WHOLE] * 2,
        work=2_000_000_000,
    )(corners, loading)


def finish_kernel(message_ref, rim_ref, head_ref, _, node_ref, cell_ref, rows_ref, top_ref, total_ref, sems):
    sections = message_ref.shape[0]
    cap = message_ref.shape[1] - EXTRA
    per = 128 // cap
    top_ref[...] = head_ref[...] + rim_ref[...].astype(F32)
    top_copy = pltpu.make_async_copy(top_ref, node_ref.at[pl.ds(0, HEAD), :], sems.at[0])
    top_copy.start()
    total = jnp.zeros((CELL_DEV, TW), F32)
    cell = lax.broadcasted_iota(jnp.int32, (CELL_DEV, 128), 0).astype(F32)
    for group in range(sections // per):
        ids = jnp.zeros((EXTRA, 128), F32)
        for inner in range(per):
            section = group * per + inner
            ids = ids + message_ref[section, cap:, :].astype(F32)
            rows_ref[section * cap : (section + 1) * cap, :] = message_ref[section, :cap, :]
        match = jnp.where(ids[:1] == cell, 1.0, 0.0).astype(BF16)
        total = total + jnp.dot(match, rows_ref[group * 128 : (group + 1) * 128, :], preferred_element_type=F32)
    total_ref[...] = total
    cell_copy = pltpu.make_async_copy(total_ref, cell_ref, sems.at[1])
    cell_copy.start()
    top_copy.wait()
    cell_copy.wait()


def finish(message, rim, head, nodes):
    sections = message.shape[0]
    cap = message.shape[1] - EXTRA
    return call(
        finish_kernel,
        "finish",
        (
            jax.ShapeDtypeStruct((NODE_DEV, TW), F32),
            jax.ShapeDtypeStruct((CELL_DEV, TW), F32),
        ),
        [WHOLE] * 3 + [PLACE],
        [PLACE] * 2,
        [VMEM((sections * cap, TW), BF16), VMEM((HEAD, TW), F32), VMEM((CELL_DEV, TW), F32), COPY((2,))],
        {3: 0},
    )(message, rim, head, nodes)


def swapped(array, axis, bit):
    peers = lax.axis_size(axis)
    return lax.ppermute(array, axis, [(i, i ^ bit) for i in range(peers)])


def joined(mine, other):
    span = mine.shape[0] - EXTRA
    shape = jax.ShapeDtypeStruct((2 * span + EXTRA, mine.shape[1]), BF16)
    return call(join_kernel, "join", shape, [WHOLE] * 2, WHOLE)(mine, other)


def half_chunk(signals, xyz, sections):
    count, width = signals.shape
    turned = xyz.T
    shape = jax.ShapeDtypeStruct((2 * count + EXTRA, width), BF16)
    chunk = call(first_join_kernel, "first", shape, [WHOLE] * 4, WHOLE, [VMEM((EXTRA, width), F32)])(
        signals, swapped(signals, "sect", 2), turned, swapped(turned, "sect", 2)
    )
    bit = 4
    while bit < sections:
        chunk = joined(chunk, swapped(chunk, "sect", bit))
        bit *= 2
    return chunk


def after(array, other):
    return lax.optimization_barrier((array, other))[0]


def spread_chunk(signals, xyz, sections):
    count, width = signals.shape
    extra = jnp.zeros((EXTRA, width), BF16)
    extra = lax.dynamic_update_slice(extra, xyz.T, (0, lax.axis_index("sect") * count))
    payload = jnp.concatenate([signals, extra], 0)
    everyone = jnp.broadcast_to(payload[None], (sections,) + payload.shape)
    received = lax.all_to_all(everyone, "sect", split_axis=0, concat_axis=0, tiled=True)
    return jnp.concatenate(
        [received[:, :count].reshape(sections * count, -1), received[:, count:].astype(F32).sum(0).astype(BF16)], 0
    )


def per_device(signals, observer_xyz, panel_geometry, delays, counts, connectivity, owners):
    sections = lax.axis_size("sect")
    groups = lax.axis_size("azim")
    count = signals.shape[0]
    paired = count % 16 == 0 and sections % 2 == 0 and sections // 2 * count == 128

    source = window_index(sections, groups, paired, delays)
    panel_values, slots, ids = panel_columns(sections, counts, after(panel_geometry, source), owners)

    def add(sums, places, chunks, *rest):
        return sources(places, counts, chunks, source, panel_values, sums, *rest)

    if paired:
        half = half_chunk(signals, observer_xyz, sections)
        other = swapped(half, "sect", 1)
        corners = corner_matrix(counts, after(connectivity, half))
        sums = add((), [(0, 0)], [half])
        sums = after(sums, corners)
        chunk = joined(half, other)
    else:
        chunk = spread_chunk(signals, observer_xyz, sections)
        corners = corner_matrix(counts, connectivity)
    near = swapped(chunk, "azim", 1)
    chunks = {0: chunk}
    bit = groups // 2
    while bit > 1:
        for offset in list(chunks):
            chunks[offset ^ bit] = swapped(chunks[offset], "azim", bit)
        bit //= 2
    if paired:
        sums = add(sums, [(0, 128)], [other])
    else:
        sums = add((), [(0, 0)], [chunk])
    sums = add(sums, [(1, 0)], [near])
    rest = [offset for offset in chunks if offset]
    for offset in rest:
        chunks[offset] = after(chunks[offset], sums[0])
        chunks[offset ^ 1] = swapped(chunks[offset], "azim", 1)
    sums = add(sums, [(o, 0) for o in rest], [chunks[o] for o in rest])
    rest = [offset ^ 1 for offset in rest]
    matrices = [slots, ids, corners]
    loading, message, rim = add(sums, [(o, 0) for o in rest], [chunks[o] for o in rest], matrices, sections)
    message = lax.all_to_all(message, "sect", split_axis=0, concat_axis=0, tiled=True)
    rim = lax.ppermute(rim, "sect", [(i, (i + 1) % sections) for i in range(sections)])
    nodes, head = node_sums(corners, loading)
    return finish(message, rim, head, nodes)


def solution(mesh):
    in_specs = (
        P(("azim", "sect"), None),
        P(("azim", "sect"), None),
        P(None, ("azim", "sect")),
        P(("azim", "sect"), None),
        P(("azim", "sect")),
        P(None, ("azim", "sect")),
        P(("azim", "sect")),
    )
    out_specs = (P(("azim", "sect"), None), P(("azim", "sect"), None))
    return jax.shard_map(
        per_device, mesh=mesh, in_specs=in_specs, out_specs=out_specs, check_vma=False
    )
```

```python
import functools

import jax
import jax.numpy as jnp
from jax import lax
from jax.experimental import pallas as pl
from jax.experimental.pallas import tpu as pltpu
from jax.sharding import PartitionSpec as P

NPU = 128
BLK = 128
TW = 128
CELL_DEV = 256
NODE_DEV = 1032
RIM = NPU + 1
HEAD = 136
NODE_ROWS = 1168
EXTRA = 16
FIXED = 32000.0
F32 = jnp.float32
BF16 = jnp.bfloat16
VMEM = pltpu.VMEM
SMEM = pl.BlockSpec(memory_space=pltpu.SMEM)
WHOLE = pl.BlockSpec(memory_space=pltpu.VMEM)
PLACE = pl.BlockSpec(memory_space=pl.ANY)
COPY = pltpu.SemaphoreType.DMA


def call(kernel, name, out_shape, in_specs, out_specs, scratch_shapes=(), aliases=None, work=1_000_000):
    return pl.pallas_call(
        kernel,
        out_shape=out_shape,
        in_specs=in_specs,
        out_specs=out_specs,
        scratch_shapes=list(scratch_shapes),
        input_output_aliases=aliases or {},
        compiler_params=pltpu.CompilerParams(vmem_limit_bytes=24 * 1024 * 1024),
        cost_estimate=pl.CostEstimate(flops=work, bytes_accessed=4_000_000, transcendentals=0),
        name=name,
    )


def window_kernel(delay_ref, source_ref):
    groups, blocks, span, _ = source_ref.shape
    padded = -(-blocks // 16) * 16
    delay = delay_ref[...].astype(F32)
    delay = jnp.concatenate([delay, jnp.zeros((padded - blocks, delay.shape[1]), F32)], 0).astype(BF16)
    spread = (padded, blocks * 128)
    spread = lax.broadcasted_iota(jnp.int32, spread, 1) // 128 == lax.broadcasted_iota(jnp.int32, spread, 0)
    spread = jnp.where(spread, 1.0, 0.0).astype(BF16)
    lanes = lax.broadcasted_iota(jnp.int32, (128, 128), 1)
    for piece in range(groups * span // 128):
        columns = lax.dot_general(
            delay[:, piece * 128 : (piece + 1) * 128], spread, (((0,), (0,)), ((), ())), preferred_element_type=F32
        )
        for block in range(blocks):
            source = columns[:, block * 128 : (block + 1) * 128].astype(jnp.int32) + lanes
            begin = piece * 128 % span
            source_ref[piece * 128 // span, block, begin : begin + 128, :] = source


def window_index(groups, delays):
    blocks, observers = delays.shape
    return call(
        window_kernel,
        "windows",
        jax.ShapeDtypeStruct((groups, blocks, observers // groups, 128), jnp.int32),
        [WHOLE],
        WHOLE,
        work=2_000_000_000,
    )(delays)


def column_kernel(sections, count_ref, geometry_ref, owner_ref, panel_ref, slot_ref, ids_ref):
    panels = geometry_ref.shape[1]
    spread = (32, 7 * 128)
    number = lax.broadcasted_iota(jnp.int32, spread, 0)
    spread = (lax.broadcasted_iota(jnp.int32, spread, 1) // 128 == number % 8) & (number < 24)
    spread = jnp.where(spread, 1.0, 0.0).astype(BF16)
    scale = jnp.where(lax.broadcasted_iota(jnp.int32, (8, BLK), 0) < 3, 0.25, 1.0)
    for block in range(panels // BLK):
        values = geometry_ref[:, block * BLK : (block + 1) * BLK]
        values = jnp.concatenate([values, values[:1]], 0) * scale
        high = values.astype(BF16).astype(F32)
        middle = (values - high).astype(BF16).astype(F32)
        parts = jnp.concatenate([high, middle, values - high - middle, jnp.zeros_like(values)], 0).astype(BF16)
        columns = lax.dot_general(parts, spread, (((0,), (0,)), ((), ())), preferred_element_type=F32)
        for part in range(7):
            panel_ref[block, part] = columns[:, part * 128 : (part + 1) * 128]

    cap = slot_ref.shape[0] // sections
    padded = ids_ref.shape[0]
    owner = owner_ref[...]
    dest = owner // CELL_DEV
    lane = lax.broadcasted_iota(jnp.int32, (padded, panels), 1)
    mine = dest == lax.broadcasted_iota(jnp.int32, (padded, panels), 0)
    ones = jnp.where(mine, 1.0, 0.0).astype(BF16)
    square = (128, 128)
    upto = lax.broadcasted_iota(jnp.int32, square, 0) <= lax.broadcasted_iota(jnp.int32, square, 1)
    upto = jnp.where(upto, 1.0, 0.0).astype(BF16)
    every = jnp.ones(square, BF16)
    carry = jnp.zeros((padded, 128), F32)
    counts = []
    for begin in range(0, panels, 128):
        piece = ones[:, begin : begin + 128]
        counts.append(carry + jnp.dot(piece, upto, preferred_element_type=F32))
        carry = carry + jnp.dot(piece, every, preferred_element_type=F32)
    count = jnp.concatenate(counts, 1).astype(jnp.int32)
    before = jnp.sum(jnp.where(mine, count - 1, 0), axis=0, keepdims=True)
    rank = before // 4
    slot = jnp.where(lane[:1] < count_ref[0], dest * cap + rank, -1)
    slot = jnp.broadcast_to(slot, (16, panels)).astype(jnp.int16)
    number = lax.broadcasted_iota(jnp.int16, (16, panels), 0)
    one, zero = jnp.array(1, BF16), jnp.array(0, BF16)
    for row in range(0, slot_ref.shape[0], 16):
        slot_ref[row : row + 16, :] = jnp.where(slot == number + jnp.int16(row), one, zero)

    at_lane = rank + lax.axis_index("sect") * cap % 128 == lax.broadcasted_iota(jnp.int32, (128, panels), 0)
    at_lane = jnp.where(at_lane, 1.0, 0.0).astype(BF16)
    cell = jnp.where(mine & (lane % 4 == 0), owner % CELL_DEV, 0).astype(F32).astype(BF16)
    ids_ref[...] = lax.dot_general(cell, at_lane, (((1,), (1,)), ((), ())), preferred_element_type=F32)


def panel_columns(sections, counts, geometry, owners):
    panels = geometry.shape[1]
    cap = 2 * CELL_DEV // sections
    padded = -(-sections // EXTRA) * EXTRA
    return call(
        functools.partial(column_kernel, sections),
        "columns",
        (
            jax.ShapeDtypeStruct((panels // BLK, 7, BLK, 128), F32),
            jax.ShapeDtypeStruct((sections * cap, panels), BF16),
            jax.ShapeDtypeStruct((padded, 128), F32),
        ),
        [SMEM, WHOLE, WHOLE],
        [WHOLE] * 3,
        work=2_000_000_000,
    )(counts, geometry, owners.reshape(1, panels))


def corner_kernel(count_ref, conn_ref, corner_ref):
    panels = conn_ref.shape[1]
    live = lax.broadcasted_iota(jnp.int32, (16, panels), 1) < count_ref[0]
    corners = [
        jnp.where(live, jnp.broadcast_to(conn_ref[i : i + 1, :], (16, panels)), -1).astype(jnp.int16) for i in range(4)
    ]
    number = lax.broadcasted_iota(jnp.int16, (16, panels), 0)
    share, zero = jnp.array(0.25, BF16), jnp.array(0, BF16)
    for row in range(0, NODE_ROWS, 16):
        node = number + jnp.int16(row)
        total = jnp.where(corners[0] == node, share, zero)
        for corner in corners[1:]:
            total = total + jnp.where(corner == node, share, zero)
        corner_ref[row : row + 16, :] = total


def corner_matrix(counts, connectivity):
    return call(
        corner_kernel,
        "corners",
        jax.ShapeDtypeStruct((NODE_ROWS, connectivity.shape[1]), BF16),
        [SMEM, WHOLE],
        WHOLE,
        work=2_000_000_000,
    )(counts, connectivity)


def pack_kernel(signal_ref, point_ref, message_ref, wide_ref):
    count = signal_ref.shape[0]
    wide_ref[...] = jnp.zeros_like(wide_ref)
    wide_ref[:3, :count] = point_ref[...].astype(F32)
    extra = pltpu.roll(wide_ref[...], lax.axis_index("sect") * count, 1).astype(BF16)
    for section in range(message_ref.shape[0]):
        message_ref[section, :count, :] = signal_ref[...]
        message_ref[section, count:, :] = extra


def join_kernel(message_ref, chunk_ref):
    sections = message_ref.shape[0]
    count = message_ref.shape[1] - EXTRA
    total = jnp.zeros((EXTRA, message_ref.shape[2]), F32)
    for section in range(sections):
        chunk_ref[section * count : (section + 1) * count, :] = message_ref[section, :count, :]
        total = total + message_ref[section, count:, :].astype(F32)
    chunk_ref[sections * count :, :] = total.astype(BF16)


def sources_kernel(offsets, first, last, count_ref, *refs):
    refs = list(refs)

    def take(number):
        taken = refs[:number]
        del refs[:number]
        return taken

    parts = len(offsets)
    chunks = take(parts)
    source_ref, panel_ref = take(2)
    if last:
        loading_in, thick_in, slot_ref, ids_ref, corner_ref = take(5)
        loading_ref, message_ref, rim_ref, thick_ref = take(4)
    else:
        loading_in, thick_in = (None, None) if first else take(2)
        loading_ref, thick_ref = take(2)
    code_ref, scale_ref, mass_ref, pair_ref, window_ref = take(5)

    blocks = source_ref.shape[1]
    span = chunks[0].shape[0] - EXTRA
    observers = parts * span
    points = []
    for number, chunk in enumerate(chunks):
        low = chunk[:span, :128].astype(F32)
        high = chunk[:span, 128:].astype(F32)
        most = jnp.max(jnp.maximum(jnp.abs(low), jnp.abs(high)), axis=1, keepdims=True)
        most = jnp.maximum(jnp.broadcast_to(most, (span, 128)), 1e-30)
        low = jnp.floor(low * (FIXED / most) + 0.5).astype(jnp.int32)
        high = jnp.floor(high * (FIXED / most) + 0.5).astype(jnp.int32)
        code_ref[number * span : (number + 1) * span, :] = (high << 16) | (low & 0xFFFF)
        scale_ref[number * span : (number + 1) * span, :] = most * (1 / (FIXED * 65536))
        points.append(chunk[span : span + EXTRA, :].astype(F32) * 0.25)

    lanes = lax.broadcasted_iota(jnp.int32, (128, 128), 1)
    for block in range(blocks):
        for number, offset in enumerate(offsets):
            group = lax.axis_index("azim") ^ offset
            for piece in range(span // 128):
                here = number * span + piece * 128
                source = source_ref[group, block, piece * 128 : (piece + 1) * 128, :]
                at = source & 127
                code = jnp.take_along_axis(code_ref[here : here + 128, :], at, axis=1, mode="promise_in_bounds")
                scale = scale_ref[here : here + 128, :]
                current = jnp.where(source < 128, code << 16, code)
                following = (jnp.where(lanes == 0, code, current).astype(F32) * scale).astype(BF16)
                following = pltpu.roll(following, 127, 1)
                current = (current.astype(F32) * scale).astype(BF16)
                window_ref[block, here : here + 128, :] = current
                window_ref[block, observers + here : observers + here + 128, :] = following - current

        for strip in range(BLK // 16):
            rows = slice(strip * 16, strip * 16 + 16)
            x, y, z, normal_x, normal_y, normal_z, area = (panel_ref[block, i, rows, :] for i in range(7))
            for piece in range(observers // 128):
                here = piece * 128
                at_x, at_y, at_z = (
                    points[here // span][i : i + 1, here % span : here % span + 128] for i in range(3)
                )
                delta_x = at_x - x
                delta_y = at_y - y
                delta_z = at_z - z
                inverse = lax.rsqrt(delta_x * delta_x + delta_y * delta_y + delta_z * delta_z)
                flux = normal_x * delta_x + normal_y * delta_y + normal_z * delta_z
                far = flux * inverse * inverse
                pair_ref[block, rows, here : here + 128] = (far * inverse).astype(BF16)
                pair_ref[block, rows, observers + here : observers + here + 128] = far.astype(BF16)
                mass_ref[block, rows, here : here + 128] = (area * inverse).astype(BF16)
        rows = slice(block * BLK, (block + 1) * BLK)
        thick = jnp.dot(mass_ref[block], window_ref[block, observers:, :], preferred_element_type=F32)
        loading = jnp.dot(pair_ref[block], window_ref[block], preferred_element_type=F32)
        if not first:
            thick = thick + thick_in[rows, :]
            loading = loading + loading_in[rows, :]
        if last:
            alive = block * BLK + lax.broadcasted_iota(jnp.int32, (BLK, TW), 0) < count_ref[0]
            thick = jnp.where(alive, thick, 0.0).astype(BF16)
            loading = jnp.where(alive, loading, 0.0).astype(BF16)
        thick_ref[rows, :] = thick
        loading_ref[rows, :] = loading

    if last:
        sections = message_ref.shape[0]
        cap = slot_ref.shape[0] // sections
        slots = jnp.dot(slot_ref[...], thick_ref[...], preferred_element_type=F32).astype(BF16)
        for section in range(sections):
            message_ref[section, :cap, :] = slots[section * cap : (section + 1) * cap]
            ids = jnp.broadcast_to(ids_ref[section : section + 1, :], (EXTRA, 128))
            message_ref[section, cap:, :] = ids.astype(BF16)
        rim = jnp.dot(corner_ref[NODE_DEV - 8 :, :], loading_ref[...], preferred_element_type=F32)
        rim_ref[...] = rim[8:].astype(BF16)


def sources(offsets, counts, chunks, source, panel_values, sums=(), slots=None, sections=None):
    blocks = source.shape[1]
    panels = panel_values.shape[0] * BLK
    observers = len(offsets) * (chunks[0].shape[0] - EXTRA)
    last = slots is not None
    operands = [counts, *chunks, source, panel_values, *sums]
    scratch = [
        VMEM((observers, 128), jnp.int32),
        VMEM((observers, 128), F32),
        VMEM((blocks, BLK, observers), BF16),
        VMEM((blocks, BLK, 2 * observers), BF16),
        VMEM((blocks, 2 * observers, TW), BF16),
    ]
    aliases = {}
    if last:
        operands += slots
        cap = 2 * CELL_DEV // sections
        out_shape = [
            jax.ShapeDtypeStruct((panels, TW), BF16),
            jax.ShapeDtypeStruct((sections, cap + EXTRA, TW), BF16),
            jax.ShapeDtypeStruct((HEAD, TW), BF16),
        ]
        scratch = [VMEM((panels, TW), BF16)] + scratch
    else:
        out_shape = [jax.ShapeDtypeStruct((panels, TW), F32)] * 2
        if sums:
            aliases = {len(operands) - 2: 0, len(operands) - 1: 1}
    return call(
        functools.partial(sources_kernel, offsets, not sums, last),
        "sources",
        out_shape,
        [SMEM] + [WHOLE] * (len(operands) - 1),
        [WHOLE] * len(out_shape),
        scratch,
        aliases,
        work=3_000_000_000,
    )(*operands)


def node_kernel(corner_ref, loading_ref, node_ref, head_ref):
    nodes = jnp.dot(corner_ref[: NODE_DEV + 8, :], loading_ref[...], preferred_element_type=F32)
    head_ref[...] = nodes[:HEAD]
    node_ref[...] = nodes[:NODE_DEV]


def node_sums(corners, loading):
    return call(
        node_kernel,
        "nodes",
        (jax.ShapeDtypeStruct((NODE_DEV, TW), F32), jax.ShapeDtypeStruct((HEAD, TW), F32)),
        [WHOLE] * 2,
        [WHOLE] * 2,
        work=2_000_000_000,
    )(corners, loading)


def finish_kernel(message_ref, rim_ref, head_ref, _, node_ref, cell_ref, rows_ref, top_ref, total_ref, sems):
    sections = message_ref.shape[0]
    cap = message_ref.shape[1] - EXTRA
    per = 128 // cap
    top_ref[...] = head_ref[...] + rim_ref[...].astype(F32)
    top_copy = pltpu.make_async_copy(top_ref, node_ref.at[pl.ds(0, HEAD), :], sems.at[0])
    top_copy.start()
    total = jnp.zeros((CELL_DEV, TW), F32)
    cell = lax.broadcasted_iota(jnp.int32, (CELL_DEV, 128), 0).astype(F32)
    for group in range(sections // per):
        ids = jnp.zeros((EXTRA, 128), F32)
        for inner in range(per):
            section = group * per + inner
            ids = ids + message_ref[section, cap:, :].astype(F32)
            rows_ref[section * cap : (section + 1) * cap, :] = message_ref[section, :cap, :]
        match = jnp.where(ids[:1] == cell, 1.0, 0.0).astype(BF16)
        total = total + jnp.dot(match, rows_ref[group * 128 : (group + 1) * 128, :], preferred_element_type=F32)
    total_ref[...] = total
    cell_copy = pltpu.make_async_copy(total_ref, cell_ref, sems.at[1])
    cell_copy.start()
    top_copy.wait()
    cell_copy.wait()


def finish(message, rim, head, nodes):
    sections = message.shape[0]
    cap = message.shape[1] - EXTRA
    return call(
        finish_kernel,
        "finish",
        (
            jax.ShapeDtypeStruct((NODE_DEV, TW), F32),
            jax.ShapeDtypeStruct((CELL_DEV, TW), F32),
        ),
        [WHOLE] * 3 + [PLACE],
        [PLACE] * 2,
        [VMEM((sections * cap, TW), BF16), VMEM((HEAD, TW), F32), VMEM((CELL_DEV, TW), F32), COPY((2,))],
        {3: 0},
    )(message, rim, head, nodes)


def swapped(array, axis, bit):
    peers = lax.axis_size(axis)
    return lax.ppermute(array, axis, [(i, i ^ bit) for i in range(peers)])


def after(array, other):
    return lax.optimization_barrier((array, other))[0]


def section_chunk(signals, xyz, sections):
    count, width = signals.shape
    span = sections * count
    kernels = count % 16 == 0
    if kernels:
        shape = jax.ShapeDtypeStruct((sections, count + EXTRA, width), BF16)
        message = call(pack_kernel, "pack", shape, [WHOLE] * 2, WHOLE, [VMEM((EXTRA, width), F32)])(signals, xyz.T)
    else:
        extra = jnp.zeros((EXTRA, width), BF16)
        extra = lax.dynamic_update_slice(extra, xyz.T, (0, lax.axis_index("sect") * count))
        message = jnp.broadcast_to(jnp.concatenate([signals, extra], 0), (sections, count + EXTRA, width))
    message = lax.all_to_all(message, "sect", split_axis=0, concat_axis=0, tiled=True)
    if kernels:
        return call(join_kernel, "join", jax.ShapeDtypeStruct((span + EXTRA, width), BF16), [WHOLE], WHOLE)(message)
    return jnp.concatenate(
        [message[:, :count].reshape(span, width), message[:, count:].astype(F32).sum(0).astype(BF16)], 0
    )


def per_device(signals, observer_xyz, panel_geometry, delays, counts, connectivity, owners):
    sections = lax.axis_size("sect")
    groups = lax.axis_size("azim")

    source = window_index(groups, delays)
    panel_values, slots, ids = panel_columns(sections, counts, panel_geometry, owners)
    corners = corner_matrix(counts, connectivity)

    def add(sums, offsets, chunks, *rest):
        return sources(offsets, counts, chunks, source, panel_values, sums, *rest)

    chunk = section_chunk(signals, observer_xyz, sections)
    near = swapped(chunk, "azim", 1)
    chunks = {0: chunk}
    bit = groups // 2
    while bit > 1:
        for offset in list(chunks):
            chunks[offset ^ bit] = swapped(chunks[offset], "azim", bit)
        bit //= 2
    sums = add((), [0], [chunk])
    sums = add(sums, [1], [near])
    rest = [offset for offset in chunks if offset]
    for offset in rest:
        chunks[offset] = after(chunks[offset], sums[0])
        chunks[offset ^ 1] = swapped(chunks[offset], "azim", 1)
    sums = add(sums, rest, [chunks[o] for o in rest])
    rest = [offset ^ 1 for offset in rest]
    matrices = [slots, ids, corners]
    loading, message, rim = add(sums, rest, [chunks[o] for o in rest], matrices, sections)
    message = lax.all_to_all(message, "sect", split_axis=0, concat_axis=0, tiled=True)
    rim = lax.ppermute(rim, "sect", [(i, (i + 1) % sections) for i in range(sections)])
    nodes, head = node_sums(corners, loading)
    return finish(message, rim, head, nodes)


def solution(mesh):
    in_specs = (
        P(("azim", "sect"), None),
        P(("azim", "sect"), None),
        P(None, ("azim", "sect")),
        P(("azim", "sect"), None),
        P(("azim", "sect")),
        P(None, ("azim", "sect")),
        P(("azim", "sect")),
    )
    out_specs = (P(("azim", "sect"), None), P(("azim", "sect"), None))
    return jax.shard_map(
        per_device, mesh=mesh, in_specs=in_specs, out_specs=out_specs, check_vma=False
    )
```

```python
import functools

import jax
import jax.numpy as jnp
from jax import lax
from jax.experimental import pallas as pl
from jax.experimental.pallas import tpu as pltpu
from jax.sharding import PartitionSpec as P

NPU = 128
BLK = 128
TW = 128
CELL_DEV = 256
NODE_DEV = 1032
RIM = NPU + 1
HEAD = 136
NODE_ROWS = 1168
EXTRA = 16
FIXED = 32000.0
F32 = jnp.float32
BF16 = jnp.bfloat16
VMEM = pltpu.VMEM
SMEM = pl.BlockSpec(memory_space=pltpu.SMEM)
WHOLE = pl.BlockSpec(memory_space=pltpu.VMEM)
PLACE = pl.BlockSpec(memory_space=pl.ANY)
COPY = pltpu.SemaphoreType.DMA


def call(kernel, name, out_shape, in_specs, out_specs, scratch_shapes=(), aliases=None, work=1_000_000):
    return pl.pallas_call(
        kernel,
        out_shape=out_shape,
        in_specs=in_specs,
        out_specs=out_specs,
        scratch_shapes=list(scratch_shapes),
        input_output_aliases=aliases or {},
        compiler_params=pltpu.CompilerParams(vmem_limit_bytes=24 * 1024 * 1024),
        cost_estimate=pl.CostEstimate(flops=work, bytes_accessed=4_000_000, transcendentals=0),
        name=name,
    )


def window_kernel(sections, paired, delay_ref, source_ref):
    groups, blocks, span, _ = source_ref.shape
    count = span // sections
    piece_rows = count if paired else 128
    padded = -(-blocks // 16) * 16
    delay = delay_ref[...].astype(F32)
    delay = jnp.concatenate([delay, jnp.zeros((padded - blocks, delay.shape[1]), F32)], 0).astype(BF16)
    spread = (padded, blocks * 128)
    spread = lax.broadcasted_iota(jnp.int32, spread, 1) // 128 == lax.broadcasted_iota(jnp.int32, spread, 0)
    spread = jnp.where(spread, 1.0, 0.0).astype(BF16)
    lanes = lax.broadcasted_iota(jnp.int32, (128, 128), 1)
    for piece in range(groups * span // 128):
        columns = lax.dot_general(
            delay[:, piece * 128 : (piece + 1) * 128], spread, (((0,), (0,)), ((), ())), preferred_element_type=F32
        )
        for block in range(blocks):
            source = columns[:, block * 128 : (block + 1) * 128].astype(jnp.int32) + lanes
            for part in range(128 // piece_rows):
                row = piece * 128 + part * piece_rows
                begin = row % span
                if paired:
                    apart = lax.axis_index("sect") ^ (begin // count)
                    turned = apart // 4 + apart // 2 % 2 * 2 + apart % 2 * 4
                    begin = pl.multiple_of(turned * count, count)
                source_ref[row // span, block, pl.ds(begin, piece_rows), :] = source[
                    part * piece_rows : (part + 1) * piece_rows
                ]


def window_index(sections, groups, paired, delays):
    blocks, observers = delays.shape
    return call(
        functools.partial(window_kernel, sections, paired),
        "windows",
        jax.ShapeDtypeStruct((groups, blocks, observers // groups, 128), jnp.int32),
        [WHOLE],
        WHOLE,
        work=2_000_000_000,
    )(delays)


def column_kernel(sections, count_ref, geometry_ref, owner_ref, panel_ref, slot_ref, ids_ref):
    panels = geometry_ref.shape[1]
    spread = (32, 7 * 128)
    number = lax.broadcasted_iota(jnp.int32, spread, 0)
    spread = (lax.broadcasted_iota(jnp.int32, spread, 1) // 128 == number % 8) & (number < 24)
    spread = jnp.where(spread, 1.0, 0.0).astype(BF16)
    scale = jnp.where(lax.broadcasted_iota(jnp.int32, (8, BLK), 0) < 3, 0.25, 1.0)
    for block in range(panels // BLK):
        values = geometry_ref[:, block * BLK : (block + 1) * BLK]
        values = jnp.concatenate([values, values[:1]], 0) * scale
        high = values.astype(BF16).astype(F32)
        middle = (values - high).astype(BF16).astype(F32)
        parts = jnp.concatenate([high, middle, values - high - middle, jnp.zeros_like(values)], 0).astype(BF16)
        columns = lax.dot_general(parts, spread, (((0,), (0,)), ((), ())), preferred_element_type=F32)
        for part in range(7):
            panel_ref[block, part] = columns[:, part * 128 : (part + 1) * 128]

    cap = slot_ref.shape[0] // sections
    padded = ids_ref.shape[0]
    owner = owner_ref[...]
    dest = owner // CELL_DEV
    lane = lax.broadcasted_iota(jnp.int32, (padded, panels), 1)
    mine = dest == lax.broadcasted_iota(jnp.int32, (padded, panels), 0)
    ones = jnp.where(mine, 1.0, 0.0).astype(BF16)
    square = (128, 128)
    upto = lax.broadcasted_iota(jnp.int32, square, 0) <= lax.broadcasted_iota(jnp.int32, square, 1)
    upto = jnp.where(upto, 1.0, 0.0).astype(BF16)
    every = jnp.ones(square, BF16)
    carry = jnp.zeros((padded, 128), F32)
    counts = []
    for begin in range(0, panels, 128):
        piece = ones[:, begin : begin + 128]
        counts.append(carry + jnp.dot(piece, upto, preferred_element_type=F32))
        carry = carry + jnp.dot(piece, every, preferred_element_type=F32)
    count = jnp.concatenate(counts, 1).astype(jnp.int32)
    before = jnp.sum(jnp.where(mine, count - 1, 0), axis=0, keepdims=True)
    rank = before // 4
    slot = jnp.where(lane[:1] < count_ref[0], dest * cap + rank, -1)
    slot = jnp.broadcast_to(slot, (16, panels)).astype(jnp.int16)
    number = lax.broadcasted_iota(jnp.int16, (16, panels), 0)
    one, zero = jnp.array(1, BF16), jnp.array(0, BF16)
    for row in range(0, slot_ref.shape[0], 16):
        slot_ref[row : row + 16, :] = jnp.where(slot == number + jnp.int16(row), one, zero)

    at_lane = rank + lax.axis_index("sect") * cap % 128 == lax.broadcasted_iota(jnp.int32, (128, panels), 0)
    at_lane = jnp.where(at_lane, 1.0, 0.0).astype(BF16)
    cell = jnp.where(mine & (lane % 4 == 0), owner % CELL_DEV, 0).astype(F32).astype(BF16)
    ids_ref[...] = lax.dot_general(cell, at_lane, (((1,), (1,)), ((), ())), preferred_element_type=F32)


def panel_columns(sections, counts, geometry, owners):
    panels = geometry.shape[1]
    cap = 2 * CELL_DEV // sections
    padded = -(-sections // EXTRA) * EXTRA
    return call(
        functools.partial(column_kernel, sections),
        "columns",
        (
            jax.ShapeDtypeStruct((panels // BLK, 7, BLK, 128), F32),
            jax.ShapeDtypeStruct((sections * cap, panels), BF16),
            jax.ShapeDtypeStruct((padded, 128), F32),
        ),
        [SMEM, WHOLE, WHOLE],
        [WHOLE] * 3,
        work=2_000_000_000,
    )(counts, geometry, owners.reshape(1, panels))


def corner_kernel(count_ref, conn_ref, corner_ref):
    panels = conn_ref.shape[1]
    live = lax.broadcasted_iota(jnp.int32, (16, panels), 1) < count_ref[0]
    corners = [
        jnp.where(live, jnp.broadcast_to(conn_ref[i : i + 1, :], (16, panels)), -1).astype(jnp.int16) for i in range(4)
    ]
    number = lax.broadcasted_iota(jnp.int16, (16, panels), 0)
    share, zero = jnp.array(0.25, BF16), jnp.array(0, BF16)
    for row in range(0, NODE_ROWS, 16):
        node = number + jnp.int16(row)
        total = jnp.where(corners[0] == node, share, zero)
        for corner in corners[1:]:
            total = total + jnp.where(corner == node, share, zero)
        corner_ref[row : row + 16, :] = total


def corner_matrix(counts, connectivity):
    return call(
        corner_kernel,
        "corners",
        jax.ShapeDtypeStruct((NODE_ROWS, connectivity.shape[1]), BF16),
        [SMEM, WHOLE],
        WHOLE,
        work=2_000_000_000,
    )(counts, connectivity)


def first_join_kernel(*refs):
    *inputs, chunk_ref, wide_ref = refs
    parts = len(inputs) // 2
    count = inputs[0].shape[0]
    wide_ref[...] = jnp.zeros_like(wide_ref)
    total = jnp.zeros(wide_ref.shape, F32)
    for part in range(parts):
        chunk_ref[part * count : (part + 1) * count, :] = inputs[part][...]
        wide_ref[:3, :count] = inputs[parts + part][...].astype(F32)
        total = total + (pltpu.roll(wide_ref[...], part * count, 1) if part else wide_ref[...])
    chunk_ref[parts * count :, :] = total.astype(BF16)


def join_kernel(mine_ref, other_ref, chunk_ref):
    span = mine_ref.shape[0] - EXTRA
    chunk_ref[:span, :] = mine_ref[:span, :]
    chunk_ref[span : 2 * span, :] = other_ref[:span, :]
    moved = pltpu.roll(other_ref[span:, :].astype(F32), span, 1)
    chunk_ref[2 * span :, :] = (mine_ref[span:, :].astype(F32) + moved).astype(BF16)


def sources_kernel(places, first, last, count_ref, *refs):
    refs = list(refs)

    def take(number):
        taken = refs[:number]
        del refs[:number]
        return taken

    parts = len(places)
    chunks = take(parts)
    source_ref, panel_ref = take(2)
    if last:
        loading_in, thick_in, slot_ref, ids_ref, corner_ref = take(5)
        loading_ref, message_ref, rim_ref, thick_ref = take(4)
    else:
        loading_in, thick_in = (None, None) if first else take(2)
        loading_ref, thick_ref = take(2)
    code_ref, scale_ref, mass_ref, pair_ref, window_ref = take(5)

    blocks = source_ref.shape[1]
    span = chunks[0].shape[0] - EXTRA
    observers = parts * span
    points = []
    for number, chunk in enumerate(chunks):
        low = chunk[:span, :128].astype(F32)
        high = chunk[:span, 128:].astype(F32)
        most = jnp.max(jnp.maximum(jnp.abs(low), jnp.abs(high)), axis=1, keepdims=True)
        most = jnp.maximum(jnp.broadcast_to(most, (span, 128)), 1e-30)
        low = jnp.floor(low * (FIXED / most) + 0.5).astype(jnp.int32)
        high = jnp.floor(high * (FIXED / most) + 0.5).astype(jnp.int32)
        code_ref[number * span : (number + 1) * span, :] = (high << 16) | (low & 0xFFFF)
        scale_ref[number * span : (number + 1) * span, :] = most * (1 / (FIXED * 65536))
        points.append(chunk[span : span + EXTRA, :].astype(F32) * 0.25)

    lanes = lax.broadcasted_iota(jnp.int32, (128, 128), 1)
    for block in range(blocks):
        for number, (offset, begin) in enumerate(places):
            group = lax.axis_index("azim") ^ offset
            for piece in range(span // 128):
                here = number * span + piece * 128
                source = source_ref[group, block, begin + piece * 128 : begin + (piece + 1) * 128, :]
                at = source & 127
                code = jnp.take_along_axis(code_ref[here : here + 128, :], at, axis=1, mode="promise_in_bounds")
                scale = scale_ref[here : here + 128, :]
                current = jnp.where(source < 128, code << 16, code)
                following = (jnp.where(lanes == 0, code, current).astype(F32) * scale).astype(BF16)
                following = pltpu.roll(following, 127, 1)
                current = (current.astype(F32) * scale).astype(BF16)
                window_ref[block, here : here + 128, :] = current
                window_ref[block, observers + here : observers + here + 128, :] = following - current

        for strip in range(BLK // 16):
            rows = slice(strip * 16, strip * 16 + 16)
            x, y, z, normal_x, normal_y, normal_z, area = (panel_ref[block, i, rows, :] for i in range(7))
            for piece in range(observers // 128):
                here = piece * 128
                at_x, at_y, at_z = (
                    points[here // span][i : i + 1, here % span : here % span + 128] for i in range(3)
                )
                delta_x = at_x - x
                delta_y = at_y - y
                delta_z = at_z - z
                inverse = lax.rsqrt(delta_x * delta_x + delta_y * delta_y + delta_z * delta_z)
                flux = normal_x * delta_x + normal_y * delta_y + normal_z * delta_z
                far = flux * inverse * inverse
                pair_ref[block, rows, here : here + 128] = (far * inverse).astype(BF16)
                pair_ref[block, rows, observers + here : observers + here + 128] = far.astype(BF16)
                mass_ref[block, rows, here : here + 128] = (area * inverse).astype(BF16)
        rows = slice(block * BLK, (block + 1) * BLK)
        thick = jnp.dot(mass_ref[block], window_ref[block, observers:, :], preferred_element_type=F32)
        loading = jnp.dot(pair_ref[block], window_ref[block], preferred_element_type=F32)
        if not first:
            thick = thick + thick_in[rows, :]
            loading = loading + loading_in[rows, :]
        if last:
            alive = block * BLK + lax.broadcasted_iota(jnp.int32, (BLK, TW), 0) < count_ref[0]
            thick = jnp.where(alive, thick, 0.0).astype(BF16)
            loading = jnp.where(alive, loading, 0.0).astype(BF16)
        thick_ref[rows, :] = thick
        loading_ref[rows, :] = loading

    if last:
        sections = message_ref.shape[0]
        cap = slot_ref.shape[0] // sections
        slots = jnp.dot(slot_ref[...], thick_ref[...], preferred_element_type=F32).astype(BF16)
        for section in range(sections):
            message_ref[section, :cap, :] = slots[section * cap : (section + 1) * cap]
            ids = jnp.broadcast_to(ids_ref[section : section + 1, :], (EXTRA, 128))
            message_ref[section, cap:, :] = ids.astype(BF16)
        rim = jnp.dot(corner_ref[NODE_DEV - 8 :, :], loading_ref[...], preferred_element_type=F32)
        rim_ref[...] = rim[8:].astype(BF16)


def sources(places, counts, chunks, source, panel_values, sums=(), slots=None, sections=None):
    blocks = source.shape[1]
    panels = panel_values.shape[0] * BLK
    observers = len(places) * (chunks[0].shape[0] - EXTRA)
    last = slots is not None
    operands = [counts, *chunks, source, panel_values, *sums]
    scratch = [
        VMEM((observers, 128), jnp.int32),
        VMEM((observers, 128), F32),
        VMEM((blocks, BLK, observers), BF16),
        VMEM((blocks, BLK, 2 * observers), BF16),
        VMEM((blocks, 2 * observers, TW), BF16),
    ]
    aliases = {}
    if last:
        operands += slots
        cap = 2 * CELL_DEV // sections
        out_shape = [
            jax.ShapeDtypeStruct((panels, TW), BF16),
            jax.ShapeDtypeStruct((sections, cap + EXTRA, TW), BF16),
            jax.ShapeDtypeStruct((HEAD, TW), BF16),
        ]
        scratch = [VMEM((panels, TW), BF16)] + scratch
    else:
        out_shape = [jax.ShapeDtypeStruct((panels, TW), F32)] * 2
        if sums:
            aliases = {len(operands) - 2: 0, len(operands) - 1: 1}
    return call(
        functools.partial(sources_kernel, places, not sums, last),
        "sources",
        out_shape,
        [SMEM] + [WHOLE] * (len(operands) - 1),
        [WHOLE] * len(out_shape),
        scratch,
        aliases,
        work=3_000_000_000,
    )(*operands)


def node_kernel(corner_ref, loading_ref, node_ref, head_ref):
    nodes = jnp.dot(corner_ref[: NODE_DEV + 8, :], loading_ref[...], preferred_element_type=F32)
    head_ref[...] = nodes[:HEAD]
    node_ref[...] = nodes[:NODE_DEV]


def node_sums(corners, loading):
    return call(
        node_kernel,
        "nodes",
        (jax.ShapeDtypeStruct((NODE_DEV, TW), F32), jax.ShapeDtypeStruct((HEAD, TW), F32)),
        [WHOLE] * 2,
        [WHOLE] * 2,
        work=2_000_000_000,
    )(corners, loading)


def finish_kernel(message_ref, rim_ref, head_ref, _, node_ref, cell_ref, rows_ref, top_ref, total_ref, sems):
    sections = message_ref.shape[0]
    cap = message_ref.shape[1] - EXTRA
    per = 128 // cap
    top_ref[...] = head_ref[...] + rim_ref[...].astype(F32)
    top_copy = pltpu.make_async_copy(top_ref, node_ref.at[pl.ds(0, HEAD), :], sems.at[0])
    top_copy.start()
    total = jnp.zeros((CELL_DEV, TW), F32)
    cell = lax.broadcasted_iota(jnp.int32, (CELL_DEV, 128), 0).astype(F32)
    for group in range(sections // per):
        ids = jnp.zeros((EXTRA, 128), F32)
        for inner in range(per):
            section = group * per + inner
            ids = ids + message_ref[section, cap:, :].astype(F32)
            rows_ref[section * cap : (section + 1) * cap, :] = message_ref[section, :cap, :]
        match = jnp.where(ids[:1] == cell, 1.0, 0.0).astype(BF16)
        total = total + jnp.dot(match, rows_ref[group * 128 : (group + 1) * 128, :], preferred_element_type=F32)
    total_ref[...] = total
    cell_copy = pltpu.make_async_copy(total_ref, cell_ref, sems.at[1])
    cell_copy.start()
    top_copy.wait()
    cell_copy.wait()


def finish(message, rim, head, nodes):
    sections = message.shape[0]
    cap = message.shape[1] - EXTRA
    return call(
        finish_kernel,
        "finish",
        (
            jax.ShapeDtypeStruct((NODE_DEV, TW), F32),
            jax.ShapeDtypeStruct((CELL_DEV, TW), F32),
        ),
        [WHOLE] * 3 + [PLACE],
        [PLACE] * 2,
        [VMEM((sections * cap, TW), BF16), VMEM((HEAD, TW), F32), VMEM((CELL_DEV, TW), F32), COPY((2,))],
        {3: 0},
    )(message, rim, head, nodes)


def swapped(array, axis, bit):
    peers = lax.axis_size(axis)
    return lax.ppermute(array, axis, [(i, i ^ bit) for i in range(peers)])


def joined(mine, other):
    span = mine.shape[0] - EXTRA
    shape = jax.ShapeDtypeStruct((2 * span + EXTRA, mine.shape[1]), BF16)
    return call(join_kernel, "join", shape, [WHOLE] * 2, WHOLE)(mine, other)


def half_chunk(signals, xyz):
    count, width = signals.shape
    turned = xyz.T
    shape = jax.ShapeDtypeStruct((2 * count + EXTRA, width), BF16)
    chunk = call(first_join_kernel, "first", shape, [WHOLE] * 4, WHOLE, [VMEM((EXTRA, width), F32)])(
        signals, swapped(signals, "sect", 4), turned, swapped(turned, "sect", 4)
    )
    return joined(chunk, swapped(chunk, "sect", 2))


def after(array, other):
    return lax.optimization_barrier((array, other))[0]


def spread_chunk(signals, xyz, sections):
    count, width = signals.shape
    extra = jnp.zeros((EXTRA, width), BF16)
    extra = lax.dynamic_update_slice(extra, xyz.T, (0, lax.axis_index("sect") * count))
    payload = jnp.concatenate([signals, extra], 0)
    everyone = jnp.broadcast_to(payload[None], (sections,) + payload.shape)
    received = lax.all_to_all(everyone, "sect", split_axis=0, concat_axis=0, tiled=True)
    return jnp.concatenate(
        [received[:, :count].reshape(sections * count, -1), received[:, count:].astype(F32).sum(0).astype(BF16)], 0
    )


def per_device(signals, observer_xyz, panel_geometry, delays, counts, connectivity, owners):
    sections = lax.axis_size("sect")
    groups = lax.axis_size("azim")
    count = signals.shape[0]
    paired = sections == 8 and groups == 4 and count % 16 == 0

    source = window_index(sections, groups, paired, delays)
    panel_values, slots, ids = panel_columns(sections, counts, after(panel_geometry, source), owners)

    def add(sums, *parts, matrices=None):
        places, chunks = [part[:2] for part in parts], [part[2] for part in parts]
        return sources(places, counts, chunks, source, panel_values, sums, matrices, sections)

    if paired:
        half = half_chunk(signals, observer_xyz)
        other = swapped(half, "sect", 1)
        near = swapped(half, "azim", 1)
        sums = add((), (0, 0, half))
        far = swapped(after(half, sums[0]), "azim", 2)
        sums = add(sums, (1, 0, near))
        far = after(far, sums[0])
        far_near = swapped(far, "azim", 1)
        other_near, other_far = swapped(other, "azim", 1), swapped(other, "azim", 2)
        sums = add(sums, (0, 128, other), (1, 128, other_near), (2, 0, far), (3, 0, far_near))
        corners = corner_matrix(counts, after(connectivity, sums[0]))
        other_far = after(other_far, sums[0])
        last = (3, 128, swapped(other_far, "azim", 1))
        sums = add(sums, (2, 128, other_far))
    else:
        chunk = spread_chunk(signals, observer_xyz, sections)
        corners = corner_matrix(counts, connectivity)
        parts = [(0, 0, chunk)]
        bit = groups // 2
        while bit:
            parts += [(offset ^ bit, 0, swapped(array, "azim", bit)) for offset, _, array in parts]
            bit //= 2
        *parts, last = parts
        sums = add((), *parts)
    loading, message, rim = add(sums, last, matrices=[slots, ids, corners])
    message = lax.all_to_all(message, "sect", split_axis=0, concat_axis=0, tiled=True)
    rim = lax.ppermute(rim, "sect", [(i, (i + 1) % sections) for i in range(sections)])
    nodes, head = node_sums(corners, loading)
    return finish(message, rim, head, nodes)


def solution(mesh):
    in_specs = (
        P(("azim", "sect"), None),
        P(("azim", "sect"), None),
        P(None, ("azim", "sect")),
        P(("azim", "sect"), None),
        P(("azim", "sect")),
        P(None, ("azim", "sect")),
        P(("azim", "sect")),
    )
    out_specs = (P(("azim", "sect"), None), P(("azim", "sect"), None))
    return jax.shard_map(
        per_device, mesh=mesh, in_specs=in_specs, out_specs=out_specs, check_vma=False
    )
```

```python
import functools

import jax
import jax.numpy as jnp
from jax import lax
from jax.experimental import pallas as pl
from jax.experimental.pallas import tpu as pltpu
from jax.sharding import PartitionSpec as P

NPU = 128
BLK = 128
TW = 128
CELL_DEV = 256
NODE_DEV = 1032
RIM = NPU + 1
HEAD = 136
NODE_ROWS = 1168
EXTRA = 16
FIXED = 32000.0
F32 = jnp.float32
BF16 = jnp.bfloat16
VMEM = pltpu.VMEM
SMEM = pl.BlockSpec(memory_space=pltpu.SMEM)
WHOLE = pl.BlockSpec(memory_space=pltpu.VMEM)
PLACE = pl.BlockSpec(memory_space=pl.ANY)
COPY = pltpu.SemaphoreType.DMA


def call(kernel, name, out_shape, in_specs, out_specs, scratch_shapes=(), aliases=None, work=1_000_000):
    return pl.pallas_call(
        kernel,
        out_shape=out_shape,
        in_specs=in_specs,
        out_specs=out_specs,
        scratch_shapes=list(scratch_shapes),
        input_output_aliases=aliases or {},
        compiler_params=pltpu.CompilerParams(vmem_limit_bytes=24 * 1024 * 1024),
        cost_estimate=pl.CostEstimate(flops=work, bytes_accessed=4_000_000, transcendentals=0),
        name=name,
    )


def window_kernel(sections, paired, delay_ref, source_ref):
    groups, blocks, span, _ = source_ref.shape
    count = span // sections
    piece_rows = count if paired else 128
    padded = -(-blocks // 16) * 16
    delay = delay_ref[...].astype(F32)
    delay = jnp.concatenate([delay, jnp.zeros((padded - blocks, delay.shape[1]), F32)], 0).astype(BF16)
    spread = (padded, blocks * 128)
    spread = lax.broadcasted_iota(jnp.int32, spread, 1) // 128 == lax.broadcasted_iota(jnp.int32, spread, 0)
    spread = jnp.where(spread, 1.0, 0.0).astype(BF16)
    lanes = lax.broadcasted_iota(jnp.int32, (128, 128), 1)
    for piece in range(groups * span // 128):
        columns = lax.dot_general(
            delay[:, piece * 128 : (piece + 1) * 128], spread, (((0,), (0,)), ((), ())), preferred_element_type=F32
        )
        for block in range(blocks):
            source = columns[:, block * 128 : (block + 1) * 128].astype(jnp.int32) + lanes
            for part in range(128 // piece_rows):
                row = piece * 128 + part * piece_rows
                begin = row % span
                if paired:
                    apart = lax.axis_index("sect") ^ (begin // count)
                    begin = pl.multiple_of((apart // 2 + apart % 2 * (sections // 2)) * count, count)
                source_ref[row // span, block, pl.ds(begin, piece_rows), :] = source[
                    part * piece_rows : (part + 1) * piece_rows
                ]


def window_index(sections, groups, paired, delays):
    blocks, observers = delays.shape
    return call(
        functools.partial(window_kernel, sections, paired),
        "windows",
        jax.ShapeDtypeStruct((groups, blocks, observers // groups, 128), jnp.int32),
        [WHOLE],
        WHOLE,
        work=2_000_000_000,
    )(delays)


def column_kernel(sections, count_ref, geometry_ref, owner_ref, panel_ref, slot_ref, ids_ref):
    panels = geometry_ref.shape[1]
    spread = (32, 7 * 128)
    number = lax.broadcasted_iota(jnp.int32, spread, 0)
    spread = (lax.broadcasted_iota(jnp.int32, spread, 1) // 128 == number % 8) & (number < 24)
    spread = jnp.where(spread, 1.0, 0.0).astype(BF16)
    scale = jnp.where(lax.broadcasted_iota(jnp.int32, (8, BLK), 0) < 3, 0.25, 1.0)
    for block in range(panels // BLK):
        values = geometry_ref[:, block * BLK : (block + 1) * BLK]
        values = jnp.concatenate([values, values[:1]], 0) * scale
        high = values.astype(BF16).astype(F32)
        middle = (values - high).astype(BF16).astype(F32)
        parts = jnp.concatenate([high, middle, values - high - middle, jnp.zeros_like(values)], 0).astype(BF16)
        columns = lax.dot_general(parts, spread, (((0,), (0,)), ((), ())), preferred_element_type=F32)
        for part in range(7):
            panel_ref[block, part] = columns[:, part * 128 : (part + 1) * 128]

    cap = slot_ref.shape[0] // sections
    padded = ids_ref.shape[0]
    owner = owner_ref[...]
    dest = owner // CELL_DEV
    lane = lax.broadcasted_iota(jnp.int32, (padded, panels), 1)
    mine = dest == lax.broadcasted_iota(jnp.int32, (padded, panels), 0)
    ones = jnp.where(mine, 1.0, 0.0).astype(BF16)
    square = (128, 128)
    upto = lax.broadcasted_iota(jnp.int32, square, 0) <= lax.broadcasted_iota(jnp.int32, square, 1)
    upto = jnp.where(upto, 1.0, 0.0).astype(BF16)
    every = jnp.ones(square, BF16)
    carry = jnp.zeros((padded, 128), F32)
    counts = []
    for begin in range(0, panels, 128):
        piece = ones[:, begin : begin + 128]
        counts.append(carry + jnp.dot(piece, upto, preferred_element_type=F32))
        carry = carry + jnp.dot(piece, every, preferred_element_type=F32)
    count = jnp.concatenate(counts, 1).astype(jnp.int32)
    before = jnp.sum(jnp.where(mine, count - 1, 0), axis=0, keepdims=True)
    rank = before // 4
    slot = jnp.where(lane[:1] < count_ref[0], dest * cap + rank, -1)
    slot = jnp.broadcast_to(slot, (16, panels)).astype(jnp.int16)
    number = lax.broadcasted_iota(jnp.int16, (16, panels), 0)
    one, zero = jnp.array(1, BF16), jnp.array(0, BF16)
    for row in range(0, slot_ref.shape[0], 16):
        slot_ref[row : row + 16, :] = jnp.where(slot == number + jnp.int16(row), one, zero)

    at_lane = rank + lax.axis_index("sect") * cap % 128 == lax.broadcasted_iota(jnp.int32, (128, panels), 0)
    at_lane = jnp.where(at_lane, 1.0, 0.0).astype(BF16)
    cell = jnp.where(mine & (lane % 4 == 0), owner % CELL_DEV, 0).astype(F32).astype(BF16)
    ids_ref[...] = lax.dot_general(cell, at_lane, (((1,), (1,)), ((), ())), preferred_element_type=F32)


def panel_columns(sections, counts, geometry, owners):
    panels = geometry.shape[1]
    cap = 2 * CELL_DEV // sections
    padded = -(-sections // EXTRA) * EXTRA
    return call(
        functools.partial(column_kernel, sections),
        "columns",
        (
            jax.ShapeDtypeStruct((panels // BLK, 7, BLK, 128), F32),
            jax.ShapeDtypeStruct((sections * cap, panels), BF16),
            jax.ShapeDtypeStruct((padded, 128), F32),
        ),
        [SMEM, WHOLE, WHOLE],
        [WHOLE] * 3,
        work=2_000_000_000,
    )(counts, geometry, owners.reshape(1, panels))


def corner_kernel(count_ref, conn_ref, corner_ref):
    panels = conn_ref.shape[1]
    live = lax.broadcasted_iota(jnp.int32, (16, panels), 1) < count_ref[0]
    corners = [
        jnp.where(live, jnp.broadcast_to(conn_ref[i : i + 1, :], (16, panels)), -1).astype(jnp.int16) for i in range(4)
    ]
    number = lax.broadcasted_iota(jnp.int16, (16, panels), 0)
    share, zero = jnp.array(0.25, BF16), jnp.array(0, BF16)
    for row in range(0, NODE_ROWS, 16):
        node = number + jnp.int16(row)
        total = jnp.where(corners[0] == node, share, zero)
        for corner in corners[1:]:
            total = total + jnp.where(corner == node, share, zero)
        corner_ref[row : row + 16, :] = total


def corner_matrix(counts, connectivity):
    return call(
        corner_kernel,
        "corners",
        jax.ShapeDtypeStruct((NODE_ROWS, connectivity.shape[1]), BF16),
        [SMEM, WHOLE],
        WHOLE,
        work=2_000_000_000,
    )(counts, connectivity)


def first_join_kernel(*refs):
    *inputs, chunk_ref, wide_ref = refs
    parts = len(inputs) // 2
    count = inputs[0].shape[0]
    wide_ref[...] = jnp.zeros_like(wide_ref)
    total = jnp.zeros(wide_ref.shape, F32)
    for part in range(parts):
        chunk_ref[part * count : (part + 1) * count, :] = inputs[part][...]
        wide_ref[:3, :count] = inputs[parts + part][...].astype(F32)
        total = total + (pltpu.roll(wide_ref[...], part * count, 1) if part else wide_ref[...])
    chunk_ref[parts * count :, :] = total.astype(BF16)


def join_kernel(mine_ref, other_ref, chunk_ref):
    span = mine_ref.shape[0] - EXTRA
    chunk_ref[:span, :] = mine_ref[:span, :]
    chunk_ref[span : 2 * span, :] = other_ref[:span, :]
    moved = pltpu.roll(other_ref[span:, :].astype(F32), span, 1)
    chunk_ref[2 * span :, :] = (mine_ref[span:, :].astype(F32) + moved).astype(BF16)


def sources_kernel(places, first, last, count_ref, *refs):
    refs = list(refs)

    def take(number):
        taken = refs[:number]
        del refs[:number]
        return taken

    parts = len(places)
    chunks = take(parts)
    source_ref, panel_ref = take(2)
    if last:
        loading_in, thick_in, slot_ref, ids_ref, corner_ref = take(5)
        loading_ref, message_ref, rim_ref, thick_ref = take(4)
    else:
        loading_in, thick_in = (None, None) if first else take(2)
        loading_ref, thick_ref = take(2)
    code_ref, scale_ref, mass_ref, pair_ref, window_ref = take(5)

    blocks = source_ref.shape[1]
    span = chunks[0].shape[0] - EXTRA
    observers = parts * span
    points = []
    for number, chunk in enumerate(chunks):
        low = chunk[:span, :128].astype(F32)
        high = chunk[:span, 128:].astype(F32)
        most = jnp.max(jnp.maximum(jnp.abs(low), jnp.abs(high)), axis=1, keepdims=True)
        most = jnp.maximum(jnp.broadcast_to(most, (span, 128)), 1e-30)
        low = jnp.floor(low * (FIXED / most) + 0.5).astype(jnp.int32)
        high = jnp.floor(high * (FIXED / most) + 0.5).astype(jnp.int32)
        code_ref[number * span : (number + 1) * span, :] = (high << 16) | (low & 0xFFFF)
        scale_ref[number * span : (number + 1) * span, :] = most * (1 / (FIXED * 65536))
        points.append(chunk[span : span + EXTRA, :].astype(F32) * 0.25)

    lanes = lax.broadcasted_iota(jnp.int32, (128, 128), 1)
    for block in range(blocks):
        for number, (offset, begin) in enumerate(places):
            group = lax.axis_index("azim") ^ offset
            for piece in range(span // 128):
                here = number * span + piece * 128
                source = source_ref[group, block, begin + piece * 128 : begin + (piece + 1) * 128, :]
                at = source & 127
                code = jnp.take_along_axis(code_ref[here : here + 128, :], at, axis=1, mode="promise_in_bounds")
                scale = scale_ref[here : here + 128, :]
                current = jnp.where(source < 128, code << 16, code)
                following = (jnp.where(lanes == 0, code, current).astype(F32) * scale).astype(BF16)
                following = pltpu.roll(following, 127, 1)
                current = (current.astype(F32) * scale).astype(BF16)
                window_ref[block, here : here + 128, :] = current
                window_ref[block, observers + here : observers + here + 128, :] = following - current

        for strip in range(BLK // 16):
            rows = slice(strip * 16, strip * 16 + 16)
            x, y, z, normal_x, normal_y, normal_z, area = (panel_ref[block, i, rows, :] for i in range(7))
            for piece in range(observers // 128):
                here = piece * 128
                at_x, at_y, at_z = (
                    points[here // span][i : i + 1, here % span : here % span + 128] for i in range(3)
                )
                delta_x = at_x - x
                delta_y = at_y - y
                delta_z = at_z - z
                inverse = lax.rsqrt(delta_x * delta_x + delta_y * delta_y + delta_z * delta_z)
                flux = normal_x * delta_x + normal_y * delta_y + normal_z * delta_z
                far = flux * inverse * inverse
                pair_ref[block, rows, here : here + 128] = (far * inverse).astype(BF16)
                pair_ref[block, rows, observers + here : observers + here + 128] = far.astype(BF16)
                mass_ref[block, rows, here : here + 128] = (area * inverse).astype(BF16)
        rows = slice(block * BLK, (block + 1) * BLK)
        thick = jnp.dot(mass_ref[block], window_ref[block, observers:, :], preferred_element_type=F32)
        loading = jnp.dot(pair_ref[block], window_ref[block], preferred_element_type=F32)
        if not first:
            thick = thick + thick_in[rows, :]
            loading = loading + loading_in[rows, :]
        if last:
            alive = block * BLK + lax.broadcasted_iota(jnp.int32, (BLK, TW), 0) < count_ref[0]
            thick = jnp.where(alive, thick, 0.0).astype(BF16)
            loading = jnp.where(alive, loading, 0.0).astype(BF16)
        thick_ref[rows, :] = thick
        loading_ref[rows, :] = loading

    if last:
        sections = message_ref.shape[0]
        cap = slot_ref.shape[0] // sections
        slots = jnp.dot(slot_ref[...], thick_ref[...], preferred_element_type=F32).astype(BF16)
        for section in range(sections):
            message_ref[section, :cap, :] = slots[section * cap : (section + 1) * cap]
            ids = jnp.broadcast_to(ids_ref[section : section + 1, :], (EXTRA, 128))
            message_ref[section, cap:, :] = ids.astype(BF16)
        rim = jnp.dot(corner_ref[NODE_DEV - 8 :, :], loading_ref[...], preferred_element_type=F32)
        rim_ref[...] = rim[8:].astype(BF16)


def sources(places, counts, chunks, source, panel_values, sums=(), slots=None, sections=None):
    blocks = source.shape[1]
    panels = panel_values.shape[0] * BLK
    observers = len(places) * (chunks[0].shape[0] - EXTRA)
    last = slots is not None
    operands = [counts, *chunks, source, panel_values, *sums]
    scratch = [
        VMEM((observers, 128), jnp.int32),
        VMEM((observers, 128), F32),
        VMEM((blocks, BLK, observers), BF16),
        VMEM((blocks, BLK, 2 * observers), BF16),
        VMEM((blocks, 2 * observers, TW), BF16),
    ]
    aliases = {}
    if last:
        operands += slots
        cap = 2 * CELL_DEV // sections
        out_shape = [
            jax.ShapeDtypeStruct((panels, TW), BF16),
            jax.ShapeDtypeStruct((sections, cap + EXTRA, TW), BF16),
            jax.ShapeDtypeStruct((HEAD, TW), BF16),
        ]
        scratch = [VMEM((panels, TW), BF16)] + scratch
    else:
        out_shape = [jax.ShapeDtypeStruct((panels, TW), F32)] * 2
        if sums:
            aliases = {len(operands) - 2: 0, len(operands) - 1: 1}
    return call(
        functools.partial(sources_kernel, places, not sums, last),
        "sources",
        out_shape,
        [SMEM] + [WHOLE] * (len(operands) - 1),
        [WHOLE] * len(out_shape),
        scratch,
        aliases,
        work=3_000_000_000,
    )(*operands)


def node_kernel(corner_ref, loading_ref, node_ref, head_ref):
    nodes = jnp.dot(corner_ref[: NODE_DEV + 8, :], loading_ref[...], preferred_element_type=F32)
    head_ref[...] = nodes[:HEAD]
    node_ref[...] = nodes[:NODE_DEV]


def node_sums(corners, loading):
    return call(
        node_kernel,
        "nodes",
        (jax.ShapeDtypeStruct((NODE_DEV, TW), F32), jax.ShapeDtypeStruct((HEAD, TW), F32)),
        [WHOLE] * 2,
        [WHOLE] * 2,
        work=2_000_000_000,
    )(corners, loading)


def finish_kernel(message_ref, rim_ref, head_ref, _, node_ref, cell_ref, rows_ref, top_ref, total_ref, sems):
    sections = message_ref.shape[0]
    cap = message_ref.shape[1] - EXTRA
    per = 128 // cap
    top_ref[...] = head_ref[...] + rim_ref[...].astype(F32)
    top_copy = pltpu.make_async_copy(top_ref, node_ref.at[pl.ds(0, HEAD), :], sems.at[0])
    top_copy.start()
    total = jnp.zeros((CELL_DEV, TW), F32)
    cell = lax.broadcasted_iota(jnp.int32, (CELL_DEV, 128), 0).astype(F32)
    for group in range(sections // per):
        ids = jnp.zeros((EXTRA, 128), F32)
        for inner in range(per):
            section = group * per + inner
            ids = ids + message_ref[section, cap:, :].astype(F32)
            rows_ref[section * cap : (section + 1) * cap, :] = message_ref[section, :cap, :]
        match = jnp.where(ids[:1] == cell, 1.0, 0.0).astype(BF16)
        total = total + jnp.dot(match, rows_ref[group * 128 : (group + 1) * 128, :], preferred_element_type=F32)
    total_ref[...] = total
    cell_copy = pltpu.make_async_copy(total_ref, cell_ref, sems.at[1])
    cell_copy.start()
    top_copy.wait()
    cell_copy.wait()


def finish(message, rim, head, nodes):
    sections = message.shape[0]
    cap = message.shape[1] - EXTRA
    return call(
        finish_kernel,
        "finish",
        (
            jax.ShapeDtypeStruct((NODE_DEV, TW), F32),
            jax.ShapeDtypeStruct((CELL_DEV, TW), F32),
        ),
        [WHOLE] * 3 + [PLACE],
        [PLACE] * 2,
        [VMEM((sections * cap, TW), BF16), VMEM((HEAD, TW), F32), VMEM((CELL_DEV, TW), F32), COPY((2,))],
        {3: 0},
    )(message, rim, head, nodes)


def swapped(array, axis, bit):
    peers = lax.axis_size(axis)
    return lax.ppermute(array, axis, [(i, i ^ bit) for i in range(peers)])


def joined(mine, other):
    span = mine.shape[0] - EXTRA
    shape = jax.ShapeDtypeStruct((2 * span + EXTRA, mine.shape[1]), BF16)
    return call(join_kernel, "join", shape, [WHOLE] * 2, WHOLE)(mine, other)


def half_chunk(signals, xyz, sections):
    count, width = signals.shape
    turned = xyz.T
    shape = jax.ShapeDtypeStruct((2 * count + EXTRA, width), BF16)
    chunk = call(first_join_kernel, "first", shape, [WHOLE] * 4, WHOLE, [VMEM((EXTRA, width), F32)])(
        signals, swapped(signals, "sect", 2), turned, swapped(turned, "sect", 2)
    )
    bit = 4
    while bit < sections:
        chunk = joined(chunk, swapped(chunk, "sect", bit))
        bit *= 2
    return chunk


def after(array, other):
    return lax.optimization_barrier((array, other))[0]


def spread_chunk(signals, xyz, sections):
    count, width = signals.shape
    extra = jnp.zeros((EXTRA, width), BF16)
    extra = lax.dynamic_update_slice(extra, xyz.T, (0, lax.axis_index("sect") * count))
    payload = jnp.concatenate([signals, extra], 0)
    everyone = jnp.broadcast_to(payload[None], (sections,) + payload.shape)
    received = lax.all_to_all(everyone, "sect", split_axis=0, concat_axis=0, tiled=True)
    return jnp.concatenate(
        [received[:, :count].reshape(sections * count, -1), received[:, count:].astype(F32).sum(0).astype(BF16)], 0
    )


def per_device(signals, observer_xyz, panel_geometry, delays, counts, connectivity, owners):
    sections = lax.axis_size("sect")
    groups = lax.axis_size("azim")
    count = signals.shape[0]
    paired = count % 16 == 0 and sections % 2 == 0 and sections // 2 * count == 128

    source = window_index(sections, groups, paired, delays)
    panel_values, slots, ids = panel_columns(sections, counts, after(panel_geometry, source), owners)

    def add(sums, places, chunks, *rest):
        return sources(places, counts, chunks, source, panel_values, sums, *rest)

    if paired:
        half = half_chunk(signals, observer_xyz, sections)
        other = swapped(half, "sect", 1)
        corners = corner_matrix(counts, after(connectivity, half))
        sums = add((), [(0, 0)], [half])
        sums = after(sums, corners)
        chunk = joined(half, other)
    else:
        chunk = spread_chunk(signals, observer_xyz, sections)
        corners = corner_matrix(counts, connectivity)
    near = swapped(chunk, "azim", 1)
    chunks = {0: chunk}
    bit = groups // 2
    while bit > 1:
        for offset in list(chunks):
            chunks[offset ^ bit] = swapped(chunks[offset], "azim", bit)
        bit //= 2
    if paired:
        sums = add(sums, [(0, 128)], [other])
    else:
        sums = add((), [(0, 0)], [chunk])
    sums = add(sums, [(1, 0)], [near])
    rest = [offset for offset in chunks if offset]
    for offset in rest:
        chunks[offset] = after(chunks[offset], sums[0])
        chunks[offset ^ 1] = swapped(chunks[offset], "azim", 1)
    sums = add(sums, [(o, 0) for o in rest], [chunks[o] for o in rest])
    rest = [offset ^ 1 for offset in rest]
    matrices = [slots, ids, corners]
    loading, message, rim = add(sums, [(o, 0) for o in rest], [chunks[o] for o in rest], matrices, sections)
    message = lax.all_to_all(message, "sect", split_axis=0, concat_axis=0, tiled=True)
    rim = lax.ppermute(rim, "sect", [(i, (i + 1) % sections) for i in range(sections)])
    nodes, head = node_sums(corners, loading)
    return finish(message, rim, head, nodes)


def solution(mesh):
    in_specs = (
        P(("azim", "sect"), None),
        P(("azim", "sect"), None),
        P(None, ("azim", "sect")),
        P(("azim", "sect"), None),
        P(("azim", "sect")),
        P(None, ("azim", "sect")),
        P(("azim", "sect")),
    )
    out_specs = (P(("azim", "sect"), None), P(("azim", "sect"), None))
    return jax.shard_map(
        per_device, mesh=mesh, in_specs=in_specs, out_specs=out_specs, check_vma=False
    )
```

```python
import functools

import jax
import jax.numpy as jnp
from jax import lax
from jax.experimental import pallas as pl
from jax.experimental.pallas import tpu as pltpu
from jax.sharding import PartitionSpec as P

NPU = 128
BLK = 128
TW = 128
CELL_DEV = 256
NODE_DEV = 1032
RIM = NPU + 1
HEAD = 136
NODE_ROWS = 1168
EXTRA = 16
FIXED = 32000.0
F32 = jnp.float32
BF16 = jnp.bfloat16
VMEM = pltpu.VMEM
SMEM = pl.BlockSpec(memory_space=pltpu.SMEM)
WHOLE = pl.BlockSpec(memory_space=pltpu.VMEM)
PLACE = pl.BlockSpec(memory_space=pl.ANY)
COPY = pltpu.SemaphoreType.DMA


def call(kernel, name, out_shape, in_specs, out_specs, scratch_shapes=(), aliases=None, work=1_000_000):
    return pl.pallas_call(
        kernel,
        out_shape=out_shape,
        in_specs=in_specs,
        out_specs=out_specs,
        scratch_shapes=list(scratch_shapes),
        input_output_aliases=aliases or {},
        compiler_params=pltpu.CompilerParams(vmem_limit_bytes=24 * 1024 * 1024),
        cost_estimate=pl.CostEstimate(flops=work, bytes_accessed=4_000_000, transcendentals=0),
        name=name,
    )


def window_kernel(sections, paired, delay_ref, source_ref):
    groups, blocks, span, _ = source_ref.shape
    count = span // sections
    piece_rows = count if paired else 128
    padded = -(-blocks // 16) * 16
    delay = delay_ref[...].astype(F32)
    delay = jnp.concatenate([delay, jnp.zeros((padded - blocks, delay.shape[1]), F32)], 0).astype(BF16)
    spread = (padded, blocks * 128)
    spread = lax.broadcasted_iota(jnp.int32, spread, 1) // 128 == lax.broadcasted_iota(jnp.int32, spread, 0)
    spread = jnp.where(spread, 1.0, 0.0).astype(BF16)
    lanes = lax.broadcasted_iota(jnp.int32, (128, 128), 1)
    for piece in range(groups * span // 128):
        columns = lax.dot_general(
            delay[:, piece * 128 : (piece + 1) * 128], spread, (((0,), (0,)), ((), ())), preferred_element_type=F32
        )
        for block in range(blocks):
            source = columns[:, block * 128 : (block + 1) * 128].astype(jnp.int32) + lanes
            for part in range(128 // piece_rows):
                row = piece * 128 + part * piece_rows
                begin = row % span
                if paired:
                    apart = lax.axis_index("sect") ^ (begin // count)
                    begin = pl.multiple_of((apart // 2 + apart % 2 * (sections // 2)) * count, count)
                source_ref[row // span, block, pl.ds(begin, piece_rows), :] = source[
                    part * piece_rows : (part + 1) * piece_rows
                ]


def window_index(sections, groups, paired, delays):
    blocks, observers = delays.shape
    return call(
        functools.partial(window_kernel, sections, paired),
        "windows",
        jax.ShapeDtypeStruct((groups, blocks, observers // groups, 128), jnp.int32),
        [WHOLE],
        WHOLE,
        work=2_000_000_000,
    )(delays)


def column_kernel(sections, count_ref, geometry_ref, owner_ref, panel_ref, slot_ref, ids_ref):
    panels = geometry_ref.shape[1]
    spread = (32, 7 * 128)
    number = lax.broadcasted_iota(jnp.int32, spread, 0)
    spread = (lax.broadcasted_iota(jnp.int32, spread, 1) // 128 == number % 8) & (number < 24)
    spread = jnp.where(spread, 1.0, 0.0).astype(BF16)
    scale = jnp.where(lax.broadcasted_iota(jnp.int32, (8, BLK), 0) < 3, 0.25, 1.0)
    for block in range(panels // BLK):
        values = geometry_ref[:, block * BLK : (block + 1) * BLK]
        values = jnp.concatenate([values, values[:1]], 0) * scale
        high = values.astype(BF16).astype(F32)
        middle = (values - high).astype(BF16).astype(F32)
        parts = jnp.concatenate([high, middle, values - high - middle, jnp.zeros_like(values)], 0).astype(BF16)
        columns = lax.dot_general(parts, spread, (((0,), (0,)), ((), ())), preferred_element_type=F32)
        for part in range(7):
            panel_ref[block, part] = columns[:, part * 128 : (part + 1) * 128]

    cap = slot_ref.shape[0] // sections
    padded = ids_ref.shape[0]
    owner = owner_ref[...]
    dest = owner // CELL_DEV
    lane = lax.broadcasted_iota(jnp.int32, (padded, panels), 1)
    mine = dest == lax.broadcasted_iota(jnp.int32, (padded, panels), 0)
    ones = jnp.where(mine, 1.0, 0.0).astype(BF16)
    square = (128, 128)
    upto = lax.broadcasted_iota(jnp.int32, square, 0) <= lax.broadcasted_iota(jnp.int32, square, 1)
    upto = jnp.where(upto, 1.0, 0.0).astype(BF16)
    every = jnp.ones(square, BF16)
    carry = jnp.zeros((padded, 128), F32)
    counts = []
    for begin in range(0, panels, 128):
        piece = ones[:, begin : begin + 128]
        counts.append(carry + jnp.dot(piece, upto, preferred_element_type=F32))
        carry = carry + jnp.dot(piece, every, preferred_element_type=F32)
    count = jnp.concatenate(counts, 1).astype(jnp.int32)
    before = jnp.sum(jnp.where(mine, count - 1, 0), axis=0, keepdims=True)
    rank = before // 4
    slot = jnp.where(lane[:1] < count_ref[0], dest * cap + rank, -1)
    slot = jnp.broadcast_to(slot, (16, panels)).astype(jnp.int16)
    number = lax.broadcasted_iota(jnp.int16, (16, panels), 0)
    one, zero = jnp.array(1, BF16), jnp.array(0, BF16)
    for row in range(0, slot_ref.shape[0], 16):
        slot_ref[row : row + 16, :] = jnp.where(slot == number + jnp.int16(row), one, zero)

    at_lane = rank + lax.axis_index("sect") * cap % 128 == lax.broadcasted_iota(jnp.int32, (128, panels), 0)
    at_lane = jnp.where(at_lane, 1.0, 0.0).astype(BF16)
    cell = jnp.where(mine & (lane % 4 == 0), owner % CELL_DEV, 0).astype(F32).astype(BF16)
    ids_ref[...] = lax.dot_general(cell, at_lane, (((1,), (1,)), ((), ())), preferred_element_type=F32)


def panel_columns(sections, counts, geometry, owners):
    panels = geometry.shape[1]
    cap = 2 * CELL_DEV // sections
    padded = -(-sections // EXTRA) * EXTRA
    return call(
        functools.partial(column_kernel, sections),
        "columns",
        (
            jax.ShapeDtypeStruct((panels // BLK, 7, BLK, 128), F32),
            jax.ShapeDtypeStruct((sections * cap, panels), BF16),
            jax.ShapeDtypeStruct((padded, 128), F32),
        ),
        [SMEM, WHOLE, WHOLE],
        [WHOLE] * 3,
        work=2_000_000_000,
    )(counts, geometry, owners.reshape(1, panels))


def corner_kernel(count_ref, conn_ref, corner_ref, edge_ref):
    panels = conn_ref.shape[1]
    live = lax.broadcasted_iota(jnp.int32, (16, panels), 1) < count_ref[0]
    corners = [
        jnp.where(live, jnp.broadcast_to(conn_ref[i : i + 1, :], (16, panels)), -1).astype(jnp.int16) for i in range(4)
    ]
    number = lax.broadcasted_iota(jnp.int16, (16, panels), 0)
    share, zero = jnp.array(0.25, BF16), jnp.array(0, BF16)
    for row in range(0, NODE_ROWS, 16):
        node = number + jnp.int16(row)
        total = jnp.where(corners[0] == node, share, zero)
        for corner in corners[1:]:
            total = total + jnp.where(corner == node, share, zero)
        if row < NODE_DEV + 8:
            corner_ref[row : row + 16, :] = total
        if row + 16 > NODE_DEV:
            edge_ref[row - NODE_DEV + 8 : row - NODE_DEV + 24, :] = total


def corner_matrix(counts, connectivity):
    return call(
        corner_kernel,
        "corners",
        (
            jax.ShapeDtypeStruct((NODE_DEV + 8, connectivity.shape[1]), BF16),
            jax.ShapeDtypeStruct((HEAD + 8, connectivity.shape[1]), BF16),
        ),
        [SMEM, WHOLE],
        [WHOLE] * 2,
        work=2_000_000_000,
    )(counts, connectivity)


def first_join_kernel(*refs):
    *inputs, chunk_ref, wide_ref = refs
    parts = len(inputs) // 2
    count = inputs[0].shape[0]
    wide_ref[...] = jnp.zeros_like(wide_ref)
    total = jnp.zeros(wide_ref.shape, F32)
    for part in range(parts):
        chunk_ref[part * count : (part + 1) * count, :] = inputs[part][...]
        wide_ref[:3, :count] = inputs[parts + part][...].astype(F32)
        total = total + (pltpu.roll(wide_ref[...], part * count, 1) if part else wide_ref[...])
    chunk_ref[parts * count :, :] = total.astype(BF16)


def join_kernel(mine_ref, other_ref, chunk_ref):
    span = mine_ref.shape[0] - EXTRA
    chunk_ref[:span, :] = mine_ref[:span, :]
    chunk_ref[span : 2 * span, :] = other_ref[:span, :]
    moved = pltpu.roll(other_ref[span:, :].astype(F32), span, 1)
    chunk_ref[2 * span :, :] = (mine_ref[span:, :].astype(F32) + moved).astype(BF16)


def sources_kernel(places, first, last, count_ref, *refs):
    refs = list(refs)

    def take(number):
        taken = refs[:number]
        del refs[:number]
        return taken

    parts = len(places)
    chunks = take(parts)
    source_ref, panel_ref = take(2)
    if last:
        loading_in, thick_in, slot_ref, ids_ref, edge_ref = take(5)
        loading_ref, message_ref, rim_ref, thick_ref = take(4)
    else:
        loading_in, thick_in = (None, None) if first else take(2)
        loading_ref, thick_ref = take(2)
    code_ref, scale_ref, weight_ref, window_ref = take(4)

    blocks = source_ref.shape[1]
    span = chunks[0].shape[0] - EXTRA
    observers = parts * span
    points = []
    for number, chunk in enumerate(chunks):
        low = chunk[:span, :128].astype(F32)
        high = chunk[:span, 128:].astype(F32)
        most = jnp.max(jnp.maximum(jnp.abs(low), jnp.abs(high)), axis=1, keepdims=True)
        most = jnp.maximum(jnp.broadcast_to(most, (span, 128)), 1e-30)
        low = jnp.floor(low * (FIXED / most) + 0.5).astype(jnp.int32)
        high = jnp.floor(high * (FIXED / most) + 0.5).astype(jnp.int32)
        code_ref[number * span : (number + 1) * span, :] = (high << 16) | (low & 0xFFFF)
        scale_ref[number * span : (number + 1) * span, :] = most * (1 / (FIXED * 65536))
        points.append(chunk[span : span + EXTRA, :].astype(F32) * 0.25)

    lanes = lax.broadcasted_iota(jnp.int32, (128, 128), 1)
    for block in range(blocks):
        for number, (offset, begin) in enumerate(places):
            group = lax.axis_index("azim") ^ offset
            for piece in range(span // 128):
                here = number * span + piece * 128
                source = source_ref[group, block, begin + piece * 128 : begin + (piece + 1) * 128, :]
                at = source & 127
                code = jnp.take_along_axis(code_ref[here : here + 128, :], at, axis=1, mode="promise_in_bounds")
                scale = scale_ref[here : here + 128, :]
                current = jnp.where(source < 128, code << 16, code)
                following = (jnp.where(lanes == 0, code, current).astype(F32) * scale).astype(BF16)
                following = pltpu.roll(following, 127, 1)
                current = (current.astype(F32) * scale).astype(BF16)
                window_ref[block, here : here + 128, :TW] = current
                window_ref[block, here : here + 128, TW:] = following - current

        for strip in range(BLK // 16):
            rows = slice(strip * 16, strip * 16 + 16)
            x, y, z, normal_x, normal_y, normal_z, area = (panel_ref[block, i, rows, :] for i in range(7))
            for piece in range(observers // 128):
                here = piece * 128
                at_x, at_y, at_z = (
                    points[here // span][i : i + 1, here % span : here % span + 128] for i in range(3)
                )
                delta_x = at_x - x
                delta_y = at_y - y
                delta_z = at_z - z
                inverse = lax.rsqrt(delta_x * delta_x + delta_y * delta_y + delta_z * delta_z)
                flux = normal_x * delta_x + normal_y * delta_y + normal_z * delta_z
                far = flux * inverse * inverse
                cols = slice(here, here + 128)
                weight_ref[block, rows, cols] = (far * inverse).astype(BF16)
                weight_ref[block, BLK + strip * 16 : BLK + strip * 16 + 16, cols] = far.astype(BF16)
                weight_ref[block, 2 * BLK + strip * 16 : 2 * BLK + strip * 16 + 16, cols] = (area * inverse).astype(BF16)
        rows = slice(block * BLK, (block + 1) * BLK)
        products = jnp.dot(weight_ref[block], window_ref[block], preferred_element_type=F32)
        thick = products[2 * BLK :, TW:]
        loading = products[:BLK, :TW] + products[BLK : 2 * BLK, TW:]
        if not first:
            thick = thick + thick_in[rows, :]
            loading = loading + loading_in[rows, :]
        if last:
            alive = block * BLK + lax.broadcasted_iota(jnp.int32, (BLK, TW), 0) < count_ref[0]
            thick = jnp.where(alive, thick, 0.0).astype(BF16)
            loading = jnp.where(alive, loading, 0.0).astype(BF16)
        thick_ref[rows, :] = thick
        loading_ref[rows, :] = loading

    if last:
        sections = message_ref.shape[0]
        cap = slot_ref.shape[0] // sections
        slots = jnp.dot(slot_ref[...], thick_ref[...], preferred_element_type=F32).astype(BF16)
        for section in range(sections):
            message_ref[section, :cap, :] = slots[section * cap : (section + 1) * cap]
            ids = jnp.broadcast_to(ids_ref[section : section + 1, :], (EXTRA, 128))
            message_ref[section, cap:, :] = ids.astype(BF16)
        rim = jnp.dot(edge_ref[...], loading_ref[...], preferred_element_type=F32)
        rim_ref[...] = rim[8:].astype(BF16)


def sources(places, counts, chunks, source, panel_values, sums=(), slots=None, sections=None):
    blocks = source.shape[1]
    panels = panel_values.shape[0] * BLK
    observers = len(places) * (chunks[0].shape[0] - EXTRA)
    last = slots is not None
    operands = [counts, *chunks, source, panel_values, *sums]
    scratch = [
        VMEM((observers, 128), jnp.int32),
        VMEM((observers, 128), F32),
        VMEM((blocks, 3 * BLK, observers), BF16),
        VMEM((blocks, observers, 2 * TW), BF16),
    ]
    aliases = {}
    if last:
        operands += slots
        cap = 2 * CELL_DEV // sections
        out_shape = [
            jax.ShapeDtypeStruct((panels, TW), BF16),
            jax.ShapeDtypeStruct((sections, cap + EXTRA, TW), BF16),
            jax.ShapeDtypeStruct((HEAD, TW), BF16),
        ]
        scratch = [VMEM((panels, TW), BF16)] + scratch
    else:
        out_shape = [jax.ShapeDtypeStruct((panels, TW), F32)] * 2
        if sums:
            aliases = {len(operands) - 2: 0, len(operands) - 1: 1}
    return call(
        functools.partial(sources_kernel, places, not sums, last),
        "sources",
        out_shape,
        [SMEM] + [WHOLE] * (len(operands) - 1),
        [WHOLE] * len(out_shape),
        scratch,
        aliases,
        work=3_000_000_000,
    )(*operands)


def node_kernel(corner_ref, loading_ref, node_ref, head_ref):
    nodes = jnp.dot(corner_ref[...], loading_ref[...], preferred_element_type=F32)
    head_ref[...] = nodes[:HEAD]
    node_ref[...] = nodes[:NODE_DEV]


def node_sums(corners, loading):
    return call(
        node_kernel,
        "nodes",
        (jax.ShapeDtypeStruct((NODE_DEV, TW), F32), jax.ShapeDtypeStruct((HEAD, TW), F32)),
        [WHOLE] * 2,
        [WHOLE] * 2,
        work=2_000_000_000,
    )(corners, loading)


def finish_kernel(message_ref, rim_ref, head_ref, _, node_ref, cell_ref, rows_ref, top_ref, total_ref, sems):
    sections = message_ref.shape[0]
    cap = message_ref.shape[1] - EXTRA
    per = 128 // cap
    top_ref[...] = head_ref[...] + rim_ref[...].astype(F32)
    top_copy = pltpu.make_async_copy(top_ref, node_ref.at[pl.ds(0, HEAD), :], sems.at[0])
    top_copy.start()
    total = jnp.zeros((CELL_DEV, TW), F32)
    cell = lax.broadcasted_iota(jnp.int32, (CELL_DEV, 128), 0).astype(F32)
    for group in range(sections // per):
        ids = jnp.zeros((EXTRA, 128), F32)
        for inner in range(per):
            section = group * per + inner
            ids = ids + message_ref[section, cap:, :].astype(F32)
            rows_ref[section * cap : (section + 1) * cap, :] = message_ref[section, :cap, :]
        match = jnp.where(ids[:1] == cell, 1.0, 0.0).astype(BF16)
        total = total + jnp.dot(match, rows_ref[group * 128 : (group + 1) * 128, :], preferred_element_type=F32)
    total_ref[...] = total
    cell_copy = pltpu.make_async_copy(total_ref, cell_ref, sems.at[1])
    cell_copy.start()
    top_copy.wait()
    cell_copy.wait()


def finish(message, rim, head, nodes):
    sections = message.shape[0]
    cap = message.shape[1] - EXTRA
    return call(
        finish_kernel,
        "finish",
        (
            jax.ShapeDtypeStruct((NODE_DEV, TW), F32),
            jax.ShapeDtypeStruct((CELL_DEV, TW), F32),
        ),
        [WHOLE] * 3 + [PLACE],
        [PLACE] * 2,
        [VMEM((sections * cap, TW), BF16), VMEM((HEAD, TW), F32), VMEM((CELL_DEV, TW), F32), COPY((2,))],
        {3: 0},
    )(message, rim, head, nodes)


def swapped(array, axis, bit):
    peers = lax.axis_size(axis)
    return lax.ppermute(array, axis, [(i, i ^ bit) for i in range(peers)])


def joined(mine, other):
    span = mine.shape[0] - EXTRA
    shape = jax.ShapeDtypeStruct((2 * span + EXTRA, mine.shape[1]), BF16)
    return call(join_kernel, "join", shape, [WHOLE] * 2, WHOLE)(mine, other)


def half_chunk(signals, xyz, sections):
    count, width = signals.shape
    turned = xyz.T
    shape = jax.ShapeDtypeStruct((2 * count + EXTRA, width), BF16)
    chunk = call(first_join_kernel, "first", shape, [WHOLE] * 4, WHOLE, [VMEM((EXTRA, width), F32)])(
        signals, swapped(signals, "sect", 2), turned, swapped(turned, "sect", 2)
    )
    bit = 4
    while bit < sections:
        chunk = joined(chunk, swapped(chunk, "sect", bit))
        bit *= 2
    return chunk


def after(array, other):
    return lax.optimization_barrier((array, other))[0]


def spread_chunk(signals, xyz, sections):
    count, width = signals.shape
    extra = jnp.zeros((EXTRA, width), BF16)
    extra = lax.dynamic_update_slice(extra, xyz.T, (0, lax.axis_index("sect") * count))
    payload = jnp.concatenate([signals, extra], 0)
    everyone = jnp.broadcast_to(payload[None], (sections,) + payload.shape)
    received = lax.all_to_all(everyone, "sect", split_axis=0, concat_axis=0, tiled=True)
    return jnp.concatenate(
        [received[:, :count].reshape(sections * count, -1), received[:, count:].astype(F32).sum(0).astype(BF16)], 0
    )


def per_device(signals, observer_xyz, panel_geometry, delays, counts, connectivity, owners):
    sections = lax.axis_size("sect")
    groups = lax.axis_size("azim")
    count = signals.shape[0]
    paired = count % 16 == 0 and sections % 2 == 0 and sections // 2 * count == 128

    source = window_index(sections, groups, paired, delays)
    panel_values, slots, ids = panel_columns(sections, counts, after(panel_geometry, source), owners)

    def add(sums, places, chunks, *rest):
        return sources(places, counts, chunks, source, panel_values, sums, *rest)

    if paired:
        half = half_chunk(signals, observer_xyz, sections)
        other = swapped(half, "sect", 1)
        corners, edges = corner_matrix(counts, after(connectivity, half))
        sums = add((), [(0, 0)], [half])
        sums = after(sums, edges)
        chunk = joined(half, other)
    else:
        chunk = spread_chunk(signals, observer_xyz, sections)
        corners, edges = corner_matrix(counts, connectivity)
    near = swapped(chunk, "azim", 1)
    chunks = {0: chunk}
    bit = groups // 2
    while bit > 1:
        for offset in list(chunks):
            chunks[offset ^ bit] = swapped(chunks[offset], "azim", bit)
        bit //= 2
    if paired:
        sums = add(sums, [(0, 128)], [other])
    else:
        sums = add((), [(0, 0)], [chunk])
    sums = add(sums, [(1, 0)], [near])
    rest = [offset for offset in chunks if offset]
    for offset in rest:
        chunks[offset] = after(chunks[offset], sums[0])
        chunks[offset ^ 1] = swapped(chunks[offset], "azim", 1)
    sums = add(sums, [(o, 0) for o in rest], [chunks[o] for o in rest])
    rest = [offset ^ 1 for offset in rest]
    matrices = [slots, ids, edges]
    loading, message, rim = add(sums, [(o, 0) for o in rest], [chunks[o] for o in rest], matrices, sections)
    message = lax.all_to_all(message, "sect", split_axis=0, concat_axis=0, tiled=True)
    rim = lax.ppermute(rim, "sect", [(i, (i + 1) % sections) for i in range(sections)])
    nodes, head = node_sums(corners, loading)
    return finish(message, rim, head, nodes)


def solution(mesh):
    in_specs = (
        P(("azim", "sect"), None),
        P(("azim", "sect"), None),
        P(None, ("azim", "sect")),
        P(("azim", "sect"), None),
        P(("azim", "sect")),
        P(None, ("azim", "sect")),
        P(("azim", "sect")),
    )
    out_specs = (P(("azim", "sect"), None), P(("azim", "sect"), None))
    return jax.shard_map(
        per_device, mesh=mesh, in_specs=in_specs, out_specs=out_specs, check_vma=False
    )
```

```python
import functools

import jax
import jax.numpy as jnp
from jax import lax
from jax.experimental import pallas as pl
from jax.experimental.pallas import tpu as pltpu
from jax.sharding import PartitionSpec as P

NPU = 128
BLK = 128
TW = 128
CELL_DEV = 256
NODE_DEV = 1032
RIM = NPU + 1
HEAD = 136
NODE_ROWS = 1168
EXTRA = 16
FIXED = 32000.0
F32 = jnp.float32
BF16 = jnp.bfloat16
VMEM = pltpu.VMEM
SMEM = pl.BlockSpec(memory_space=pltpu.SMEM)
WHOLE = pl.BlockSpec(memory_space=pltpu.VMEM)
PLACE = pl.BlockSpec(memory_space=pl.ANY)
COPY = pltpu.SemaphoreType.DMA


def call(kernel, name, out_shape, in_specs, out_specs, scratch_shapes=(), aliases=None, work=1_000_000):
    return pl.pallas_call(
        kernel,
        out_shape=out_shape,
        in_specs=in_specs,
        out_specs=out_specs,
        scratch_shapes=list(scratch_shapes),
        input_output_aliases=aliases or {},
        compiler_params=pltpu.CompilerParams(vmem_limit_bytes=24 * 1024 * 1024),
        cost_estimate=pl.CostEstimate(flops=work, bytes_accessed=4_000_000, transcendentals=0),
        name=name,
    )


def window_kernel(sections, paired, delay_ref, source_ref):
    groups, blocks, span, _ = source_ref.shape
    count = span // sections
    piece_rows = count if paired else 128
    padded = -(-blocks // 16) * 16
    delay = delay_ref[...].astype(F32)
    delay = jnp.concatenate([delay, jnp.zeros((padded - blocks, delay.shape[1]), F32)], 0).astype(BF16)
    spread = (padded, blocks * 128)
    spread = lax.broadcasted_iota(jnp.int32, spread, 1) // 128 == lax.broadcasted_iota(jnp.int32, spread, 0)
    spread = jnp.where(spread, 1.0, 0.0).astype(BF16)
    lanes = lax.broadcasted_iota(jnp.int32, (128, 128), 1)
    for piece in range(groups * span // 128):
        columns = lax.dot_general(
            delay[:, piece * 128 : (piece + 1) * 128], spread, (((0,), (0,)), ((), ())), preferred_element_type=F32
        )
        for block in range(blocks):
            source = columns[:, block * 128 : (block + 1) * 128].astype(jnp.int32) + lanes
            for part in range(128 // piece_rows):
                row = piece * 128 + part * piece_rows
                begin = row % span
                if paired:
                    apart = lax.axis_index("sect") ^ (begin // count)
                    begin = pl.multiple_of((apart // 2 + apart % 2 * (sections // 2)) * count, count)
                source_ref[row // span, block, pl.ds(begin, piece_rows), :] = source[
                    part * piece_rows : (part + 1) * piece_rows
                ]


def window_index(sections, groups, paired, delays):
    blocks, observers = delays.shape
    return call(
        functools.partial(window_kernel, sections, paired),
        "windows",
        jax.ShapeDtypeStruct((groups, blocks, observers // groups, 128), jnp.int32),
        [WHOLE],
        WHOLE,
        work=2_000_000_000,
    )(delays)


def column_kernel(sections, count_ref, geometry_ref, owner_ref, panel_ref, slot_ref, ids_ref):
    panels = geometry_ref.shape[1]
    spread = (32, 7 * 128)
    number = lax.broadcasted_iota(jnp.int32, spread, 0)
    spread = (lax.broadcasted_iota(jnp.int32, spread, 1) // 128 == number % 8) & (number < 24)
    spread = jnp.where(spread, 1.0, 0.0).astype(BF16)
    scale = jnp.where(lax.broadcasted_iota(jnp.int32, (8, BLK), 0) < 3, 0.25, 1.0)
    for block in range(panels // BLK):
        values = geometry_ref[:, block * BLK : (block + 1) * BLK]
        values = jnp.concatenate([values, values[:1]], 0) * scale
        high = values.astype(BF16).astype(F32)
        middle = (values - high).astype(BF16).astype(F32)
        parts = jnp.concatenate([high, middle, values - high - middle, jnp.zeros_like(values)], 0).astype(BF16)
        columns = lax.dot_general(parts, spread, (((0,), (0,)), ((), ())), preferred_element_type=F32)
        for part in range(7):
            panel_ref[block, part] = columns[:, part * 128 : (part + 1) * 128]

    cap = slot_ref.shape[0] // sections
    padded = ids_ref.shape[0]
    owner = owner_ref[...]
    dest = owner // CELL_DEV
    lane = lax.broadcasted_iota(jnp.int32, (padded, panels), 1)
    mine = dest == lax.broadcasted_iota(jnp.int32, (padded, panels), 0)
    ones = jnp.where(mine, 1.0, 0.0).astype(BF16)
    square = (128, 128)
    upto = lax.broadcasted_iota(jnp.int32, square, 0) <= lax.broadcasted_iota(jnp.int32, square, 1)
    upto = jnp.where(upto, 1.0, 0.0).astype(BF16)
    every = jnp.ones(square, BF16)
    carry = jnp.zeros((padded, 128), F32)
    counts = []
    for begin in range(0, panels, 128):
        piece = ones[:, begin : begin + 128]
        counts.append(carry + jnp.dot(piece, upto, preferred_element_type=F32))
        carry = carry + jnp.dot(piece, every, preferred_element_type=F32)
    count = jnp.concatenate(counts, 1).astype(jnp.int32)
    before = jnp.sum(jnp.where(mine, count - 1, 0), axis=0, keepdims=True)
    rank = before // 4
    slot = jnp.where(lane[:1] < count_ref[0], dest * cap + rank, -1)
    slot = jnp.broadcast_to(slot, (16, panels)).astype(jnp.int16)
    number = lax.broadcasted_iota(jnp.int16, (16, panels), 0)
    one, zero = jnp.array(1, BF16), jnp.array(0, BF16)
    for row in range(0, slot_ref.shape[0], 16):
        slot_ref[row : row + 16, :] = jnp.where(slot == number + jnp.int16(row), one, zero)

    at_lane = rank + lax.axis_index("sect") * cap % 128 == lax.broadcasted_iota(jnp.int32, (128, panels), 0)
    at_lane = jnp.where(at_lane, 1.0, 0.0).astype(BF16)
    cell = jnp.where(mine & (lane % 4 == 0), owner % CELL_DEV, 0).astype(F32).astype(BF16)
    ids_ref[...] = lax.dot_general(cell, at_lane, (((1,), (1,)), ((), ())), preferred_element_type=F32)


def panel_columns(sections, counts, geometry, owners):
    panels = geometry.shape[1]
    cap = 2 * CELL_DEV // sections
    padded = -(-sections // EXTRA) * EXTRA
    return call(
        functools.partial(column_kernel, sections),
        "columns",
        (
            jax.ShapeDtypeStruct((panels // BLK, 7, BLK, 128), F32),
            jax.ShapeDtypeStruct((sections * cap, panels), BF16),
            jax.ShapeDtypeStruct((padded, 128), F32),
        ),
        [SMEM, WHOLE, WHOLE],
        [WHOLE] * 3,
        work=2_000_000_000,
    )(counts, geometry, owners.reshape(1, panels))


def corner_kernel(count_ref, conn_ref, corner_ref, edge_ref):
    panels = conn_ref.shape[1]
    live = lax.broadcasted_iota(jnp.int32, (16, panels), 1) < count_ref[0]
    corners = [
        jnp.where(live, jnp.broadcast_to(conn_ref[i : i + 1, :], (16, panels)), -1).astype(jnp.int16) for i in range(4)
    ]
    number = lax.broadcasted_iota(jnp.int16, (16, panels), 0)
    share, zero = jnp.array(0.25, BF16), jnp.array(0, BF16)
    for row in range(0, NODE_ROWS, 16):
        node = number + jnp.int16(row)
        total = jnp.where(corners[0] == node, share, zero)
        for corner in corners[1:]:
            total = total + jnp.where(corner == node, share, zero)
        if row < NODE_DEV + 8:
            corner_ref[row : row + 16, :] = total
        if row + 16 > NODE_DEV:
            edge_ref[row - NODE_DEV + 8 : row - NODE_DEV + 24, :] = total


def corner_matrix(counts, connectivity):
    return call(
        corner_kernel,
        "corners",
        (
            jax.ShapeDtypeStruct((NODE_DEV + 8, connectivity.shape[1]), BF16),
            jax.ShapeDtypeStruct((HEAD + 8, connectivity.shape[1]), BF16),
        ),
        [SMEM, WHOLE],
        [WHOLE] * 2,
        work=2_000_000_000,
    )(counts, connectivity)


def join_kernel(mine_ref, other_ref, chunk_ref):
    span = mine_ref.shape[0] - EXTRA
    chunk_ref[:span, :] = mine_ref[:span, :]
    chunk_ref[span : 2 * span, :] = other_ref[:span, :]
    moved = pltpu.roll(other_ref[span:, :].astype(F32), span, 1)
    chunk_ref[2 * span :, :] = (mine_ref[span:, :].astype(F32) + moved).astype(BF16)


def sources_kernel(places, first, last, count_ref, *refs):
    refs = list(refs)

    def take(number):
        taken = refs[:number]
        del refs[:number]
        return taken

    parts = len(places)
    chunks = take(parts)
    source_ref, panel_ref = take(2)
    if last:
        loading_in, thick_in, slot_ref, ids_ref, edge_ref = take(5)
        loading_ref, message_at, rim_ref, thick_ref, message_ref, sem = take(6)
    else:
        loading_in, thick_in = (None, None) if first else take(2)
        loading_ref, thick_ref = take(2)
    code_ref, scale_ref, weight_ref, window_ref = take(4)

    blocks = source_ref.shape[1]
    span = chunks[0].shape[0] - EXTRA
    observers = parts * span
    points = []
    for number, chunk in enumerate(chunks):
        low = chunk[:span, :128].astype(F32)
        high = chunk[:span, 128:].astype(F32)
        most = jnp.max(jnp.maximum(jnp.abs(low), jnp.abs(high)), axis=1, keepdims=True)
        most = jnp.maximum(jnp.broadcast_to(most, (span, 128)), 1e-30)
        low = jnp.floor(low * (FIXED / most) + 0.5).astype(jnp.int32)
        high = jnp.floor(high * (FIXED / most) + 0.5).astype(jnp.int32)
        code_ref[number * span : (number + 1) * span, :] = (high << 16) | (low & 0xFFFF)
        scale_ref[number * span : (number + 1) * span, :] = most * (1 / (FIXED * 65536))
        points.append(chunk[span : span + EXTRA, :].astype(F32) * 0.25)

    lanes = lax.broadcasted_iota(jnp.int32, (128, 128), 1)
    for block in range(blocks):
        for number, (offset, begin) in enumerate(places):
            group = lax.axis_index("azim") ^ offset
            for piece in range(span // 128):
                here = number * span + piece * 128
                source = source_ref[group, block, begin + piece * 128 : begin + (piece + 1) * 128, :]
                at = source & 127
                code = jnp.take_along_axis(code_ref[here : here + 128, :], at, axis=1, mode="promise_in_bounds")
                scale = scale_ref[here : here + 128, :]
                current = jnp.where(source < 128, code << 16, code)
                following = (jnp.where(lanes == 0, code, current).astype(F32) * scale).astype(BF16)
                following = pltpu.roll(following, 127, 1)
                current = (current.astype(F32) * scale).astype(BF16)
                window_ref[block, here : here + 128, :TW] = current
                window_ref[block, here : here + 128, TW:] = following - current

        for strip in range(BLK // 16):
            rows = slice(strip * 16, strip * 16 + 16)
            x, y, z, normal_x, normal_y, normal_z, area = (panel_ref[block, i, rows, :] for i in range(7))
            for piece in range(observers // 128):
                here = piece * 128
                at_x, at_y, at_z = (
                    points[here // span][i : i + 1, here % span : here % span + 128] for i in range(3)
                )
                delta_x = at_x - x
                delta_y = at_y - y
                delta_z = at_z - z
                inverse = lax.rsqrt(delta_x * delta_x + delta_y * delta_y + delta_z * delta_z)
                flux = normal_x * delta_x + normal_y * delta_y + normal_z * delta_z
                far = flux * inverse * inverse
                cols = slice(here, here + 128)
                weight_ref[block, rows, cols] = (far * inverse).astype(BF16)
                weight_ref[block, BLK + strip * 16 : BLK + strip * 16 + 16, cols] = far.astype(BF16)
                weight_ref[block, 2 * BLK + strip * 16 : 2 * BLK + strip * 16 + 16, cols] = (area * inverse).astype(BF16)
        rows = slice(block * BLK, (block + 1) * BLK)
        if last:
            alive = block * BLK + lax.broadcasted_iota(jnp.int32, (BLK, TW), 0) < count_ref[0]
            thick = jnp.dot(weight_ref[block, 2 * BLK :, :], window_ref[block, :, TW:], preferred_element_type=F32)
            thick_ref[rows, :] = jnp.where(alive, thick + thick_in[rows, :], 0.0).astype(BF16)
            continue
        products = jnp.dot(weight_ref[block], window_ref[block], preferred_element_type=F32)
        thick = products[2 * BLK :, TW:]
        loading = products[:BLK, :TW] + products[BLK : 2 * BLK, TW:]
        if not first:
            thick = thick + thick_in[rows, :]
            loading = loading + loading_in[rows, :]
        thick_ref[rows, :] = thick
        loading_ref[rows, :] = loading

    if last:
        sections = message_ref.shape[0]
        cap = slot_ref.shape[0] // sections
        slots = jnp.dot(slot_ref[...], thick_ref[...], preferred_element_type=F32).astype(BF16)
        for section in range(sections):
            message_ref[section, :cap, :] = slots[section * cap : (section + 1) * cap]
            ids = jnp.broadcast_to(ids_ref[section : section + 1, :], (EXTRA, 128))
            message_ref[section, cap:, :] = ids.astype(BF16)
        copy = pltpu.make_async_copy(message_ref, message_at, sem.at[0])
        copy.start()
        for block in range(blocks):
            rows = slice(block * BLK, (block + 1) * BLK)
            alive = block * BLK + lax.broadcasted_iota(jnp.int32, (BLK, TW), 0) < count_ref[0]
            loading = loading_in[rows, :]
            for half in range(2):
                weight = weight_ref[block, half * BLK : (half + 1) * BLK, :]
                window = window_ref[block, :, half * TW : (half + 1) * TW]
                loading = loading + jnp.dot(weight, window, preferred_element_type=F32)
            loading_ref[rows, :] = jnp.where(alive, loading, 0.0).astype(BF16)
        rim = jnp.dot(edge_ref[...], loading_ref[...], preferred_element_type=F32)
        rim_ref[...] = rim[8:].astype(BF16)
        copy.wait()


def sources(places, counts, chunks, source, panel_values, sums=(), slots=None, sections=None):
    blocks = source.shape[1]
    panels = panel_values.shape[0] * BLK
    observers = len(places) * (chunks[0].shape[0] - EXTRA)
    last = slots is not None
    operands = [counts, *chunks, source, panel_values, *sums]
    scratch = [
        VMEM((observers, 128), jnp.int32),
        VMEM((observers, 128), F32),
        VMEM((blocks, 3 * BLK, observers), BF16),
        VMEM((blocks, observers, 2 * TW), BF16),
    ]
    aliases = {}
    if last:
        operands += slots
        cap = 2 * CELL_DEV // sections
        out_shape = [
            jax.ShapeDtypeStruct((panels, TW), BF16),
            jax.ShapeDtypeStruct((sections, cap + EXTRA, TW), BF16),
            jax.ShapeDtypeStruct((HEAD, TW), BF16),
        ]
        scratch = [VMEM((panels, TW), BF16), VMEM(out_shape[1].shape, BF16), COPY((1,))] + scratch
    else:
        out_shape = [jax.ShapeDtypeStruct((panels, TW), F32)] * 2
        if sums:
            aliases = {len(operands) - 2: 0, len(operands) - 1: 1}
    out_specs = [WHOLE] * len(out_shape)
    if last:
        out_specs[1] = PLACE
    return call(
        functools.partial(sources_kernel, places, not sums, last),
        "sources",
        out_shape,
        [SMEM] + [WHOLE] * (len(operands) - 1),
        out_specs,
        scratch,
        aliases,
        work=3_000_000_000,
    )(*operands)


def node_kernel(corner_ref, loading_ref, node_ref, head_ref):
    nodes = jnp.dot(corner_ref[...], loading_ref[...], preferred_element_type=F32)
    head_ref[...] = nodes[:HEAD]
    node_ref[...] = nodes[:NODE_DEV]


def node_sums(corners, loading):
    return call(
        node_kernel,
        "nodes",
        (jax.ShapeDtypeStruct((NODE_DEV, TW), F32), jax.ShapeDtypeStruct((HEAD, TW), F32)),
        [WHOLE] * 2,
        [WHOLE] * 2,
        work=2_000_000_000,
    )(corners, loading)


def finish_kernel(message_ref, rim_ref, head_ref, _, node_ref, cell_ref, rows_ref, top_ref, total_ref, sems):
    sections = message_ref.shape[0]
    cap = message_ref.shape[1] - EXTRA
    per = 128 // cap
    top_ref[...] = head_ref[...] + rim_ref[...].astype(F32)
    top_copy = pltpu.make_async_copy(top_ref, node_ref.at[pl.ds(0, HEAD), :], sems.at[0])
    top_copy.start()
    total = jnp.zeros((CELL_DEV, TW), F32)
    cell = lax.broadcasted_iota(jnp.int32, (CELL_DEV, 128), 0).astype(F32)
    for group in range(sections // per):
        ids = jnp.zeros((EXTRA, 128), F32)
        for inner in range(per):
            section = group * per + inner
            ids = ids + message_ref[section, cap:, :].astype(F32)
            rows_ref[section * cap : (section + 1) * cap, :] = message_ref[section, :cap, :]
        match = jnp.where(ids[:1] == cell, 1.0, 0.0).astype(BF16)
        total = total + jnp.dot(match, rows_ref[group * 128 : (group + 1) * 128, :], preferred_element_type=F32)
    total_ref[...] = total
    cell_copy = pltpu.make_async_copy(total_ref, cell_ref, sems.at[1])
    cell_copy.start()
    top_copy.wait()
    cell_copy.wait()


def finish(message, rim, head, nodes):
    sections = message.shape[0]
    cap = message.shape[1] - EXTRA
    return call(
        finish_kernel,
        "finish",
        (
            jax.ShapeDtypeStruct((NODE_DEV, TW), F32),
            jax.ShapeDtypeStruct((CELL_DEV, TW), F32),
        ),
        [WHOLE] * 3 + [PLACE],
        [PLACE] * 2,
        [VMEM((sections * cap, TW), BF16), VMEM((HEAD, TW), F32), VMEM((CELL_DEV, TW), F32), COPY((2,))],
        {3: 0},
    )(message, rim, head, nodes)


def swapped(array, axis, bit):
    peers = lax.axis_size(axis)
    return lax.ppermute(array, axis, [(i, i ^ bit) for i in range(peers)])


def joined(mine, other):
    span = mine.shape[0] - EXTRA
    shape = jax.ShapeDtypeStruct((2 * span + EXTRA, mine.shape[1]), BF16)
    return call(join_kernel, "join", shape, [WHOLE] * 2, WHOLE)(mine, other)


def half_chunk(signals, xyz, sections):
    count, width = signals.shape
    extra = jnp.pad(xyz.T, ((0, EXTRA - 3), (0, width - count)))
    chunk = jnp.concatenate([signals, extra], 0)
    bit = 2
    while bit < sections:
        chunk = joined(chunk, swapped(chunk, "sect", bit))
        bit *= 2
    return chunk


def after(array, other):
    return lax.optimization_barrier((array, other))[0]


def spread_chunk(signals, xyz, sections):
    count, width = signals.shape
    extra = jnp.zeros((EXTRA, width), BF16)
    extra = lax.dynamic_update_slice(extra, xyz.T, (0, lax.axis_index("sect") * count))
    payload = jnp.concatenate([signals, extra], 0)
    everyone = jnp.broadcast_to(payload[None], (sections,) + payload.shape)
    received = lax.all_to_all(everyone, "sect", split_axis=0, concat_axis=0, tiled=True)
    return jnp.concatenate(
        [received[:, :count].reshape(sections * count, -1), received[:, count:].astype(F32).sum(0).astype(BF16)], 0
    )


def per_device(signals, observer_xyz, panel_geometry, delays, counts, connectivity, owners):
    sections = lax.axis_size("sect")
    groups = lax.axis_size("azim")
    count = signals.shape[0]
    paired = count % 16 == 0 and sections % 2 == 0 and sections // 2 * count == 128

    source = window_index(sections, groups, paired, delays)
    panel_values, slots, ids = panel_columns(sections, counts, after(panel_geometry, source), owners)

    def add(sums, places, chunks, *rest):
        return sources(places, counts, chunks, source, panel_values, sums, *rest)

    if paired:
        half = half_chunk(signals, observer_xyz, sections)
        other = swapped(half, "sect", 1)
        corners, edges = corner_matrix(counts, after(connectivity, half))
        sums = add((), [(0, 0)], [half])
        sums = after(sums, edges)
        chunk = joined(half, other)
    else:
        chunk = spread_chunk(signals, observer_xyz, sections)
        corners, edges = corner_matrix(counts, connectivity)
    near = swapped(chunk, "azim", 1)
    chunks = {0: chunk}
    bit = groups // 2
    while bit > 1:
        for offset in list(chunks):
            chunks[offset ^ bit] = swapped(chunks[offset], "azim", bit)
        bit //= 2
    if paired:
        sums = add(sums, [(0, 128)], [other])
    else:
        sums = add((), [(0, 0)], [chunk])
    sums = add(sums, [(1, 0)], [near])
    rest = [offset for offset in chunks if offset]
    for offset in rest:
        chunks[offset] = after(chunks[offset], sums[0])
        chunks[offset ^ 1] = swapped(chunks[offset], "azim", 1)
    sums = add(sums, [(o, 0) for o in rest], [chunks[o] for o in rest])
    rest = [offset ^ 1 for offset in rest]
    matrices = [slots, ids, edges]
    loading, message, rim = add(sums, [(o, 0) for o in rest], [chunks[o] for o in rest], matrices, sections)
    message = lax.all_to_all(message, "sect", split_axis=0, concat_axis=0, tiled=True)
    rim = lax.ppermute(rim, "sect", [(i, (i + 1) % sections) for i in range(sections)])
    nodes, head = node_sums(corners, loading)
    return finish(message, rim, head, nodes)


def solution(mesh):
    in_specs = (
        P(("azim", "sect"), None),
        P(("azim", "sect"), None),
        P(None, ("azim", "sect")),
        P(("azim", "sect"), None),
        P(("azim", "sect")),
        P(None, ("azim", "sect")),
        P(("azim", "sect")),
    )
    out_specs = (P(("azim", "sect"), None), P(("azim", "sect"), None))
    return jax.shard_map(
        per_device, mesh=mesh, in_specs=in_specs, out_specs=out_specs, check_vma=False
    )
```

```python
import functools

import jax
import jax.numpy as jnp
from jax import lax
from jax.experimental import pallas as pl
from jax.experimental.pallas import tpu as pltpu
from jax.sharding import PartitionSpec as P

NPU = 128
BLK = 128
TW = 128
CELL_DEV = 256
NODE_DEV = 1032
RIM = NPU + 1
HEAD = 136
NODE_ROWS = 1168
EXTRA = 16
FIXED = 32000.0
F32 = jnp.float32
BF16 = jnp.bfloat16
VMEM = pltpu.VMEM
SMEM = pl.BlockSpec(memory_space=pltpu.SMEM)
WHOLE = pl.BlockSpec(memory_space=pltpu.VMEM)
PLACE = pl.BlockSpec(memory_space=pl.ANY)
COPY = pltpu.SemaphoreType.DMA


def call(kernel, name, out_shape, in_specs, out_specs, scratch_shapes=(), aliases=None, work=1_000_000):
    return pl.pallas_call(
        kernel,
        out_shape=out_shape,
        in_specs=in_specs,
        out_specs=out_specs,
        scratch_shapes=list(scratch_shapes),
        input_output_aliases=aliases or {},
        compiler_params=pltpu.CompilerParams(vmem_limit_bytes=24 * 1024 * 1024),
        cost_estimate=pl.CostEstimate(flops=work, bytes_accessed=4_000_000, transcendentals=0),
        name=name,
    )


def window_kernel(sections, paired, delay_ref, source_ref):
    groups, blocks, span, _ = source_ref.shape
    count = span // sections
    piece_rows = count if paired else 128
    padded = -(-blocks // 16) * 16
    delay = delay_ref[...].astype(F32)
    delay = jnp.concatenate([delay, jnp.zeros((padded - blocks, delay.shape[1]), F32)], 0).astype(BF16)
    spread = (padded, blocks * 128)
    spread = lax.broadcasted_iota(jnp.int32, spread, 1) // 128 == lax.broadcasted_iota(jnp.int32, spread, 0)
    spread = jnp.where(spread, 1.0, 0.0).astype(BF16)
    lanes = lax.broadcasted_iota(jnp.int32, (128, 128), 1)
    for piece in range(groups * span // 128):
        columns = lax.dot_general(
            delay[:, piece * 128 : (piece + 1) * 128], spread, (((0,), (0,)), ((), ())), preferred_element_type=F32
        )
        for block in range(blocks):
            source = columns[:, block * 128 : (block + 1) * 128].astype(jnp.int32) + lanes
            for part in range(128 // piece_rows):
                row = piece * 128 + part * piece_rows
                begin = row % span
                if paired:
                    apart = lax.axis_index("sect") ^ (begin // count)
                    begin = pl.multiple_of((apart // 2 + apart % 2 * (sections // 2)) * count, count)
                source_ref[row // span, block, pl.ds(begin, piece_rows), :] = source[
                    part * piece_rows : (part + 1) * piece_rows
                ]


def window_index(sections, groups, paired, delays):
    blocks, observers = delays.shape
    return call(
        functools.partial(window_kernel, sections, paired),
        "windows",
        jax.ShapeDtypeStruct((groups, blocks, observers // groups, 128), jnp.int32),
        [WHOLE],
        WHOLE,
        work=2_000_000_000,
    )(delays)


def column_kernel(sections, count_ref, geometry_ref, owner_ref, panel_ref, slot_ref, ids_ref):
    panels = geometry_ref.shape[1]
    spread = (32, 7 * 128)
    number = lax.broadcasted_iota(jnp.int32, spread, 0)
    spread = (lax.broadcasted_iota(jnp.int32, spread, 1) // 128 == number % 8) & (number < 24)
    spread = jnp.where(spread, 1.0, 0.0).astype(BF16)
    scale = jnp.where(lax.broadcasted_iota(jnp.int32, (8, BLK), 0) < 3, 0.25, 1.0)
    for block in range(panels // BLK):
        values = geometry_ref[:, block * BLK : (block + 1) * BLK]
        values = jnp.concatenate([values, values[:1]], 0) * scale
        high = values.astype(BF16).astype(F32)
        middle = (values - high).astype(BF16).astype(F32)
        parts = jnp.concatenate([high, middle, values - high - middle, jnp.zeros_like(values)], 0).astype(BF16)
        columns = lax.dot_general(parts, spread, (((0,), (0,)), ((), ())), preferred_element_type=F32)
        for part in range(7):
            panel_ref[block, part] = columns[:, part * 128 : (part + 1) * 128]

    cap = slot_ref.shape[0] // sections
    padded = ids_ref.shape[0]
    owner = owner_ref[...]
    dest = owner // CELL_DEV
    lane = lax.broadcasted_iota(jnp.int32, (padded, panels), 1)
    mine = dest == lax.broadcasted_iota(jnp.int32, (padded, panels), 0)
    ones = jnp.where(mine, 1.0, 0.0).astype(BF16)
    square = (128, 128)
    upto = lax.broadcasted_iota(jnp.int32, square, 0) <= lax.broadcasted_iota(jnp.int32, square, 1)
    upto = jnp.where(upto, 1.0, 0.0).astype(BF16)
    every = jnp.ones(square, BF16)
    carry = jnp.zeros((padded, 128), F32)
    counts = []
    for begin in range(0, panels, 128):
        piece = ones[:, begin : begin + 128]
        counts.append(carry + jnp.dot(piece, upto, preferred_element_type=F32))
        carry = carry + jnp.dot(piece, every, preferred_element_type=F32)
    count = jnp.concatenate(counts, 1).astype(jnp.int32)
    before = jnp.sum(jnp.where(mine, count - 1, 0), axis=0, keepdims=True)
    rank = before // 4
    slot = jnp.where(lane[:1] < count_ref[0], dest * cap + rank, -1)
    slot = jnp.broadcast_to(slot, (16, panels)).astype(jnp.int16)
    number = lax.broadcasted_iota(jnp.int16, (16, panels), 0)
    one, zero = jnp.array(1, BF16), jnp.array(0, BF16)
    for row in range(0, slot_ref.shape[0], 16):
        slot_ref[row : row + 16, :] = jnp.where(slot == number + jnp.int16(row), one, zero)

    at_lane = rank + lax.axis_index("sect") * cap % 128 == lax.broadcasted_iota(jnp.int32, (128, panels), 0)
    at_lane = jnp.where(at_lane, 1.0, 0.0).astype(BF16)
    cell = jnp.where(mine & (lane % 4 == 0), owner % CELL_DEV, 0).astype(F32).astype(BF16)
    ids_ref[...] = lax.dot_general(cell, at_lane, (((1,), (1,)), ((), ())), preferred_element_type=F32)


def panel_columns(sections, counts, geometry, owners):
    panels = geometry.shape[1]
    cap = 2 * CELL_DEV // sections
    padded = -(-sections // EXTRA) * EXTRA
    return call(
        functools.partial(column_kernel, sections),
        "columns",
        (
            jax.ShapeDtypeStruct((panels // BLK, 7, BLK, 128), F32),
            jax.ShapeDtypeStruct((sections * cap, panels), BF16),
            jax.ShapeDtypeStruct((padded, 128), F32),
        ),
        [SMEM, WHOLE, WHOLE],
        [WHOLE] * 3,
        work=2_000_000_000,
    )(counts, geometry, owners.reshape(1, panels))


def corner_kernel(count_ref, conn_ref, corner_ref, edge_ref):
    panels = conn_ref.shape[1]
    live = lax.broadcasted_iota(jnp.int32, (16, panels), 1) < count_ref[0]
    corners = [
        jnp.where(live, jnp.broadcast_to(conn_ref[i : i + 1, :], (16, panels)), -1).astype(jnp.int16) for i in range(4)
    ]
    number = lax.broadcasted_iota(jnp.int16, (16, panels), 0)
    share, zero = jnp.array(0.25, BF16), jnp.array(0, BF16)
    for row in range(0, NODE_ROWS, 16):
        node = number + jnp.int16(row)
        total = jnp.where(corners[0] == node, share, zero)
        for corner in corners[1:]:
            total = total + jnp.where(corner == node, share, zero)
        if row < NODE_DEV + 8:
            corner_ref[row : row + 16, :] = total
        if row + 16 > NODE_DEV:
            edge_ref[row - NODE_DEV + 8 : row - NODE_DEV + 24, :] = total


def corner_matrix(counts, connectivity):
    return call(
        corner_kernel,
        "corners",
        (
            jax.ShapeDtypeStruct((NODE_DEV + 8, connectivity.shape[1]), BF16),
            jax.ShapeDtypeStruct((HEAD + 8, connectivity.shape[1]), BF16),
        ),
        [SMEM, WHOLE],
        [WHOLE] * 2,
        work=2_000_000_000,
    )(counts, connectivity)


def first_join_kernel(*refs):
    *inputs, chunk_ref, wide_ref = refs
    parts = len(inputs) // 2
    count = inputs[0].shape[0]
    wide_ref[...] = jnp.zeros_like(wide_ref)
    total = jnp.zeros(wide_ref.shape, F32)
    for part in range(parts):
        chunk_ref[part * count : (part + 1) * count, :] = inputs[part][...]
        wide_ref[:3, :count] = inputs[parts + part][...].astype(F32)
        total = total + (pltpu.roll(wide_ref[...], part * count, 1) if part else wide_ref[...])
    chunk_ref[parts * count :, :] = total.astype(BF16)


def join_kernel(mine_ref, other_ref, chunk_ref):
    span = mine_ref.shape[0] - EXTRA
    chunk_ref[:span, :] = mine_ref[:span, :]
    chunk_ref[span : 2 * span, :] = other_ref[:span, :]
    moved = pltpu.roll(other_ref[span:, :].astype(F32), span, 1)
    chunk_ref[2 * span :, :] = (mine_ref[span:, :].astype(F32) + moved).astype(BF16)


def sources_kernel(places, first, last, count_ref, *refs):
    refs = list(refs)

    def take(number):
        taken = refs[:number]
        del refs[:number]
        return taken

    parts = len(places)
    chunks = take(parts)
    source_ref, panel_ref = take(2)
    if last:
        loading_in, thick_in, slot_ref, ids_ref, edge_ref = take(5)
        loading_ref, message_ref, rim_ref, thick_ref = take(4)
    else:
        loading_in, thick_in = (None, None) if first else take(2)
        loading_ref, thick_ref = take(2)
    code_ref, scale_ref, weight_ref, window_ref = take(4)

    blocks = source_ref.shape[1]
    span = chunks[0].shape[0] - EXTRA
    observers = parts * span
    points = []
    for number, chunk in enumerate(chunks):
        low = chunk[:span, :128].astype(F32)
        high = chunk[:span, 128:].astype(F32)
        most = jnp.max(jnp.maximum(jnp.abs(low), jnp.abs(high)), axis=1, keepdims=True)
        most = jnp.maximum(jnp.broadcast_to(most, (span, 128)), 1e-30)
        low = jnp.floor(low * (FIXED / most) + 0.5).astype(jnp.int32)
        high = jnp.floor(high * (FIXED / most) + 0.5).astype(jnp.int32)
        code_ref[number * span : (number + 1) * span, :] = (high << 16) | (low & 0xFFFF)
        scale_ref[number * span : (number + 1) * span, :] = most * (1 / (FIXED * 65536))
        points.append(chunk[span : span + EXTRA, :].astype(F32) * 0.25)

    lanes = lax.broadcasted_iota(jnp.int32, (128, 128), 1)
    for block in range(blocks):
        for number, (offset, begin) in enumerate(places):
            group = lax.axis_index("azim") ^ offset
            for piece in range(span // 128):
                here = number * span + piece * 128
                source = source_ref[group, block, begin + piece * 128 : begin + (piece + 1) * 128, :]
                at = source & 127
                code = jnp.take_along_axis(code_ref[here : here + 128, :], at, axis=1, mode="promise_in_bounds")
                scale = scale_ref[here : here + 128, :]
                current = jnp.where(source < 128, code << 16, code)
                following = (jnp.where(lanes == 0, code, current).astype(F32) * scale).astype(BF16)
                following = pltpu.roll(following, 127, 1)
                current = (current.astype(F32) * scale).astype(BF16)
                window_ref[block, here : here + 128, :TW] = current
                window_ref[block, here : here + 128, TW:] = following - current

        for strip in range(BLK // 16):
            rows = slice(strip * 16, strip * 16 + 16)
            x, y, z, normal_x, normal_y, normal_z, area = (panel_ref[block, i, rows, :] for i in range(7))
            for piece in range(observers // 128):
                here = piece * 128
                at_x, at_y, at_z = (
                    points[here // span][i : i + 1, here % span : here % span + 128] for i in range(3)
                )
                delta_x = at_x - x
                delta_y = at_y - y
                delta_z = at_z - z
                inverse = lax.rsqrt(delta_x * delta_x + delta_y * delta_y + delta_z * delta_z)
                flux = normal_x * delta_x + normal_y * delta_y + normal_z * delta_z
                far = flux * inverse * inverse
                cols = slice(here, here + 128)
                weight_ref[block, rows, cols] = (far * inverse).astype(BF16)
                weight_ref[block, BLK + strip * 16 : BLK + strip * 16 + 16, cols] = far.astype(BF16)
                weight_ref[block, 2 * BLK + strip * 16 : 2 * BLK + strip * 16 + 16, cols] = (area * inverse).astype(BF16)
        rows = slice(block * BLK, (block + 1) * BLK)
        products = jnp.dot(weight_ref[block], window_ref[block], preferred_element_type=F32)
        thick = products[2 * BLK :, TW:]
        loading = products[:BLK, :TW] + products[BLK : 2 * BLK, TW:]
        if not first:
            thick = thick + thick_in[rows, :]
            loading = loading + loading_in[rows, :]
        if last:
            alive = block * BLK + lax.broadcasted_iota(jnp.int32, (BLK, TW), 0) < count_ref[0]
            thick = jnp.where(alive, thick, 0.0).astype(BF16)
            loading = jnp.where(alive, loading, 0.0).astype(BF16)
        thick_ref[rows, :] = thick
        loading_ref[rows, :] = loading

    if last:
        sections = message_ref.shape[0]
        cap = slot_ref.shape[0] // sections
        slots = jnp.dot(slot_ref[...], thick_ref[...], preferred_element_type=F32).astype(BF16)
        for section in range(sections):
            message_ref[section, :cap, :] = slots[section * cap : (section + 1) * cap]
            ids = jnp.broadcast_to(ids_ref[section : section + 1, :], (EXTRA, 128))
            message_ref[section, cap:, :] = ids.astype(BF16)
        rim = jnp.dot(edge_ref[...], loading_ref[...], preferred_element_type=F32)
        rim_ref[...] = rim[8:].astype(BF16)


def sources(places, counts, chunks, source, panel_values, sums=(), slots=None, sections=None):
    blocks = source.shape[1]
    panels = panel_values.shape[0] * BLK
    observers = len(places) * (chunks[0].shape[0] - EXTRA)
    last = slots is not None
    operands = [counts, *chunks, source, panel_values, *sums]
    scratch = [
        VMEM((observers, 128), jnp.int32),
        VMEM((observers, 128), F32),
        VMEM((blocks, 3 * BLK, observers), BF16),
        VMEM((blocks, observers, 2 * TW), BF16),
    ]
    aliases = {}
    if last:
        operands += slots
        cap = 2 * CELL_DEV // sections
        out_shape = [
            jax.ShapeDtypeStruct((panels, TW), BF16),
            jax.ShapeDtypeStruct((sections, cap + EXTRA, TW), BF16),
            jax.ShapeDtypeStruct((HEAD, TW), BF16),
        ]
        scratch = [VMEM((panels, TW), BF16)] + scratch
    else:
        out_shape = [jax.ShapeDtypeStruct((panels, TW), F32)] * 2
        if sums:
            aliases = {len(operands) - 2: 0, len(operands) - 1: 1}
    return call(
        functools.partial(sources_kernel, places, not sums, last),
        "sources",
        out_shape,
        [SMEM] + [WHOLE] * (len(operands) - 1),
        [WHOLE] * len(out_shape),
        scratch,
        aliases,
        work=3_000_000_000,
    )(*operands)


def node_kernel(corner_ref, loading_ref, rim_ref, node_ref):
    nodes = jnp.dot(corner_ref[...], loading_ref[...], preferred_element_type=F32)
    node_ref[:HEAD, :] = nodes[:HEAD] + rim_ref[...].astype(F32)
    node_ref[HEAD:, :] = nodes[HEAD:NODE_DEV]


def node_sums(corners, loading, rim):
    return call(
        node_kernel,
        "nodes",
        jax.ShapeDtypeStruct((NODE_DEV, TW), F32),
        [WHOLE] * 3,
        WHOLE,
        work=20_000_000_000,
    )(corners, loading, rim)


def cell_kernel(message_ref, cell_ref, rows_ref):
    sections = message_ref.shape[0]
    cap = message_ref.shape[1] - EXTRA
    per = 128 // cap
    total = jnp.zeros((CELL_DEV, TW), F32)
    cell = lax.broadcasted_iota(jnp.int32, (CELL_DEV, 128), 0).astype(F32)
    for group in range(sections // per):
        ids = jnp.zeros((EXTRA, 128), F32)
        for inner in range(per):
            section = group * per + inner
            ids = ids + message_ref[section, cap:, :].astype(F32)
            rows_ref[section * cap : (section + 1) * cap, :] = message_ref[section, :cap, :]
        match = jnp.where(ids[:1] == cell, 1.0, 0.0).astype(BF16)
        total = total + jnp.dot(match, rows_ref[group * 128 : (group + 1) * 128, :], preferred_element_type=F32)
    cell_ref[...] = total


def cell_sums(message):
    sections = message.shape[0]
    cap = message.shape[1] - EXTRA
    return call(
        cell_kernel,
        "cells",
        jax.ShapeDtypeStruct((CELL_DEV, TW), F32),
        [WHOLE],
        WHOLE,
        [VMEM((sections * cap, TW), BF16)],
    )(message)


def swapped(array, axis, bit):
    peers = lax.axis_size(axis)
    return lax.ppermute(array, axis, [(i, i ^ bit) for i in range(peers)])


def joined(mine, other):
    span = mine.shape[0] - EXTRA
    shape = jax.ShapeDtypeStruct((2 * span + EXTRA, mine.shape[1]), BF16)
    return call(join_kernel, "join", shape, [WHOLE] * 2, WHOLE)(mine, other)


def half_chunk(signals, xyz, sections):
    count, width = signals.shape
    turned = xyz.T
    shape = jax.ShapeDtypeStruct((2 * count + EXTRA, width), BF16)
    chunk = call(first_join_kernel, "first", shape, [WHOLE] * 4, WHOLE, [VMEM((EXTRA, width), F32)])(
        signals, swapped(signals, "sect", 2), turned, swapped(turned, "sect", 2)
    )
    bit = 4
    while bit < sections:
        chunk = joined(chunk, swapped(chunk, "sect", bit))
        bit *= 2
    return chunk


def after(array, other):
    return lax.optimization_barrier((array, other))[0]


def spread_chunk(signals, xyz, sections):
    count, width = signals.shape
    extra = jnp.zeros((EXTRA, width), BF16)
    extra = lax.dynamic_update_slice(extra, xyz.T, (0, lax.axis_index("sect") * count))
    payload = jnp.concatenate([signals, extra], 0)
    everyone = jnp.broadcast_to(payload[None], (sections,) + payload.shape)
    received = lax.all_to_all(everyone, "sect", split_axis=0, concat_axis=0, tiled=True)
    return jnp.concatenate(
        [received[:, :count].reshape(sections * count, -1), received[:, count:].astype(F32).sum(0).astype(BF16)], 0
    )


def per_device(signals, observer_xyz, panel_geometry, delays, counts, connectivity, owners):
    sections = lax.axis_size("sect")
    groups = lax.axis_size("azim")
    count = signals.shape[0]
    paired = count % 16 == 0 and sections % 2 == 0 and sections // 2 * count == 128

    source = window_index(sections, groups, paired, delays)
    panel_values, slots, ids = panel_columns(sections, counts, after(panel_geometry, source), owners)

    def add(sums, places, chunks, *rest):
        return sources(places, counts, chunks, source, panel_values, sums, *rest)

    if paired:
        half = half_chunk(signals, observer_xyz, sections)
        other = swapped(half, "sect", 1)
        corners, edges = corner_matrix(counts, after(connectivity, half))
        sums = add((), [(0, 0)], [half])
        sums = after(sums, edges)
        chunk = joined(half, other)
    else:
        chunk = spread_chunk(signals, observer_xyz, sections)
        corners, edges = corner_matrix(counts, connectivity)
    near = swapped(chunk, "azim", 1)
    chunks = {0: chunk}
    bit = groups // 2
    while bit > 1:
        for offset in list(chunks):
            chunks[offset ^ bit] = swapped(chunks[offset], "azim", bit)
        bit //= 2
    if paired:
        sums = add(sums, [(0, 128)], [other])
    else:
        sums = add((), [(0, 0)], [chunk])
    sums = add(sums, [(1, 0)], [near])
    rest = [offset for offset in chunks if offset]
    for offset in rest:
        chunks[offset] = after(chunks[offset], sums[0])
        chunks[offset ^ 1] = swapped(chunks[offset], "azim", 1)
    sums = add(sums, [(o, 0) for o in rest], [chunks[o] for o in rest])
    rest = [offset ^ 1 for offset in rest]
    matrices = [slots, ids, edges]
    loading, message, rim = add(sums, [(o, 0) for o in rest], [chunks[o] for o in rest], matrices, sections)
    message = lax.all_to_all(message, "sect", split_axis=0, concat_axis=0, tiled=True)
    rim = lax.ppermute(rim, "sect", [(i, (i + 1) % sections) for i in range(sections)])
    return node_sums(corners, loading, rim), cell_sums(message)


def solution(mesh):
    in_specs = (
        P(("azim", "sect"), None),
        P(("azim", "sect"), None),
        P(None, ("azim", "sect")),
        P(("azim", "sect"), None),
        P(("azim", "sect")),
        P(None, ("azim", "sect")),
        P(("azim", "sect")),
    )
    out_specs = (P(("azim", "sect"), None), P(("azim", "sect"), None))
    return jax.shard_map(
        per_device, mesh=mesh, in_specs=in_specs, out_specs=out_specs, check_vma=False
    )
```

```python
import functools

import jax
import jax.numpy as jnp
from jax import lax
from jax.experimental import pallas as pl
from jax.experimental.pallas import tpu as pltpu
from jax.sharding import PartitionSpec as P

NPU = 128
BLK = 128
TW = 128
CELL_DEV = 256
NODE_DEV = 1032
RIM = NPU + 1
HEAD = 136
NODE_ROWS = 1168
EXTRA = 16
FIXED = 32000.0
F32 = jnp.float32
BF16 = jnp.bfloat16
VMEM = pltpu.VMEM
SMEM = pl.BlockSpec(memory_space=pltpu.SMEM)
WHOLE = pl.BlockSpec(memory_space=pltpu.VMEM)
PLACE = pl.BlockSpec(memory_space=pl.ANY)
COPY = pltpu.SemaphoreType.DMA


def call(kernel, name, out_shape, in_specs, out_specs, scratch_shapes=(), aliases=None, work=1_000_000):
    return pl.pallas_call(
        kernel,
        out_shape=out_shape,
        in_specs=in_specs,
        out_specs=out_specs,
        scratch_shapes=list(scratch_shapes),
        input_output_aliases=aliases or {},
        compiler_params=pltpu.CompilerParams(vmem_limit_bytes=24 * 1024 * 1024),
        cost_estimate=pl.CostEstimate(flops=work, bytes_accessed=4_000_000, transcendentals=0),
        name=name,
    )


def window_kernel(sections, paired, delay_ref, source_ref):
    groups, blocks, span, _ = source_ref.shape
    count = span // sections
    piece_rows = count if paired else 128
    padded = -(-blocks // 16) * 16
    delay = delay_ref[...].astype(F32)
    delay = jnp.concatenate([delay, jnp.zeros((padded - blocks, delay.shape[1]), F32)], 0).astype(BF16)
    spread = (padded, blocks * 128)
    spread = lax.broadcasted_iota(jnp.int32, spread, 1) // 128 == lax.broadcasted_iota(jnp.int32, spread, 0)
    spread = jnp.where(spread, 1.0, 0.0).astype(BF16)
    lanes = lax.broadcasted_iota(jnp.int32, (128, 128), 1)
    for piece in range(groups * span // 128):
        columns = lax.dot_general(
            delay[:, piece * 128 : (piece + 1) * 128], spread, (((0,), (0,)), ((), ())), preferred_element_type=F32
        )
        for block in range(blocks):
            source = columns[:, block * 128 : (block + 1) * 128].astype(jnp.int32) + lanes
            for part in range(128 // piece_rows):
                row = piece * 128 + part * piece_rows
                begin = row % span
                if paired:
                    apart = lax.axis_index("sect") ^ (begin // count)
                    begin = pl.multiple_of((apart // 2 + apart % 2 * (sections // 2)) * count, count)
                source_ref[row // span, block, pl.ds(begin, piece_rows), :] = source[
                    part * piece_rows : (part + 1) * piece_rows
                ]


def window_index(sections, groups, paired, delays):
    blocks, observers = delays.shape
    return call(
        functools.partial(window_kernel, sections, paired),
        "windows",
        jax.ShapeDtypeStruct((groups, blocks, observers // groups, 128), jnp.int32),
        [WHOLE],
        WHOLE,
        work=2_000_000_000,
    )(delays)


def column_kernel(sections, count_ref, geometry_ref, owner_ref, panel_ref, slot_ref, ids_ref):
    panels = geometry_ref.shape[1]
    spread = (32, 7 * 128)
    number = lax.broadcasted_iota(jnp.int32, spread, 0)
    spread = (lax.broadcasted_iota(jnp.int32, spread, 1) // 128 == number % 8) & (number < 24)
    spread = jnp.where(spread, 1.0, 0.0).astype(BF16)
    scale = jnp.where(lax.broadcasted_iota(jnp.int32, (8, BLK), 0) < 3, 0.25, 1.0)
    for block in range(panels // BLK):
        values = geometry_ref[:, block * BLK : (block + 1) * BLK]
        values = jnp.concatenate([values, values[:1]], 0) * scale
        high = values.astype(BF16).astype(F32)
        middle = (values - high).astype(BF16).astype(F32)
        parts = jnp.concatenate([high, middle, values - high - middle, jnp.zeros_like(values)], 0).astype(BF16)
        columns = lax.dot_general(parts, spread, (((0,), (0,)), ((), ())), preferred_element_type=F32)
        for part in range(7):
            panel_ref[block, part] = columns[:, part * 128 : (part + 1) * 128]

    cap = slot_ref.shape[0] // sections
    padded = ids_ref.shape[0]
    owner = owner_ref[...]
    dest = owner // CELL_DEV
    lane = lax.broadcasted_iota(jnp.int32, (padded, panels), 1)
    mine = dest == lax.broadcasted_iota(jnp.int32, (padded, panels), 0)
    ones = jnp.where(mine, 1.0, 0.0).astype(BF16)
    square = (128, 128)
    upto = lax.broadcasted_iota(jnp.int32, square, 0) <= lax.broadcasted_iota(jnp.int32, square, 1)
    upto = jnp.where(upto, 1.0, 0.0).astype(BF16)
    every = jnp.ones(square, BF16)
    carry = jnp.zeros((padded, 128), F32)
    counts = []
    for begin in range(0, panels, 128):
        piece = ones[:, begin : begin + 128]
        counts.append(carry + jnp.dot(piece, upto, preferred_element_type=F32))
        carry = carry + jnp.dot(piece, every, preferred_element_type=F32)
    count = jnp.concatenate(counts, 1).astype(jnp.int32)
    before = jnp.sum(jnp.where(mine, count - 1, 0), axis=0, keepdims=True)
    rank = before // 4
    slot = jnp.where(lane[:1] < count_ref[0], dest * cap + rank, -1)
    slot = jnp.broadcast_to(slot, (16, panels)).astype(jnp.int16)
    number = lax.broadcasted_iota(jnp.int16, (16, panels), 0)
    one, zero = jnp.array(1, BF16), jnp.array(0, BF16)
    for row in range(0, slot_ref.shape[0], 16):
        slot_ref[row : row + 16, :] = jnp.where(slot == number + jnp.int16(row), one, zero)

    at_lane = rank + lax.axis_index("sect") * cap % 128 == lax.broadcasted_iota(jnp.int32, (128, panels), 0)
    at_lane = jnp.where(at_lane, 1.0, 0.0).astype(BF16)
    cell = jnp.where(mine & (lane % 4 == 0), owner % CELL_DEV, 0).astype(F32).astype(BF16)
    ids_ref[...] = lax.dot_general(cell, at_lane, (((1,), (1,)), ((), ())), preferred_element_type=F32)


def panel_columns(sections, counts, geometry, owners):
    panels = geometry.shape[1]
    cap = 2 * CELL_DEV // sections
    padded = -(-sections // EXTRA) * EXTRA
    return call(
        functools.partial(column_kernel, sections),
        "columns",
        (
            jax.ShapeDtypeStruct((panels // BLK, 7, BLK, 128), F32),
            jax.ShapeDtypeStruct((sections * cap, panels), BF16),
            jax.ShapeDtypeStruct((padded, 128), F32),
        ),
        [SMEM, WHOLE, WHOLE],
        [WHOLE] * 3,
        work=2_000_000_000,
    )(counts, geometry, owners.reshape(1, panels))


def corner_kernel(count_ref, conn_ref, corner_ref, edge_ref):
    panels = conn_ref.shape[1]
    live = lax.broadcasted_iota(jnp.int32, (16, panels), 1) < count_ref[0]
    corners = [
        jnp.where(live, jnp.broadcast_to(conn_ref[i : i + 1, :], (16, panels)), -1).astype(jnp.int16) for i in range(4)
    ]
    number = lax.broadcasted_iota(jnp.int16, (16, panels), 0)
    share, zero = jnp.array(0.25, BF16), jnp.array(0, BF16)
    for row in range(0, NODE_ROWS, 16):
        node = number + jnp.int16(row)
        total = jnp.where(corners[0] == node, share, zero)
        for corner in corners[1:]:
            total = total + jnp.where(corner == node, share, zero)
        if row < NODE_DEV + 8:
            corner_ref[row : row + 16, :] = total
        if row + 16 > NODE_DEV:
            edge_ref[row - NODE_DEV + 8 : row - NODE_DEV + 24, :] = total


def corner_matrix(counts, connectivity):
    return call(
        corner_kernel,
        "corners",
        (
            jax.ShapeDtypeStruct((NODE_DEV + 8, connectivity.shape[1]), BF16),
            jax.ShapeDtypeStruct((HEAD + 8, connectivity.shape[1]), BF16),
        ),
        [SMEM, WHOLE],
        [WHOLE] * 2,
        work=2_000_000_000,
    )(counts, connectivity)


def first_join_kernel(*refs):
    *inputs, chunk_ref, wide_ref = refs
    parts = len(inputs) // 2
    count = inputs[0].shape[0]
    wide_ref[...] = jnp.zeros_like(wide_ref)
    total = jnp.zeros(wide_ref.shape, F32)
    for part in range(parts):
        chunk_ref[part * count : (part + 1) * count, :] = inputs[part][...]
        wide_ref[:3, :count] = inputs[parts + part][...].astype(F32)
        total = total + (pltpu.roll(wide_ref[...], part * count, 1) if part else wide_ref[...])
    chunk_ref[parts * count :, :] = total.astype(BF16)


def join_kernel(mine_ref, other_ref, chunk_ref):
    span = mine_ref.shape[0] - EXTRA
    chunk_ref[:span, :] = mine_ref[:span, :]
    chunk_ref[span : 2 * span, :] = other_ref[:span, :]
    moved = pltpu.roll(other_ref[span:, :].astype(F32), span, 1)
    chunk_ref[2 * span :, :] = (mine_ref[span:, :].astype(F32) + moved).astype(BF16)


def sources_kernel(places, first, last, count_ref, *refs):
    refs = list(refs)

    def take(number):
        taken = refs[:number]
        del refs[:number]
        return taken

    parts = len(places)
    chunks = take(parts)
    source_ref, panel_ref = take(2)
    if last:
        loading_in, thick_in, slot_ref, ids_ref, edge_ref = take(5)
        loading_ref, message_ref, rim_ref, thick_ref = take(4)
    else:
        loading_in, thick_in = (None, None) if first else take(2)
        loading_ref, thick_ref = take(2)
    code_ref, scale_ref, weight_ref, window_ref = take(4)

    blocks = source_ref.shape[1]
    span = chunks[0].shape[0] - EXTRA
    observers = parts * span
    points = []
    for number, chunk in enumerate(chunks):
        low = chunk[:span, :128].astype(F32)
        high = chunk[:span, 128:].astype(F32)
        most = jnp.max(jnp.maximum(jnp.abs(low), jnp.abs(high)), axis=1, keepdims=True)
        most = jnp.maximum(jnp.broadcast_to(most, (span, 128)), 1e-30)
        low = jnp.floor(low * (FIXED / most) + 0.5).astype(jnp.int32)
        high = jnp.floor(high * (FIXED / most) + 0.5).astype(jnp.int32)
        code_ref[number * span : (number + 1) * span, :] = (high << 16) | (low & 0xFFFF)
        scale_ref[number * span : (number + 1) * span, :] = most * (1 / (FIXED * 65536))
        points.append(chunk[span : span + EXTRA, :].astype(F32) * 0.25)

    lanes = lax.broadcasted_iota(jnp.int32, (128, 128), 1)
    for block in range(blocks):
        for number, (offset, begin) in enumerate(places):
            group = lax.axis_index("azim") ^ offset
            for piece in range(span // 128):
                here = number * span + piece * 128
                source = source_ref[group, block, begin + piece * 128 : begin + (piece + 1) * 128, :]
                at = source & 127
                code = jnp.take_along_axis(code_ref[here : here + 128, :], at, axis=1, mode="promise_in_bounds")
                scale = scale_ref[here : here + 128, :]
                current = jnp.where(source < 128, code << 16, code)
                following = (jnp.where(lanes == 0, code, current).astype(F32) * scale).astype(BF16)
                following = pltpu.roll(following, 127, 1)
                current = (current.astype(F32) * scale).astype(BF16)
                window_ref[block, here : here + 128, :TW] = current
                window_ref[block, here : here + 128, TW:] = following - current

        for strip in range(BLK // 16):
            rows = slice(strip * 16, strip * 16 + 16)
            x, y, z, normal_x, normal_y, normal_z, area = (panel_ref[block, i, rows, :] for i in range(7))
            for piece in range(observers // 128):
                here = piece * 128
                at_x, at_y, at_z = (
                    points[here // span][i : i + 1, here % span : here % span + 128] for i in range(3)
                )
                delta_x = at_x - x
                delta_y = at_y - y
                delta_z = at_z - z
                inverse = lax.rsqrt(delta_x * delta_x + delta_y * delta_y + delta_z * delta_z)
                flux = normal_x * delta_x + normal_y * delta_y + normal_z * delta_z
                far = flux * inverse * inverse
                cols = slice(here, here + 128)
                weight_ref[block, rows, cols] = (far * inverse).astype(BF16)
                weight_ref[block, BLK + strip * 16 : BLK + strip * 16 + 16, cols] = far.astype(BF16)
                weight_ref[block, 2 * BLK + strip * 16 : 2 * BLK + strip * 16 + 16, cols] = (area * inverse).astype(BF16)
        rows = slice(block * BLK, (block + 1) * BLK)
        products = jnp.dot(weight_ref[block], window_ref[block], preferred_element_type=F32)
        thick = products[2 * BLK :, TW:]
        loading = products[:BLK, :TW] + products[BLK : 2 * BLK, TW:]
        if not first:
            thick = thick + thick_in[rows, :]
            loading = loading + loading_in[rows, :]
        if last:
            alive = block * BLK + lax.broadcasted_iota(jnp.int32, (BLK, TW), 0) < count_ref[0]
            thick = jnp.where(alive, thick, 0.0).astype(BF16)
            loading = jnp.where(alive, loading, 0.0).astype(BF16)
        thick_ref[rows, :] = thick
        loading_ref[rows, :] = loading

    if last:
        sections = message_ref.shape[0]
        cap = slot_ref.shape[0] // sections
        slots = jnp.dot(slot_ref[...], thick_ref[...], preferred_element_type=F32).astype(BF16)
        for section in range(sections):
            message_ref[section, :cap, :] = slots[section * cap : (section + 1) * cap]
            ids = jnp.broadcast_to(ids_ref[section : section + 1, :], (EXTRA, 128))
            message_ref[section, cap:, :] = ids.astype(BF16)
        rim = jnp.dot(edge_ref[...], loading_ref[...], preferred_element_type=F32)
        rim_ref[...] = rim[8:].astype(BF16)


def sources(places, counts, chunks, source, panel_values, sums=(), slots=None, sections=None):
    blocks = source.shape[1]
    panels = panel_values.shape[0] * BLK
    observers = len(places) * (chunks[0].shape[0] - EXTRA)
    last = slots is not None
    operands = [counts, *chunks, source, panel_values, *sums]
    scratch = [
        VMEM((observers, 128), jnp.int32),
        VMEM((observers, 128), F32),
        VMEM((blocks, 3 * BLK, observers), BF16),
        VMEM((blocks, observers, 2 * TW), BF16),
    ]
    aliases = {}
    if last:
        operands += slots
        cap = 2 * CELL_DEV // sections
        out_shape = [
            jax.ShapeDtypeStruct((panels, TW), BF16),
            jax.ShapeDtypeStruct((sections, cap + EXTRA, TW), BF16),
            jax.ShapeDtypeStruct((HEAD, TW), BF16),
        ]
        scratch = [VMEM((panels, TW), BF16)] + scratch
    else:
        out_shape = [jax.ShapeDtypeStruct((panels, TW), F32)] * 2
        if sums:
            aliases = {len(operands) - 2: 0, len(operands) - 1: 1}
    return call(
        functools.partial(sources_kernel, places, not sums, last),
        "sources",
        out_shape,
        [SMEM] + [WHOLE] * (len(operands) - 1),
        [WHOLE] * len(out_shape),
        scratch,
        aliases,
        work=3_000_000_000,
    )(*operands)


def node_kernel(corner_ref, loading_ref, node_ref, head_ref):
    nodes = jnp.dot(corner_ref[...], loading_ref[...], preferred_element_type=F32)
    head_ref[...] = nodes[:HEAD]
    node_ref[...] = nodes[:NODE_DEV]


def node_sums(corners, loading):
    return call(
        node_kernel,
        "nodes",
        (jax.ShapeDtypeStruct((NODE_DEV, TW), F32), jax.ShapeDtypeStruct((HEAD, TW), F32)),
        [WHOLE] * 2,
        [WHOLE] * 2,
        work=2_000_000_000,
    )(corners, loading)


def cell_kernel(message_ref, cell_ref, rows_ref):
    sections = message_ref.shape[0]
    cap = message_ref.shape[1] - EXTRA
    per = 128 // cap
    total = jnp.zeros((CELL_DEV, TW), F32)
    cell = lax.broadcasted_iota(jnp.int32, (CELL_DEV, 128), 0).astype(F32)
    for group in range(sections // per):
        ids = jnp.zeros((EXTRA, 128), F32)
        for inner in range(per):
            section = group * per + inner
            ids = ids + message_ref[section, cap:, :].astype(F32)
            rows_ref[section * cap : (section + 1) * cap, :] = message_ref[section, :cap, :]
        match = jnp.where(ids[:1] == cell, 1.0, 0.0).astype(BF16)
        total = total + jnp.dot(match, rows_ref[group * 128 : (group + 1) * 128, :], preferred_element_type=F32)
    cell_ref[...] = total


def cell_sums(message):
    sections = message.shape[0]
    cap = message.shape[1] - EXTRA
    return call(
        cell_kernel,
        "cells",
        jax.ShapeDtypeStruct((CELL_DEV, TW), F32),
        [WHOLE],
        WHOLE,
        [VMEM((sections * cap, TW), BF16)],
    )(message)


def head_kernel(rim_ref, head_ref, _, node_ref, top_ref, sems):
    top_ref[...] = head_ref[...] + rim_ref[...].astype(F32)
    copy = pltpu.make_async_copy(top_ref, node_ref.at[pl.ds(0, HEAD), :], sems.at[0])
    copy.start()
    copy.wait()


def with_rim(rim, head, nodes):
    return call(
        head_kernel,
        "head",
        jax.ShapeDtypeStruct((NODE_DEV, TW), F32),
        [WHOLE] * 2 + [PLACE],
        PLACE,
        [VMEM((HEAD, TW), F32), COPY((1,))],
        {2: 0},
    )(rim, head, nodes)


def swapped(array, axis, bit):
    peers = lax.axis_size(axis)
    return lax.ppermute(array, axis, [(i, i ^ bit) for i in range(peers)])


def joined(mine, other):
    span = mine.shape[0] - EXTRA
    shape = jax.ShapeDtypeStruct((2 * span + EXTRA, mine.shape[1]), BF16)
    return call(join_kernel, "join", shape, [WHOLE] * 2, WHOLE)(mine, other)


def half_chunk(signals, xyz, sections):
    count, width = signals.shape
    turned = xyz.T
    shape = jax.ShapeDtypeStruct((2 * count + EXTRA, width), BF16)
    chunk = call(first_join_kernel, "first", shape, [WHOLE] * 4, WHOLE, [VMEM((EXTRA, width), F32)])(
        signals, swapped(signals, "sect", 2), turned, swapped(turned, "sect", 2)
    )
    bit = 4
    while bit < sections:
        chunk = joined(chunk, swapped(chunk, "sect", bit))
        bit *= 2
    return chunk


def after(array, other):
    return lax.optimization_barrier((array, other))[0]


def spread_chunk(signals, xyz, sections):
    count, width = signals.shape
    extra = jnp.zeros((EXTRA, width), BF16)
    extra = lax.dynamic_update_slice(extra, xyz.T, (0, lax.axis_index("sect") * count))
    payload = jnp.concatenate([signals, extra], 0)
    everyone = jnp.broadcast_to(payload[None], (sections,) + payload.shape)
    received = lax.all_to_all(everyone, "sect", split_axis=0, concat_axis=0, tiled=True)
    return jnp.concatenate(
        [received[:, :count].reshape(sections * count, -1), received[:, count:].astype(F32).sum(0).astype(BF16)], 0
    )


def per_device(signals, observer_xyz, panel_geometry, delays, counts, connectivity, owners):
    sections = lax.axis_size("sect")
    groups = lax.axis_size("azim")
    count = signals.shape[0]
    paired = count % 16 == 0 and sections % 2 == 0 and sections // 2 * count == 128

    source = window_index(sections, groups, paired, delays)
    panel_values, slots, ids = panel_columns(sections, counts, after(panel_geometry, source), owners)

    def add(sums, places, chunks, *rest):
        return sources(places, counts, chunks, source, panel_values, sums, *rest)

    if paired:
        half = half_chunk(signals, observer_xyz, sections)
        other = swapped(half, "sect", 1)
        corners, edges = corner_matrix(counts, after(connectivity, half))
        sums = add((), [(0, 0)], [half])
        sums = after(sums, edges)
        chunk = joined(half, other)
    else:
        chunk = spread_chunk(signals, observer_xyz, sections)
        corners, edges = corner_matrix(counts, connectivity)
    near = swapped(chunk, "azim", 1)
    chunks = {0: chunk}
    bit = groups // 2
    while bit > 1:
        for offset in list(chunks):
            chunks[offset ^ bit] = swapped(chunks[offset], "azim", bit)
        bit //= 2
    if paired:
        sums = add(sums, [(0, 128)], [other])
    else:
        sums = add((), [(0, 0)], [chunk])
    sums = add(sums, [(1, 0)], [near])
    rest = [offset for offset in chunks if offset]
    for offset in rest:
        chunks[offset] = after(chunks[offset], sums[0])
        chunks[offset ^ 1] = swapped(chunks[offset], "azim", 1)
    sums = add(sums, [(o, 0) for o in rest], [chunks[o] for o in rest])
    rest = [offset ^ 1 for offset in rest]
    matrices = [slots, ids, edges]
    loading, message, rim = add(sums, [(o, 0) for o in rest], [chunks[o] for o in rest], matrices, sections)
    message = lax.all_to_all(message, "sect", split_axis=0, concat_axis=0, tiled=True)
    rim = lax.ppermute(rim, "sect", [(i, (i + 1) % sections) for i in range(sections)])
    nodes, head = node_sums(corners, loading)
    cells = cell_sums(message)
    rim, cells = lax.optimization_barrier((rim, cells))
    return with_rim(rim, head, nodes), cells


def solution(mesh):
    in_specs = (
        P(("azim", "sect"), None),
        P(("azim", "sect"), None),
        P(None, ("azim", "sect")),
        P(("azim", "sect"), None),
        P(("azim", "sect")),
        P(None, ("azim", "sect")),
        P(("azim", "sect")),
    )
    out_specs = (P(("azim", "sect"), None), P(("azim", "sect"), None))
    return jax.shard_map(
        per_device, mesh=mesh, in_specs=in_specs, out_specs=out_specs, check_vma=False
    )
```
